32 devices in a mesh: row: 4 (over y, core), seq: 8 (over z, x).
Axes of the slice: x: 2, y: 2, z: 4, core: 2. Of those that a mesh axis runs over, the one named last changes fastest.
Arguments:
- tokens: bfloat16 [16, 1024, 512], P('row', 'seq'), may hold values from -6 to 6
- first_len: int32 [16], P('row'), may hold values from 512 to 1024, as said below
- gain_one: float32 [512], replicated, may hold values from 0.5 to 1.5
- conv_weight: float32 [4, 512], replicated, may hold values from -3 to 3
- w_z: bfloat16 [512, 1024], replicated, may hold values from -0.25 to 0.25
- bias_z: float32 [1024], replicated, may hold values from -12 to -3
- w_h: bfloat16 [512, 1024], replicated, may hold values from -0.25 to 0.25
- w_out: bfloat16 [1024, 512], replicated, may hold values from -0.1875 to 0.1875
- gain_two: float32 [512], replicated, may hold values from 0.5 to 1.5
- w_up: bfloat16 [512, 2048], replicated, may hold values from -0.25 to 0.25
- w_down: bfloat16 [2048, 512], replicated, may hold values from -0.125 to 0.125
- cotangent: bfloat16 [16, 1024, 512], P('row', 'seq'), may hold values from -6 to 6
Outputs:
- output: bfloat16 [16, 1024, 512], P('row', 'seq')
- grad_tokens: bfloat16 [16, 1024, 512], P('row', 'seq')
- grad_gain_one: float32 [512], replicated
- grad_conv: float32 [4, 512], replicated
- grad_w_z: float32 [512, 1024], replicated
- grad_bias_z: float32 [1024], replicated
- grad_w_h: float32 [512, 1024], replicated
- grad_w_out: float32 [1024, 512], replicated
- grad_gain_two: float32 [512], replicated
- grad_w_up: float32 [512, 2048], replicated
- grad_w_down: float32 [2048, 512], replicated
The draws below stay inside these ranges and needn't reach their ends.
Inputs may be any that keep to these rules, and one draw needn't show every extreme that they name: `first_len`: each entry is 1024 // 2 (a row of two documents) or 1024 (one document); in every aligned block of 4 rows both occur.
All inputs are finite; a program needn't handle non-finite values.
Results may differ from the reference program's by a relative error of at most 0.0075.
The reference program's roundings to bfloat16 on the way count: a program that leaves them out, or rounds other values in their place, can miss the bound.
Values sent between devices are 32-bit elements; how exact they have to be, the bound alone decides.
No kernel may reach another device: no remote copies, remote signals or barrier semaphores. Data moves between devices by JAX's collectives and lax.ppermute only.
A program may use at most 128 MiB of HBM per device.

```python
import jax
import jax.numpy as jnp
from jax import lax

D = 512
H = 1024
FF = 2048
KCONV = 4
ROWS_DEV = 4
ROW_LEN = 1024
ROWS = 16


def draw_first_len(key, part):
    key = jax.random.fold_in(key, 7)
    half_len = ROW_LEN // 2
    blocks = ROWS // ROWS_DEV
    picks = jax.random.randint(key, (blocks, ROWS_DEV), 0, 2, dtype=jnp.int32)
    long_slot = jax.random.randint(jax.random.fold_in(key, 11), (blocks, 1), 0, ROWS_DEV, dtype=jnp.int32)
    offset = jax.random.randint(jax.random.fold_in(key, 13), (blocks, 1), 0, ROWS_DEV - 1, dtype=jnp.int32)
    short_slot = (long_slot + 1 + offset) % ROWS_DEV
    slots = jnp.arange(ROWS_DEV, dtype=jnp.int32)[None, :]
    picks = jnp.where(slots == long_slot, 1, jnp.where(slots == short_slot, 0, picks))
    return (half_len + picks * half_len).reshape(ROWS).astype(jnp.int32)


def level_of(own_key, extent, cuts, low, top_value):
    gain, own = 1.0, jax.random.fold_in(own_key, 6)
    for dim, parts in cuts:
        draws = jnp.exp(jax.random.uniform(jax.random.fold_in(own, dim), (parts,), jnp.float32, low / len(cuts), top_value / len(cuts)))
        gain = gain * jnp.repeat(draws, extent[dim] // parts).reshape([-1 if axis == dim else 1 for axis in range(len(extent))])
    return gain


def gaussian(stream_key, extent, spread, most, cuts=(), kind=jnp.bfloat16):
    values = jax.random.normal(stream_key, extent, jnp.float32) * spread
    if len(cuts) > 0:
        values = level_of(stream_key, extent, cuts, -0.22, 0.18) * values
    return jnp.clip(values, min=-most, max=most).astype(kind)


def setup_inputs(seed: int = 0) -> dict:
    key_list = jax.random.split(jax.random.key(seed), 13)
    tokens = gaussian(key_list[0], (ROWS, ROW_LEN, D), 1.0, 6.0, ((0, 4), (1, 8)))
    first_len = draw_first_len(jax.random.fold_in(key_list[12], 71), 0)
    gain_one = jnp.clip(1.0 + 0.1 * jax.random.normal(key_list[2], (D,), jnp.float32), 0.5, 1.5)
    conv_weight = gaussian(key_list[3], (KCONV, D), KCONV ** -0.5, 3.0, (), jnp.float32)
    w_z = gaussian(key_list[4], (D, H), D ** -0.5, 0.25)
    bias_z = jnp.clip(jax.random.uniform(key_list[5], (H,), jnp.float32, -12.0, -3.0), -12.0, -3.0)
    w_h = gaussian(key_list[6], (D, H), D ** -0.5, 0.25)
    w_out = gaussian(key_list[7], (H, D), H ** -0.5, 0.1875)
    gain_two = jnp.clip(1.0 + 0.1 * jax.random.normal(key_list[8], (D,), jnp.float32), 0.5, 1.5)
    w_up = gaussian(key_list[9], (D, FF), D ** -0.5, 0.25)
    w_down = gaussian(key_list[10], (FF, D), FF ** -0.5, 0.125)
    cotangent = gaussian(key_list[11], (ROWS, ROW_LEN, D), 1.0, 6.0, ((0, 4), (1, 8)))
    return {"tokens": tokens, "first_len": first_len, "gain_one": gain_one, "conv_weight": conv_weight, "w_z": w_z, "bias_z": bias_z, "w_h": w_h, "w_out": w_out, "gain_two": gain_two, "w_up": w_up, "w_down": w_down, "cotangent": cotangent}


@jax.custom_vjp
def low(v):
    return lax.optimization_barrier(v.astype(jnp.bfloat16)).astype(jnp.float32)

@jax.custom_vjp
def low_back(v):
    return v

def low_keep(v):
    return (low(v), None)

def low_pass(kept, grad):
    return (grad,)

def back_keep(v):
    return (v, None)

def back_low(kept, grad):
    return (low(grad),)
low.defvjp(low_keep, low_pass)
low_back.defvjp(back_keep, back_low)

def rms_scale(values):
    return lax.rsqrt(lax.optimization_barrier(jnp.mean(values * values, axis=-1, keepdims=True)) + 1e-06)

def candidate(values):
    return jnp.where(values >= 0, values + 0.5, jax.nn.sigmoid(values))

def combine_pairs(earlier, later):
    return (earlier[0] * later[0], later[1] + later[0] * earlier[1])

def product(left, right):
    return jnp.dot(left, right, precision=lax.Precision.HIGHEST, preferred_element_type=jnp.float32)

def row_forward(inputs, first, gain_one, conv_weight, w_z, bias_z, w_h, w_out, gain_two, w_up, w_down):
    length = inputs.shape[0]
    positions = jnp.arange(length, dtype=jnp.int32)
    second_doc = (positions >= first).astype(jnp.int32)
    open_mask = (positions != first).astype(jnp.float32)[:, None]
    normed = inputs * rms_scale(inputs) * gain_one
    mixed = conv_weight[0] * normed
    for tap_index in range(1, KCONV):
        moved = jnp.concatenate([jnp.zeros((tap_index, normed.shape[1]), jnp.float32), normed[:-tap_index]], axis=0)
        moved_doc = jnp.concatenate([jnp.full((tap_index,), -1, jnp.int32), second_doc[:-tap_index]], axis=0)
        same = (moved_doc == second_doc).astype(jnp.float32)[:, None]
        mixed = mixed + conv_weight[tap_index] * moved * same
    conv_low = low(mixed)
    gate_pre = low_back(product(conv_low, w_z)) + bias_z
    cand_pre = low_back(product(conv_low, w_h))
    keep = jax.nn.sigmoid(-gate_pre) * open_mask
    drive = jax.nn.sigmoid(gate_pre) * candidate(cand_pre)
    _, state = lax.associative_scan(combine_pairs, (keep, drive), axis=0)
    middle = inputs + low_back(product(low(state), w_out))
    second = low(middle * rms_scale(middle) * gain_two)
    up_pre = low_back(product(second, w_up))
    active = low(jax.nn.gelu(up_pre, approximate=False))
    return middle + low_back(product(active, w_down))

def reference(tokens, first_len, gain_one, conv_weight, w_z, bias_z, w_h, w_out, gain_two, w_up, w_down, cotangent):
    weights = tuple((value.astype(jnp.float32) for value in (gain_one, conv_weight, w_z, bias_z, w_h, w_out, gain_two, w_up, w_down)))

    def per_row(totals, inputs):
        token_row, first, upstream = inputs

        def forward(values, *params):
            return row_forward(values, first, *params)
        result, pull = jax.vjp(forward, token_row.astype(jnp.float32), *weights)
        grads = pull(upstream.astype(jnp.float32))
        totals = tuple((total + grad for total, grad in zip(totals, grads[1:])))
        return (totals, (result.astype(jnp.bfloat16), grads[0].astype(jnp.bfloat16)))
    start = tuple((jnp.zeros(value.shape, jnp.float32) for value in weights))
    totals, (output, grad_tokens) = lax.scan(per_row, start, (tokens, first_len, cotangent))
    return (output, grad_tokens, totals[0], totals[1], totals[2], totals[3], totals[4], totals[5], totals[6], totals[7], totals[8])
```

```python
import functools

import jax
import jax.numpy as jnp
from jax import lax
from jax.experimental import pallas as pl
from jax.experimental.pallas import tpu as pltpu
from jax.sharding import PartitionSpec as P

F32, BF16 = jnp.float32, jnp.bfloat16
EPS = 1e-06
VMEM = pl.BlockSpec(memory_space=pltpu.VMEM)
SMEM = pl.BlockSpec(memory_space=pltpu.SMEM)
SUB = 8


def dot(left, right):
    return jnp.dot(left, right, preferred_element_type=F32)


def dot_lt(left, right):
    return lax.dot_general(left, right, (((0,), (0,)), ((), ())), preferred_element_type=F32)


def dot_rt(left, right):
    return lax.dot_general(left, right, (((1,), (1,)), ((), ())), preferred_element_type=F32)


def segment_order(tokens):
    steps = tokens // SUB
    to = lax.broadcasted_iota(jnp.int32, (tokens, tokens), 0)
    source = lax.broadcasted_iota(jnp.int32, (tokens, tokens), 1)
    return jnp.where(source == (to % SUB) * steps + to // SUB, 1.0, 0.0).astype(BF16)


def opened(first_len, seq_start, shape):
    sub = lax.broadcasted_iota(jnp.int32, shape, 0)
    rows = first_len.shape[0]
    result = jnp.ones(shape, F32)
    for r in range(rows):
        factor = jnp.where(first_len[r] == seq_start, 0.0, 1.0)
        result = jnp.where(sub == r * (SUB // rows), factor, result)
    return result


def at_row_start(shape, rows):
    return lax.broadcasted_iota(jnp.int32, shape, 0) % (SUB // rows) == 0


def at_row_end(shape, rows):
    parts = SUB // rows
    return lax.broadcasted_iota(jnp.int32, shape, 0) % parts == parts - 1


def rms(values):
    return lax.rsqrt(jnp.mean(values * values, axis=-1, keepdims=True) + EPS)


def fill_extended(ext, rim, first_len, seq_start, xhat_rim):
    lag, rows = rim.shape[1], rim.shape[0]
    width = ext.shape[-1]
    mask = opened(first_len, seq_start, (SUB, width))
    start = at_row_start((SUB, width), rows)
    total = ext.shape[0]
    for k in range(lag):
        near = pltpu.roll(ext[total - lag * SUB + k * SUB : total - lag * SUB + (k + 1) * SUB, :], 1, 0)
        ext[k * SUB : (k + 1) * SUB, :] = jnp.where(start, xhat_rim[k] * mask, near)


def rim_tiles(rim, spread):
    rows, lag, _ = rim.shape
    parts = SUB // rows
    spread[...] = jnp.zeros_like(spread)
    for k in range(lag):
        for r in range(rows):
            spread[k, r * parts : r * parts + 1, :] = rim[r, k : k + 1, :]
    return [spread[k] for k in range(lag)]


def gates_kernel(
    first_len, tokens, cotangent, rim, gain_one, conv_weight, w_z, bias_z, w_h,
    x_out, up_out, conv_out, keep_out, drive_out, cand_out, gate_out, pass_out, subk, subs, totals,
    ext, spread, lag_order,
):
    rows, group_len, width = tokens.shape
    count, lag = rows * group_len, rim.shape[1]
    hidden = w_z.shape[1]
    seq_start = lax.axis_index("seq") * group_len
    order = segment_order(count)
    x = dot(order, tokens[...].reshape(count, width))
    x_out[...] = x.astype(BF16)
    up_out[...] = dot(order, cotangent[...].reshape(count, width)).astype(BF16)
    normed = x * rms(x) * gain_one[...]
    ext[lag * SUB :, :] = normed
    rim_x = rim_tiles(rim, spread)
    fill_extended(ext, rim, first_len, seq_start, [v * rms(v) * gain_one[...] for v in rim_x])
    mixed = jnp.zeros((count, width), F32)
    for j in range(lag + 1):
        begin = (lag - j) * SUB
        mixed = mixed + conv_weight[j : j + 1, :] * ext[begin : begin + count, :]
    conv_low = mixed.astype(BF16)
    conv_out[...] = conv_low
    block = 256
    for b in range(hidden // block):
        cols = slice(b * block, (b + 1) * block)
        g = dot(conv_out[...], w_z[:, cols]) + bias_z[:, cols]
        c = dot(conv_out[...], w_h[:, cols])
        small = jnp.exp(-jnp.abs(g))
        large = 1.0 / (1.0 + small)
        small = small * large
        zeta = jnp.where(g >= 0, large, small)
        keep = jnp.where(g >= 0, small, large)
        sig = 1.0 / (1.0 + jnp.exp(-c))
        cand = jnp.where(c >= 0, c + 0.5, sig)
        keep_out[:, cols] = keep
        drive_out[:, cols] = zeta * cand
        cand_out[:, cols] = cand
        gate_out[:, cols] = small * large
        pass_out[:, cols] = zeta * jnp.where(c >= 0, 1.0, sig * (1.0 - sig))
    keep_out[0:SUB, :] = keep_out[0:SUB, :] * opened(first_len, seq_start, (SUB, hidden))

    def step(i, carry):
        total, state = carry
        at = pl.ds(pl.multiple_of(i * SUB, SUB), SUB)
        keep = keep_out[at, :]
        return total * keep, keep * state + drive_out[at, :]

    total, state = lax.fori_loop(
        0, count // SUB, step, (jnp.ones((SUB, hidden), F32), jnp.zeros((SUB, hidden), F32)), unroll=8
    )
    subk[...] = total
    subs[...] = state
    parts = SUB // rows
    for r in range(rows):
        at = slice(r * parts, r * parts + 1)
        k, s = subk[at, :], subs[at, :]
        for h in range(1, parts):
            at = slice(r * parts + h, r * parts + h + 1)
            s = subs[at, :] + subk[at, :] * s
            k = k * subk[at, :]
        totals[0, r : r + 1, :] = k
        totals[1, r : r + 1, :] = s


def mlp_kernel(
    first_len, carried, subk, subs, keep, drive, x, up, w_out, gain_two, w_up, w_down,
    state_out, before_out, low_out, middle_out, output, second_grad, grad_up, grad_down,
    second_low, tail,
):
    count, width = x.shape
    hidden, ff = keep.shape[1], w_up.shape[1]
    rows = carried.shape[0]
    group_len = count // rows
    parts = SUB // rows
    seq_start = lax.axis_index("seq") * group_len
    mask = opened(first_len, seq_start, (SUB, hidden))
    for r in range(rows):
        s = carried[r : r + 1, :]
        before_out[r * parts : r * parts + 1, :] = s
        for h in range(1, parts):
            at = slice(r * parts + h - 1, r * parts + h)
            s = subs[at, :] + subk[at, :] * s
            before_out[r * parts + h : r * parts + h + 1, :] = s
    before_out[...] = before_out[...] * mask

    def step(i, state):
        at = pl.ds(pl.multiple_of(i * SUB, SUB), SUB)
        state = keep[at, :] * state + drive[at, :]
        state_out[at, :] = state
        return state

    lax.fori_loop(0, count // SUB, step, before_out[...], unroll=8)
    low_out[...] = state_out[...].astype(BF16)
    middle = x[...].astype(F32) + dot(low_out[...], w_out[...])
    middle_out[...] = middle
    second_low[...] = (middle * rms(middle) * gain_two[...]).astype(BF16)
    block = 256

    def part(b, carry):
        cols = pl.ds(pl.multiple_of(b * block, block), block)
        pre = dot(second_low[...], w_up[:, cols])
        back = dot_rt(up[...], w_down[cols, :])
        scaled = pre * 0.7071067811865476
        phi = 0.5 + 0.5 * lax.erf(scaled)
        active = (pre * phi).astype(BF16)
        slope = phi + pre * (0.3989422804014327 * jnp.exp(-scaled * scaled))
        up_low = (slope * back).astype(BF16)
        grad_down[cols, :] = dot_lt(active, up[...])
        grad_up[:, cols] = dot_lt(second_low[...], up_low)
        out_part = dot(active, w_down[cols, :])
        grad_part = dot_rt(up_low, w_up[:, cols])

        @pl.when(b == 0)
        def _():
            tail[...] = out_part
            second_grad[...] = grad_part

        @pl.when(b > 0)
        def _():
            tail[...] += out_part
            second_grad[...] += grad_part

        return carry

    lax.fori_loop(0, ff // block, part, 0)
    order = segment_order(count)
    result = (middle_out[...] + tail[...]).astype(BF16)
    output[...] = dot_lt(order, result).astype(BF16).reshape(output.shape)


def middle_kernel(
    middle_ref, second_grad, up, gain_two, state_low, w_out, keep, subk,
    grad_middle_out, grad_gain_two, grad_out, grad_state, subb, totals,
):
    count, width = middle_ref.shape
    hidden = keep.shape[1]
    rows = totals.shape[0]
    middle = middle_ref[...]
    scale = rms(middle)
    unit = middle * scale
    grad = second_grad[...]
    grad_gain_two[...] = jnp.sum(grad * unit, axis=0, keepdims=True)
    grad = grad * gain_two[...]
    grad_middle = up[...].astype(F32) + scale * (grad - unit * jnp.mean(grad * unit, axis=-1, keepdims=True))
    grad_middle_out[...] = grad_middle
    middle_low = grad_middle.astype(BF16)
    grad_state[...] = dot_rt(middle_low, w_out[...])
    grad_out[...] = dot_lt(state_low[...], middle_low)
    steps = count // SUB

    def step(i, passed):
        at = pl.ds(pl.multiple_of((steps - 1 - i) * SUB, SUB), SUB)
        return keep[at, :] * (grad_state[at, :] + passed)

    subb[...] = lax.fori_loop(0, steps, step, jnp.zeros((SUB, hidden), F32), unroll=8)
    parts = SUB // rows
    for r in range(rows):
        end = r * parts + parts - 1
        b = subb[end : end + 1, :]
        for h in range(parts - 2, -1, -1):
            at = slice(r * parts + h, r * parts + h + 1)
            b = subb[at, :] + subk[at, :] * b
        totals[r : r + 1, :] = b


def first_kernel(
    first_len, returned, subk, subb, keep, grad_state, state, before, cand, gate, passing, conv_low,
    x_ref, rim, gain_one, conv_weight, w_z, w_h, grad_middle, grad_gain_two,
    grad_z, grad_h, small, grad_tokens, sent, tail_normed, tail_middle,
    incoming, gate_low, cand_low, ext, spread, grad_ext, bias_sum,
):
    count, width = x_ref.shape
    hidden = keep.shape[1]
    rows, lag = rim.shape[0], rim.shape[1]
    parts = SUB // rows
    steps = count // SUB
    seq_start = lax.axis_index("seq") * (count // rows)
    for r in range(rows):
        b = returned[r : r + 1, :]
        incoming[r * parts + parts - 1 : (r + 1) * parts, :] = b
        for h in range(parts - 2, -1, -1):
            at = slice(r * parts + h + 1, r * parts + h + 2)
            b = subb[at, :] + subk[at, :] * b
            incoming[r * parts + h : r * parts + h + 1, :] = b
    def one(step_at, passed, bias):
        at = pl.ds(pl.multiple_of(step_at * SUB, SUB), SUB)
        prior = pl.ds(pl.multiple_of(jnp.maximum(step_at - 1, 0) * SUB, SUB), SUB)
        adjoint = grad_state[at, :] + passed
        earlier = jnp.where(step_at > 0, state[prior, :], before[...])
        grad_g = adjoint * (cand[at, :] - earlier) * gate[at, :]
        return keep[at, :] * adjoint, bias + grad_g, grad_g, adjoint * passing[at, :]

    def two(i, carry):
        pair = steps // 2 - 1 - i
        passed, bias, late_g, late_c = one(2 * pair + 1, *carry)
        passed, bias, early_g, early_c = one(2 * pair, passed, bias)
        at = pl.ds(pl.multiple_of(pair * 2 * SUB, 2 * SUB), 2 * SUB)
        gate_low[at, :] = jnp.concatenate([early_g, late_g], axis=0).astype(BF16)
        cand_low[at, :] = jnp.concatenate([early_c, late_c], axis=0).astype(BF16)
        return passed, bias

    _, bias = lax.fori_loop(
        0, steps // 2, two, (incoming[...], jnp.zeros((SUB, hidden), F32)), unroll=2
    )
    bias_sum[...] = jnp.sum(bias, axis=0, keepdims=True)
    grad_z[...] = dot_lt(conv_low[...], gate_low[...])
    grad_h[...] = dot_lt(conv_low[...], cand_low[...])
    grad_mixed = dot_rt(gate_low[...], w_z[...]) + dot_rt(cand_low[...], w_h[...])

    x = x_ref[...].astype(F32)
    scale = rms(x)
    unit = x * scale
    gain = gain_one[...]
    ext[lag * SUB :, :] = unit * gain
    rim_x = rim_tiles(rim, spread)
    rim_unit = [v * rms(v) for v in rim_x]
    fill_extended(ext, rim, first_len, seq_start, [v * gain for v in rim_unit])
    small[0:1, :] = jnp.zeros((1, width), F32)
    for j in range(lag + 1):
        begin = (lag - j) * SUB
        small[1 + j : 2 + j, :] = jnp.sum(grad_mixed * ext[begin : begin + count, :], axis=0, keepdims=True)
    for j in range(hidden // width):
        at = 2 + lag + j
        small[at : at + 1, :] = bias_sum[:, j * width : (j + 1) * width]
    last = 2 + lag + hidden // width
    small[last : last + 1, :] = grad_gain_two[...]
    grad_ext[...] = jnp.zeros_like(grad_ext)
    for j in range(lag + 1):
        begin = (lag - j) * SUB
        grad_ext[begin : begin + count, :] += conv_weight[j : j + 1, :] * grad_mixed
    mask = opened(first_len, seq_start, (SUB, width))
    start = at_row_start((SUB, width), rows)
    end = at_row_end((SUB, width), rows)
    grad_gain = jnp.zeros((SUB, width), F32)
    for k in range(lag):
        head = grad_ext[k * SUB : (k + 1) * SUB, :]
        tail_at = pl.ds(count + k * SUB, SUB)
        near = pltpu.roll(head, SUB - 1, 0)
        grad_ext[tail_at, :] = grad_ext[tail_at, :] + jnp.where(end, 0.0, near)
        to_rim = jnp.where(start, head * mask, 0.0)
        grad_gain = grad_gain + to_rim * rim_unit[k]
        spread[k] = to_rim
        for r in range(rows):
            sent[r, k : k + 1, :] = spread[k, r * parts : r * parts + 1, :]
    grad_normed = grad_ext[lag * SUB :, :]
    small[0:1, :] = jnp.sum(grad_normed * unit, axis=0, keepdims=True) + jnp.sum(
        grad_gain, axis=0, keepdims=True
    )
    for k in range(lag):
        at = count - lag * SUB + k * SUB
        for r in range(rows):
            row = at + r * parts + parts - 1
            to = tail_normed.shape[1] - lag + k
            tail_normed[r, to : to + 1, :] = grad_ext[lag * SUB + row : lag * SUB + row + 1, :]
            tail_middle[r, to : to + 1, :] = grad_middle[row : row + 1, :]
    grad = grad_normed * gain
    grad_x = grad_middle[...] + scale * (grad - unit * jnp.mean(grad * unit, axis=-1, keepdims=True))
    order = segment_order(count)
    grad_tokens[...] = dot_lt(order, grad_x.astype(BF16)).astype(BF16).reshape(grad_tokens.shape)


def tail_kernel(tokens, tail_normed, tail_middle, received, gain_one, _, grad_tokens, spread):
    rows, tile, width = tokens.shape
    lag = received.shape[1]
    for r in range(rows):
        spread[tile - lag :, :] = tail_normed[r, tile - lag :, :] + received[r]
        x = tokens[r].astype(F32)
        scale = rms(x)
        unit = x * scale
        grad = spread[...] * gain_one[...]
        fixed = tail_middle[r] + scale * (grad - unit * jnp.mean(grad * unit, axis=-1, keepdims=True))
        changed = lax.broadcasted_iota(jnp.int32, (tile, width), 0) >= tile - lag
        grad_tokens[r] = jnp.where(changed, fixed, _[r].astype(F32)).astype(BF16)


def shaped(*shapes):
    return tuple(jax.ShapeDtypeStruct(shape, kind) for shape, kind in shapes)


def call(kernel, in_specs, outs, scratch, flops, **more):
    return pl.pallas_call(
        kernel,
        in_specs=in_specs,
        out_specs=(VMEM,) * len(outs),
        out_shape=shaped(*outs),
        scratch_shapes=[pltpu.VMEM(shape, kind) for shape, kind in scratch],
        compiler_params=pltpu.CompilerParams(vmem_limit_bytes=40 << 20),
        cost_estimate=pl.CostEstimate(flops=flops, bytes_accessed=1 << 20, transcendentals=0),
        **more,
    )


def swapped(array, axis, bit):
    return lax.ppermute(array, axis, [(i, i ^ bit) for i in range(lax.axis_size(axis))])


def bits_of(axis):
    bit, result = 1, []
    while bit < lax.axis_size(axis):
        result.append(bit)
        bit *= 2
    return result


def upper(axis, bit):
    return (lax.axis_index(axis) // bit) % 2 == 1


def carry_forward(totals):
    keep, state = totals[0], totals[1]
    before_k, before_s = jnp.ones_like(keep), jnp.zeros_like(state)
    levels = []
    for bit in bits_of("seq"):
        other = swapped(jnp.stack([keep, state]), "seq", bit)
        other_k, other_s = other[0], other[1]
        late = upper("seq", bit)
        levels.append((keep, other_k))
        before_s = jnp.where(late, before_s + before_k * other_s, before_s)
        before_k = jnp.where(late, before_k * other_k, before_k)
        state = jnp.where(late, state + keep * other_s, other_s + other_k * state)
        keep = keep * other_k
    return before_s, levels


def carry_backward(passed, levels):
    after_b, after_k = jnp.zeros_like(passed), jnp.ones_like(passed)
    for bit, (keep, other_k) in zip(bits_of("seq"), levels):
        other_b = swapped(passed, "seq", bit)
        late = upper("seq", bit)
        after_b = jnp.where(late, after_b, after_b + after_k * other_b)
        after_k = jnp.where(late, after_k, after_k * other_k)
        passed = jnp.where(late, other_b + other_k * passed, passed + keep * other_b)
    return after_b


def per_device(
    tokens, first_len, gain_one, conv_weight, w_z, bias_z, w_h, w_out, gain_two, w_up, w_down, cotangent
):
    rows, group_len, width = tokens.shape
    hidden, ff = w_z.shape[1], w_up.shape[1]
    lag = conv_weight.shape[0] - 1
    count = rows * group_len
    devices = lax.axis_size("seq")
    gain_one, gain_two, bias_z = gain_one[None], gain_two[None], bias_z[None]
    rim = lax.ppermute(
        tokens[:, group_len - lag :].astype(F32), "seq", [(i, i + 1) for i in range(devices - 1)]
    )
    th, tw = (count, hidden), (count, width)
    x, up, conv_low, keep, drive, cand, gate, passing, subk, subs, totals = call(
        gates_kernel,
        [SMEM] + [VMEM] * 8,
        [(tw, BF16), (tw, BF16), (tw, BF16)] + [(th, F32)] * 5
        + [((SUB, hidden), F32)] * 2 + [((2, rows, hidden), F32)],
        [((count + lag * SUB, width), F32), ((lag, SUB, width), F32), ((8, 128), F32)],
        4 * count * width * hidden,
    )(first_len, tokens, cotangent, rim, gain_one, conv_weight, w_z, bias_z, w_h)
    carried, levels = carry_forward(totals)
    state, before, state_low, middle, output, second_grad, grad_up, grad_down = call(
        mlp_kernel,
        [SMEM] + [VMEM] * 11,
        [(th, F32), ((SUB, hidden), F32), (th, BF16), (tw, F32), (tokens.shape, BF16), (tw, F32),
         ((width, ff), F32), ((ff, width), F32)],
        [(tw, BF16), (tw, F32)],
        12 * count * width * ff,
    )(first_len, carried, subk, subs, keep, drive, x, up, w_out, gain_two, w_up, w_down)
    grad_middle, grad_gain_two, grad_out, grad_state, subb, passed = call(
        middle_kernel,
        [VMEM] * 8,
        [(tw, F32), ((1, width), F32), ((hidden, width), F32), (th, F32), ((SUB, hidden), F32),
         ((rows, hidden), F32)],
        [],
        4 * count * width * hidden,
    )(middle, second_grad, up, gain_two, state_low, w_out, keep, subk)
    returned = carry_backward(passed, levels)
    tile = 16
    grad_z, grad_h, small, grad_tokens, sent, tail_normed, tail_middle = call(
        first_kernel,
        [SMEM] + [VMEM] * 19,
        [((width, hidden), F32)] * 2 + [((SUB, width), F32), (tokens.shape, BF16),
         ((rows, lag, width), F32)] + [((rows, tile, width), F32)] * 2,
        [((SUB, hidden), F32), (th, BF16), (th, BF16), ((count + lag * SUB, width), F32),
         ((lag, SUB, width), F32), ((count + lag * SUB, width), F32), ((1, hidden), F32)],
        8 * count * width * hidden,
    )(first_len, returned, subk, subb, keep, grad_state, state, before, cand, gate, passing, conv_low,
      x, rim, gain_one, conv_weight, w_z, w_h, grad_middle, grad_gain_two)
    received = lax.ppermute(sent, "seq", [(i + 1, i) for i in range(devices - 1)])
    at_tail = pl.BlockSpec((rows, tile, width), lambda i: (0, group_len // tile - 1, 0))
    whole = lambda *shape: pl.BlockSpec(shape, lambda i: (0,) * len(shape))
    grad_tokens = pl.pallas_call(
        tail_kernel,
        grid=(1,),
        in_specs=[at_tail, whole(rows, tile, width), whole(rows, tile, width), whole(rows, lag, width),
                  whole(1, width), at_tail],
        out_specs=at_tail,
        out_shape=jax.ShapeDtypeStruct(tokens.shape, BF16),
        scratch_shapes=[pltpu.VMEM((tile, width), F32)],
        input_output_aliases={5: 0},
    )(tokens, tail_normed, tail_middle, received, gain_one, grad_tokens)
    axes = ("row", "seq")
    grad_down, grad_up, grad_out, grad_z, grad_h, small = lax.psum(
        (grad_down, grad_up, grad_out, grad_z, grad_h, small), axes
    )
    bias_at = 2 + lag
    gain_at = bias_at + hidden // width
    return (
        output,
        grad_tokens,
        small[0],
        small[1:bias_at],
        grad_z,
        small[bias_at:gain_at].reshape(hidden),
        grad_h,
        grad_out,
        small[gain_at],
        grad_up,
        grad_down,
    )


def solution(mesh):
    block, copied = P("row", "seq", None), P()
    return jax.shard_map(
        per_device,
        mesh=mesh,
        in_specs=(block, P("row")) + (copied,) * 9 + (block,),
        out_specs=(block, block) + (copied,) * 9,
        check_vma=False,
    )
```

```python
import functools

import jax
import jax.numpy as jnp
from jax import lax
from jax.experimental import pallas as pl
from jax.experimental.pallas import tpu as pltpu
from jax.sharding import PartitionSpec as P

F32, BF16 = jnp.float32, jnp.bfloat16
EPS = 1e-06
VMEM = pl.BlockSpec(memory_space=pltpu.VMEM)
SMEM = pl.BlockSpec(memory_space=pltpu.SMEM)
KINDS = "TSST"
EARLY = (0, 1, 0, 1)
SUB = 8


def dot(left, right):
    return jnp.dot(left, right, preferred_element_type=F32)


def dot_lt(left, right):
    return lax.dot_general(left, right, (((0,), (0,)), ((), ())), preferred_element_type=F32)


def dot_rt(left, right):
    return lax.dot_general(left, right, (((1,), (1,)), ((), ())), preferred_element_type=F32)


def segment_order(tokens):
    steps = tokens // SUB
    to = lax.broadcasted_iota(jnp.int32, (tokens, tokens), 0)
    source = lax.broadcasted_iota(jnp.int32, (tokens, tokens), 1)
    return jnp.where(source == (to % SUB) * steps + to // SUB, 1.0, 0.0).astype(BF16)


def opened(first_len, seq_start, shape):
    sub = lax.broadcasted_iota(jnp.int32, shape, 0)
    rows = first_len.shape[0]
    result = jnp.ones(shape, F32)
    for r in range(rows):
        factor = jnp.where(first_len[r] == seq_start, 0.0, 1.0)
        result = jnp.where(sub == r * (SUB // rows), factor, result)
    return result


def at_row_start(shape, rows):
    return lax.broadcasted_iota(jnp.int32, shape, 0) % (SUB // rows) == 0


def at_row_end(shape, rows):
    parts = SUB // rows
    return lax.broadcasted_iota(jnp.int32, shape, 0) % parts == parts - 1


def rms(values):
    return lax.rsqrt(jnp.mean(values * values, axis=-1, keepdims=True) + EPS)


def fill_extended(ext, rim, first_len, seq_start, xhat_rim):
    lag, rows = rim.shape[1], rim.shape[0]
    width = ext.shape[-1]
    mask = opened(first_len, seq_start, (SUB, width))
    start = at_row_start((SUB, width), rows)
    total = ext.shape[0]
    for k in range(lag):
        near = pltpu.roll(ext[total - lag * SUB + k * SUB : total - lag * SUB + (k + 1) * SUB, :], 1, 0)
        ext[k * SUB : (k + 1) * SUB, :] = jnp.where(start, xhat_rim[k] * mask, near)


def rim_tiles(rim, spread):
    rows, lag, _ = rim.shape
    parts = SUB // rows
    spread[...] = jnp.zeros_like(spread)
    for k in range(lag):
        for r in range(rows):
            spread[k, r * parts : r * parts + 1, :] = rim[r, k : k + 1, :]
    return [spread[k] for k in range(lag)]


def gates_kernel(
    first_len, tokens, cotangent, rim, gain_one, conv_weight, w_z, bias_z, w_h,
    x_out, up_out, conv_out, keep_out, drive_out, cand_out, gate_out, pass_out, subk, subs, totals,
    ext, spread, lag_order,
):
    rows, group_len, width = tokens.shape
    count, lag = rows * group_len, rim.shape[1]
    hidden = w_z.shape[1]
    seq_start = lax.axis_index("seq") * group_len
    order = segment_order(count)
    x = dot(order, tokens[...].reshape(count, width))
    x_out[...] = x.astype(BF16)
    up_out[...] = dot(order, cotangent[...].reshape(count, width)).astype(BF16)
    normed = x * rms(x) * gain_one[...]
    ext[lag * SUB :, :] = normed
    rim_x = rim_tiles(rim, spread)
    fill_extended(ext, rim, first_len, seq_start, [v * rms(v) * gain_one[...] for v in rim_x])
    mixed = jnp.zeros((count, width), F32)
    for j in range(lag + 1):
        begin = (lag - j) * SUB
        mixed = mixed + conv_weight[j : j + 1, :] * ext[begin : begin + count, :]
    conv_low = mixed.astype(BF16)
    conv_out[...] = conv_low
    block = 256
    for b in range(hidden // block):
        cols = slice(b * block, (b + 1) * block)
        g = dot(conv_out[...], w_z[:, cols]) + bias_z[:, cols]
        c = dot(conv_out[...], w_h[:, cols])
        small = jnp.exp(-jnp.abs(g))
        large = 1.0 / (1.0 + small)
        small = small * large
        zeta = jnp.where(g >= 0, large, small)
        keep = jnp.where(g >= 0, small, large)
        sig = 1.0 / (1.0 + jnp.exp(-c))
        cand = jnp.where(c >= 0, c + 0.5, sig)
        keep_out[:, cols] = keep
        drive_out[:, cols] = zeta * cand
        cand_out[:, cols] = cand
        gate_out[:, cols] = small * large
        pass_out[:, cols] = zeta * jnp.where(c >= 0, 1.0, sig * (1.0 - sig))
    keep_out[0:SUB, :] = keep_out[0:SUB, :] * opened(first_len, seq_start, (SUB, hidden))

    def step(i, carry):
        total, state = carry
        at = pl.ds(pl.multiple_of(i * SUB, SUB), SUB)
        keep = keep_out[at, :]
        return total * keep, keep * state + drive_out[at, :]

    total, state = lax.fori_loop(
        0, count // SUB, step, (jnp.ones((SUB, hidden), F32), jnp.zeros((SUB, hidden), F32)), unroll=8
    )
    subk[...] = total
    subs[...] = state
    parts = SUB // rows
    for r in range(rows):
        at = slice(r * parts, r * parts + 1)
        k, s = subk[at, :], subs[at, :]
        for h in range(1, parts):
            at = slice(r * parts + h, r * parts + h + 1)
            s = subs[at, :] + subk[at, :] * s
            k = k * subk[at, :]
        totals[0, r : r + 1, :] = k
        totals[1, r : r + 1, :] = s


def by_core(first, mine, other, at, for_even, for_odd):
    @pl.when(first)
    def _():
        mine[at, :] = for_even
        other[at, :] = for_odd

    @pl.when(jnp.logical_not(first))
    def _():
        mine[at, :] = for_odd
        other[at, :] = for_even


def mlp_kernel(
    first_len, carried, subk, subs, keep, drive, x, up, w_out, gain_two, w_up, w_down,
    state_out, before_out, output, mine_a, other_a, mine_b, other_b,
    grad_middle_out, grad_gain_two, grad_state, subb, totals,
    low, second_low, tail, second_grad, middle_ref,
):
    count, width = x.shape
    hidden, ff = keep.shape[1], w_up.shape[1]
    rows = carried.shape[0]
    group_len = count // rows
    parts = SUB // rows
    steps = count // SUB
    seq_start = lax.axis_index("seq") * group_len
    even = lax.axis_index("row") % 2 == 0
    mask = opened(first_len, seq_start, (SUB, hidden))
    for r in range(rows):
        s = carried[r : r + 1, :]
        before_out[r * parts : r * parts + 1, :] = s
        for h in range(1, parts):
            at = slice(r * parts + h - 1, r * parts + h)
            s = subs[at, :] + subk[at, :] * s
            before_out[r * parts + h : r * parts + h + 1, :] = s
    before_out[...] = before_out[...] * mask

    def step(i, state):
        at = pl.ds(pl.multiple_of(i * SUB, SUB), SUB)
        state = keep[at, :] * state + drive[at, :]
        state_out[at, :] = state
        return state

    lax.fori_loop(0, steps, step, before_out[...], unroll=8)
    low[...] = state_out[...].astype(BF16)
    middle = x[...].astype(F32) + dot(low[...], w_out[...])
    middle_ref[...] = middle
    second_low[...] = (middle * rms(middle) * gain_two[...]).astype(BF16)
    tail[...] = jnp.zeros_like(tail)
    second_grad[...] = jnp.zeros_like(second_grad)
    block = width
    half = ff // block // 2
    for mine, other, begin in ((mine_a, other_a, 0), (mine_b, other_b, half)):

        def part(b, carry):
            cols = pl.ds(pl.multiple_of((b + begin) * block, block), block)
            at = pl.ds(pl.multiple_of(b * block, block), block)
            pre = dot(second_low[...], w_up[:, cols])
            back = dot_rt(up[...], w_down[cols, :])
            scaled = pre * 0.7071067811865476
            phi = 0.5 + 0.5 * lax.erf(scaled)
            active = (pre * phi).astype(BF16)
            slope = phi + pre * (0.3989422804014327 * jnp.exp(-scaled * scaled))
            up_low = (slope * back).astype(BF16)
            by_core(even, mine, other, at, dot_lt(active, up[...]), dot_lt(second_low[...], up_low))
            tail[...] += dot(active, w_down[cols, :])
            second_grad[...] += dot_rt(up_low, w_up[:, cols])
            return carry

        lax.fori_loop(0, half, part, 0)
    order = segment_order(count)
    result = (middle_ref[...] + tail[...]).astype(BF16)
    output[...] = dot_lt(order, result).astype(BF16).reshape(output.shape)

    middle = middle_ref[...]
    scale = rms(middle)
    unit = middle * scale
    grad = second_grad[...]
    grad_gain_two[...] = jnp.sum(grad * unit, axis=0, keepdims=True)
    grad = grad * gain_two[...]
    grad_middle = up[...].astype(F32) + scale * (grad - unit * jnp.mean(grad * unit, axis=-1, keepdims=True))
    grad_middle_out[...] = grad_middle
    middle_low = grad_middle.astype(BF16)
    grad_state[...] = dot_rt(middle_low, w_out[...])
    half_h = hidden // 2
    by_core(
        even, mine_b, other_b, slice(half * block, half * block + half_h),
        dot_lt(low[:, :half_h], middle_low), dot_lt(low[:, half_h:], middle_low),
    )

    def back_step(i, passed):
        at = pl.ds(pl.multiple_of((steps - 1 - i) * SUB, SUB), SUB)
        return keep[at, :] * (grad_state[at, :] + passed)

    subb[...] = lax.fori_loop(0, steps, back_step, jnp.zeros((SUB, hidden), F32), unroll=8)
    for r in range(rows):
        end = r * parts + parts - 1
        b = subb[end : end + 1, :]
        for h in range(parts - 2, -1, -1):
            at = slice(r * parts + h, r * parts + h + 1)
            b = subb[at, :] + subk[at, :] * b
        totals[r : r + 1, :] = b


def first_kernel(
    first_len, returned, subk, subb, keep, grad_state, state, before, cand, gate, passing, conv_low,
    x_ref, rim, gain_one, conv_weight, w_z, w_h, grad_middle, grad_gain_two, token,
    mine_a, other_a, mine_b, other_b, grad_tokens, sent, tail_normed, tail_middle,
    incoming, gate_low, cand_low, ext, spread, grad_ext, bias_sum, small,
):
    count, width = x_ref.shape
    hidden = keep.shape[1]
    rows, lag = rim.shape[0], rim.shape[1]
    parts = SUB // rows
    steps = count // SUB
    seq_start = lax.axis_index("seq") * (count // rows)
    for r in range(rows):
        b = returned[r : r + 1, :]
        incoming[r * parts + parts - 1 : (r + 1) * parts, :] = b
        for h in range(parts - 2, -1, -1):
            at = slice(r * parts + h + 1, r * parts + h + 2)
            b = subb[at, :] + subk[at, :] * b
            incoming[r * parts + h : r * parts + h + 1, :] = b
    def one(step_at, passed, bias):
        at = pl.ds(pl.multiple_of(step_at * SUB, SUB), SUB)
        prior = pl.ds(pl.multiple_of(jnp.maximum(step_at - 1, 0) * SUB, SUB), SUB)
        adjoint = grad_state[at, :] + passed
        earlier = jnp.where(step_at > 0, state[prior, :], before[...])
        grad_g = adjoint * (cand[at, :] - earlier) * gate[at, :]
        return keep[at, :] * adjoint, bias + grad_g, grad_g, adjoint * passing[at, :]

    def two(i, carry):
        pair = steps // 2 - 1 - i
        passed, bias, late_g, late_c = one(2 * pair + 1, *carry)
        passed, bias, early_g, early_c = one(2 * pair, passed, bias)
        at = pl.ds(pl.multiple_of(pair * 2 * SUB, 2 * SUB), 2 * SUB)
        gate_low[at, :] = jnp.concatenate([early_g, late_g], axis=0).astype(BF16)
        cand_low[at, :] = jnp.concatenate([early_c, late_c], axis=0).astype(BF16)
        return passed, bias

    _, bias = lax.fori_loop(
        0, steps // 2, two, (incoming[...], jnp.zeros((SUB, hidden), F32)), unroll=2
    )
    bias_sum[...] = jnp.sum(bias, axis=0, keepdims=True)
    even = lax.axis_index("row") % 2 == 0
    half = width // 2
    for k, (mine, other) in enumerate(((mine_a, other_a), (mine_b, other_b))):
        cols = slice(k * half, (k + 1) * half)
        by_core(
            even, mine.at[:, :hidden], other.at[:, :hidden], slice(0, half),
            dot_lt(conv_low[:, cols], gate_low[...]), dot_lt(conv_low[:, cols], cand_low[...]),
        )
    grad_mixed = dot_rt(gate_low[...], w_z[...]) + dot_rt(cand_low[...], w_h[...])

    x = x_ref[...].astype(F32)
    scale = rms(x)
    unit = x * scale
    gain = gain_one[...]
    ext[lag * SUB :, :] = unit * gain
    rim_x = rim_tiles(rim, spread)
    rim_unit = [v * rms(v) for v in rim_x]
    fill_extended(ext, rim, first_len, seq_start, [v * gain for v in rim_unit])
    small[0:1, :] = jnp.zeros((1, width), F32)
    for j in range(lag + 1):
        begin = (lag - j) * SUB
        small[1 + j : 2 + j, :] = jnp.sum(grad_mixed * ext[begin : begin + count, :], axis=0, keepdims=True)
    for j in range(hidden // width):
        at = 2 + lag + j
        small[at : at + 1, :] = bias_sum[:, j * width : (j + 1) * width]
    last = 2 + lag + hidden // width
    small[last : last + 1, :] = grad_gain_two[...]
    grad_ext[...] = jnp.zeros_like(grad_ext)
    for j in range(lag + 1):
        begin = (lag - j) * SUB
        grad_ext[begin : begin + count, :] += conv_weight[j : j + 1, :] * grad_mixed
    mask = opened(first_len, seq_start, (SUB, width))
    start = at_row_start((SUB, width), rows)
    end = at_row_end((SUB, width), rows)
    grad_gain = jnp.zeros((SUB, width), F32)
    for k in range(lag):
        head = grad_ext[k * SUB : (k + 1) * SUB, :]
        tail_at = pl.ds(count + k * SUB, SUB)
        near = pltpu.roll(head, SUB - 1, 0)
        grad_ext[tail_at, :] = grad_ext[tail_at, :] + jnp.where(end, 0.0, near)
        to_rim = jnp.where(start, head * mask, 0.0)
        grad_gain = grad_gain + to_rim * rim_unit[k]
        spread[k] = to_rim
        for r in range(rows):
            sent[r, k : k + 1, :] = spread[k, r * parts : r * parts + 1, :]
    grad_normed = grad_ext[lag * SUB :, :]
    small[0:1, :] = jnp.sum(grad_normed * unit, axis=0, keepdims=True) + jnp.sum(
        grad_gain, axis=0, keepdims=True
    )
    for mine, keeps in ((mine_b, even), (other_b, jnp.logical_not(even))):

        @pl.when(keeps)
        def _():
            mine[:, hidden:] = jnp.zeros((half, 128), F32)
            for j in range(width // 128):
                mine[j * SUB : (j + 1) * SUB, hidden:] = small[:, j * 128 : (j + 1) * 128]

    for k in range(lag):
        at = count - lag * SUB + k * SUB
        for r in range(rows):
            row = at + r * parts + parts - 1
            to = tail_normed.shape[1] - lag + k
            tail_normed[r, to : to + 1, :] = grad_ext[lag * SUB + row : lag * SUB + row + 1, :]
            tail_middle[r, to : to + 1, :] = grad_middle[row : row + 1, :]
    grad = grad_normed * gain
    grad_x = grad_middle[...] + scale * (grad - unit * jnp.mean(grad * unit, axis=-1, keepdims=True))
    order = segment_order(count)
    grad_tokens[...] = dot_lt(order, grad_x.astype(BF16)).astype(BF16).reshape(grad_tokens.shape)


def tail_kernel(tokens, tail_normed, tail_middle, received, gain_one, _, grad_tokens, spread):
    rows, tile, width = tokens.shape
    lag = received.shape[1]
    for r in range(rows):
        spread[tile - lag :, :] = tail_normed[r, tile - lag :, :] + received[r]
        x = tokens[r].astype(F32)
        scale = rms(x)
        unit = x * scale
        grad = spread[...] * gain_one[...]
        fixed = tail_middle[r] + scale * (grad - unit * jnp.mean(grad * unit, axis=-1, keepdims=True))
        changed = lax.broadcasted_iota(jnp.int32, (tile, width), 0) >= tile - lag
        grad_tokens[r] = jnp.where(changed, fixed, _[r].astype(F32)).astype(BF16)


def shaped(*shapes):
    return tuple(jax.ShapeDtypeStruct(shape, kind) for shape, kind in shapes)


def call(kernel, in_specs, outs, scratch, flops, **more):
    return pl.pallas_call(
        kernel,
        in_specs=in_specs,
        out_specs=(VMEM,) * len(outs),
        out_shape=shaped(*outs),
        scratch_shapes=[pltpu.VMEM(shape, kind) for shape, kind in scratch],
        compiler_params=pltpu.CompilerParams(vmem_limit_bytes=20 << 20),
        cost_estimate=pl.CostEstimate(flops=flops, bytes_accessed=1 << 20, transcendentals=0),
        **more,
    )


def swapped(array, axis, bit):
    return lax.ppermute(array, axis, [(i, i ^ bit) for i in range(lax.axis_size(axis))])


def bits_of(axis):
    bit, result = 1, []
    while bit < lax.axis_size(axis):
        result.append(bit)
        bit *= 2
    return result


def upper(axis, bit):
    return (lax.axis_index(axis) // bit) % 2 == 1


def carry_forward(totals):
    keep, state = totals[0], totals[1]
    before_k, before_s = jnp.ones_like(keep), jnp.zeros_like(state)
    levels = []
    for bit in bits_of("seq"):
        other = swapped(jnp.stack([keep, state]), "seq", bit)
        other_k, other_s = other[0], other[1]
        late = upper("seq", bit)
        levels.append((keep, other_k))
        before_s = jnp.where(late, before_s + before_k * other_s, before_s)
        before_k = jnp.where(late, before_k * other_k, before_k)
        state = jnp.where(late, state + keep * other_s, other_s + other_k * state)
        keep = keep * other_k
    return before_s, levels


def carry_backward(passed, levels):
    after_b, after_k = jnp.zeros_like(passed), jnp.ones_like(passed)
    for bit, (keep, other_k) in zip(bits_of("seq"), levels):
        other_b = swapped(passed, "seq", bit)
        late = upper("seq", bit)
        after_b = jnp.where(late, after_b, after_b + after_k * other_b)
        after_k = jnp.where(late, after_k, after_k * other_k)
        passed = jnp.where(late, other_b + other_k * passed, passed + keep * other_b)
    return after_b


BOTH = ("row", "seq")


def axis_steps(kind):
    row = [("row", bit) for bit in bits_of("row")[1:]]
    seq = [("seq", bit) for bit in bits_of("seq")]
    near, far = seq[:1], seq[1:]
    even = {"P": near + row + far, "S": near + far + row, "T": far + near + row}[kind]
    return list(zip(even, row + near + far))


def exchanged(array, even, odd):
    rows, devices = lax.axis_size("row"), lax.axis_size("seq")
    pairs = []
    for r in range(rows):
        for s in range(devices):
            axis, bit = odd if r & 1 else even
            to = ((r ^ bit) * devices + s) if axis == "row" else (r * devices + (s ^ bit))
            pairs.append((r * devices + s, to))
    return lax.ppermute(array, BOTH, pairs)


def place_bit(even, odd):
    one, two = [lax.axis_index(axis) // bit % 2 for axis, bit in (even, odd)]
    return jnp.where(lax.axis_index("row") % 2 == 0, one, two).astype(jnp.int32).reshape(1)


def by_rows(total, body):
    chunk = next((c for c in (64, 32, 16, 8) if total % c == 0), total)
    if chunk == total:
        body(0, chunk)
        return

    def turn(i, carry):
        body(pl.multiple_of(i * chunk, chunk), chunk)
        return carry

    lax.fori_loop(0, total // chunk, turn, 0)


def aligned(at, half):
    return pl.multiple_of(at, SUB) if half % SUB == 0 else at


def split_kernel(_, bit, mine, received, send, keep):
    half = send.shape[0]
    if half % SUB:
        first = mine[:half, :] + received[:half, :]
        second = mine[half:, :] + received[half:, :]
        lower = jnp.broadcast_to(bit[0] == 0, first.shape)
        send[...] = jnp.where(lower, second, first)
        keep[...] = jnp.where(lower, first, second)
        return

    def body(i, chunk):
        to = pl.ds(i, chunk)
        for out, begin in ((send, (1 - bit[0]) * half), (keep, bit[0] * half)):
            at = pl.ds(pl.multiple_of(i + begin, SUB), chunk)
            out[to, :] = mine[at, :] + received[at, :]

    by_rows(half, body)


def add_kernel(_, mine, received, out):
    def body(i, chunk):
        at = pl.ds(i, chunk)
        out[at, :] = mine[at, :] + received[at, :]

    by_rows(mine.shape[0], body)


def join_kernel(_, bit, mine, received, out):
    half = mine.shape[0]
    if half % SUB:
        lower = jnp.broadcast_to(bit[0] == 0, mine.shape)
        out[:half, :] = jnp.where(lower, mine[...], received[...])
        out[half:, :] = jnp.where(lower, received[...], mine[...])
        return

    def body(i, chunk):
        at = pl.ds(i, chunk)
        for source, begin in ((mine, bit[0] * half), (received, (1 - bit[0]) * half)):
            out[pl.ds(pl.multiple_of(i + begin, SUB), chunk), :] = source[at, :]

    by_rows(half, body)


def piece_call(kernel, specs, outs, *operands):
    return pl.pallas_call(
        kernel,
        in_specs=[pl.BlockSpec(memory_space=pl.ANY)] + specs,
        out_specs=(VMEM,) * len(outs),
        out_shape=shaped(*[(shape, F32) for shape in outs]),
        compiler_params=pltpu.CompilerParams(vmem_limit_bytes=16 << 20),
        cost_estimate=pl.CostEstimate(flops=1, bytes_accessed=1, transcendentals=0),
    )(*operands)


class Summed:
    def __init__(self, mine, other, kind):
        self.steps = axis_steps(kind)
        self.core = (("row", 1),) * 2
        self.mine, self.other, self.at = mine, other, 0
        self.width = mine.shape[1]

    def advance(self, token):
        count, at = len(self.steps), self.at
        self.at += 1
        if at == 0:
            self.received = exchanged(self.other, *self.core)
            return token
        rows = self.mine.shape[0]
        if at <= count:
            step = self.steps[at - 1]
            half = (rows // 2, self.width)
            send, self.mine = piece_call(
                split_kernel, [SMEM, VMEM, VMEM], [half, half], token, place_bit(*step), self.mine, self.received
            )
            self.received = exchanged(send, *step)
            return self.mine
        if at == count + 1:
            (self.mine,) = piece_call(add_kernel, [VMEM] * 2, [self.mine.shape], token, self.mine, self.received)
        else:
            step = self.steps[2 * count + 1 - at]
            (self.mine,) = piece_call(
                join_kernel, [SMEM, VMEM, VMEM], [(2 * rows, self.width)], token, place_bit(*step), self.mine,
                self.received,
            )
        step = self.steps[2 * count - at] if at <= 2 * count else self.core
        self.received = exchanged(self.mine, *step)
        return self.mine

    def turns(self):
        return 2 * len(self.steps) + 2


def finish_kernel(
    mine_a, got_a, mine_b, got_b, mine_c, got_c, mine_d, got_d,
    grad_down, grad_up, grad_out, grad_z, grad_h, small, sems,
):
    block = mine_a.shape[1]
    width, hidden = grad_z.shape
    half = width // 2
    even = lax.axis_index("row") % 2 == 0

    def run(a_even, a_odd, b_even, b_odd, c_even, c_odd, d_even, d_odd):
        rows = mine_a.shape[0]
        copies = [
            (a_even, grad_down.at[pl.ds(0, rows), :]),
            (b_even.at[pl.ds(0, rows), :], grad_down.at[pl.ds(rows, rows), :]),
            (b_even.at[pl.ds(rows, hidden // 2), :], grad_out.at[pl.ds(0, hidden // 2), :]),
            (b_odd.at[pl.ds(rows, hidden // 2), :], grad_out.at[pl.ds(hidden // 2, hidden // 2), :]),
        ]
        for k in range(rows // block):
            at = pl.ds(k * block, block)
            copies.append((a_odd.at[at, :], grad_up.at[:, at]))
            copies.append((b_odd.at[at, :], grad_up.at[:, pl.ds(rows + k * block, block)]))
        for k, (one, two) in enumerate(((c_even, c_odd), (d_even, d_odd))):
            to = pl.ds(k * half, half)
            copies.append((one.at[:, pl.ds(0, hidden)], grad_z.at[to, :]))
            copies.append((two.at[:, pl.ds(0, hidden)], grad_h.at[to, :]))
        copies.append((d_even.at[pl.ds(0, small.shape[0]), pl.ds(hidden, 128)], small))
        started = [pltpu.make_async_copy(*pair, sems.at[i]) for i, pair in enumerate(copies)]
        for copy in started:
            copy.start()
        for copy in started:
            copy.wait()

    pairs = ((mine_a, got_a), (mine_b, got_b), (mine_c, got_c), (mine_d, got_d))

    @pl.when(even)
    def _():
        run(*[ref for pair in pairs for ref in pair])

    @pl.when(jnp.logical_not(even))
    def _():
        run(*[ref for pair in pairs for ref in pair[::-1]])


def per_device(
    tokens, first_len, gain_one, conv_weight, w_z, bias_z, w_h, w_out, gain_two, w_up, w_down, cotangent
):
    rows, group_len, width = tokens.shape
    hidden, ff = w_z.shape[1], w_up.shape[1]
    lag = conv_weight.shape[0] - 1
    count = rows * group_len
    devices = lax.axis_size("seq")
    gain_one, gain_two, bias_z = gain_one[None], gain_two[None], bias_z[None]
    rim = lax.ppermute(
        tokens[:, group_len - lag :].astype(F32), "seq", [(i, i + 1) for i in range(devices - 1)]
    )
    th, tw = (count, hidden), (count, width)
    x, up, conv_low, keep, drive, cand, gate, passing, subk, subs, totals = call(
        gates_kernel,
        [SMEM] + [VMEM] * 8,
        [(tw, BF16), (tw, BF16), (tw, BF16)] + [(th, F32)] * 5
        + [((SUB, hidden), F32)] * 2 + [((2, rows, hidden), F32)],
        [((count + lag * SUB, width), F32), ((lag, SUB, width), F32), ((8, 128), F32)],
        4 * count * width * hidden,
    )(first_len, tokens, cotangent, rim, gain_one, conv_weight, w_z, bias_z, w_h)
    carried, levels = carry_forward(totals)
    pairs_a = ((ff // 2, width), F32)
    pairs_b = ((ff // 2 + hidden // 2, width), F32)
    state, before, output, mine_a, other_a, mine_b, other_b, grad_middle, grad_gain_two, grad_state, subb, passed = call(
        mlp_kernel,
        [SMEM] + [VMEM] * 11,
        [(th, F32), ((SUB, hidden), F32), (tokens.shape, BF16), pairs_a, pairs_a, pairs_b, pairs_b,
         (tw, F32), ((1, width), F32), (th, F32), ((SUB, hidden), F32), ((rows, hidden), F32)],
        [(th, BF16), (tw, BF16), (tw, F32), (tw, F32), (tw, F32)],
        12 * count * width * ff,
    )(first_len, carried, subk, subs, keep, drive, x, up, w_out, gain_two, w_up, w_down)
    returned = carry_backward(passed, levels)
    sums = [Summed(mine_a, other_a, KINDS[0]), Summed(mine_b, other_b, KINDS[1])]
    token = grad_gain_two
    for turn in EARLY:
        token = sums[turn].advance(token)
    tile = 16
    pair = ((width // 2, hidden), F32)
    pair_small = ((width // 2, hidden + 128), F32)
    mine_c, other_c, mine_d, other_d, grad_tokens, sent, tail_normed, tail_middle = call(
        first_kernel,
        [SMEM] + [VMEM] * 19 + [pl.BlockSpec(memory_space=pl.ANY)],
        [pair, pair, pair_small, pair_small, (tokens.shape, BF16),
         ((rows, lag, width), F32)] + [((rows, tile, width), F32)] * 2,
        [((SUB, hidden), F32), (th, BF16), (th, BF16), ((count + lag * SUB, width), F32),
         ((lag, SUB, width), F32), ((count + lag * SUB, width), F32), ((1, hidden), F32), ((SUB, width), F32)],
        8 * count * width * hidden,
    )(first_len, returned, subk, subb, keep, grad_state, state, before, cand, gate, passing, conv_low,
      x, rim, gain_one, conv_weight, w_z, w_h, grad_middle, grad_gain_two, token)
    received = lax.ppermute(sent, "seq", [(i + 1, i) for i in range(devices - 1)])
    at_tail = pl.BlockSpec((rows, tile, width), lambda i: (0, group_len // tile - 1, 0))
    whole = lambda *shape: pl.BlockSpec(shape, lambda i: (0,) * len(shape))
    grad_tokens = pl.pallas_call(
        tail_kernel,
        grid=(1,),
        in_specs=[at_tail, whole(rows, tile, width), whole(rows, tile, width), whole(rows, lag, width),
                  whole(1, width), at_tail],
        out_specs=at_tail,
        out_shape=jax.ShapeDtypeStruct(tokens.shape, BF16),
        scratch_shapes=[pltpu.VMEM((tile, width), F32)],
        input_output_aliases={5: 0},
    )(tokens, tail_normed, tail_middle, received, gain_one, grad_tokens)
    sums += [Summed(mine_c, other_c, KINDS[2]), Summed(mine_d, other_d, KINDS[3])]
    token = tail_normed
    while any(one.at < one.turns() for one in sums):
        for one in sums:
            if one.at < one.turns():
                token = one.advance(token)
    anywhere = pl.BlockSpec(memory_space=pl.ANY)
    grad_down, grad_up, grad_out, grad_z, grad_h, small = pl.pallas_call(
        finish_kernel,
        in_specs=[anywhere] * 8,
        out_specs=(anywhere,) * 6,
        out_shape=shaped(
            ((ff, width), F32), ((width, ff), F32), ((hidden, width), F32), ((width, hidden), F32),
            ((width, hidden), F32), ((SUB * width // 128, 128), F32),
        ),
        scratch_shapes=[pltpu.SemaphoreType.DMA((24,))],
    )(*[array for one in sums for array in (one.mine, one.received)])
    small = small.reshape(width // 128, SUB, 128).swapaxes(0, 1).reshape(SUB, width)
    bias_at = 2 + lag
    gain_at = bias_at + hidden // width
    return (
        output,
        grad_tokens,
        small[0],
        small[1:bias_at],
        grad_z,
        small[bias_at:gain_at].reshape(hidden),
        grad_h,
        grad_out,
        small[gain_at],
        grad_up,
        grad_down,
    )


def solution(mesh):
    block, copied = P("row", "seq", None), P()
    return jax.shard_map(
        per_device,
        mesh=mesh,
        in_specs=(block, P("row")) + (copied,) * 9 + (block,),
        out_specs=(block, block) + (copied,) * 9,
        check_vma=False,
    )
```

```python
import functools

import jax
import jax.numpy as jnp
from jax import lax
from jax.experimental import pallas as pl
from jax.experimental.pallas import tpu as pltpu
from jax.sharding import PartitionSpec as P

F32, BF16 = jnp.float32, jnp.bfloat16
EPS = 1e-06
VMEM = pl.BlockSpec(memory_space=pltpu.VMEM)
SMEM = pl.BlockSpec(memory_space=pltpu.SMEM)
KINDS = "TSST"
CHUNKS = 4
EARLY = (0, 1, 0, 1)
SUB = 8


HBM = pl.BlockSpec(memory_space=pltpu.HBM)


class Staged:
    def __init__(self, sources, buffers, targets, results, sems, chunks):
        self.ins, self.pending, self.sems, self.next = {}, [], sems, 0
        self.targets, self.results = targets, results
        order = []
        for i, (source, buffer) in enumerate(zip(sources, buffers)):
            parts = chunks.get(i, 1)
            rows = source.shape[0] // parts
            self.ins[i] = []
            for c in range(parts):
                at = pl.ds(c * rows, rows)
                pair = (source, buffer) if parts == 1 else (source.at[at], buffer.at[at])
                self.ins[i].append(self.copy(*pair))
                order.append((c, self.ins[i][-1]))
        for _, copy in sorted(order, key=lambda pair: pair[0]):
            copy.start()

    def copy(self, source, target):
        self.next += 1
        return pltpu.make_async_copy(source, target, self.sems.at[self.next - 1])

    def need(self, *indices):
        for i in indices:
            for copy in self.ins[i]:
                copy.wait()

    def need_chunk(self, c, *indices):
        for i in indices:
            self.ins[i][c].wait()

    def done(self, *indices):
        for i in indices:
            copy = self.copy(self.results[i], self.targets[i])
            copy.start()
            self.pending.append(copy)

    def send(self, source, target):
        copy = self.copy(source, target)
        copy.start()
        self.pending.append(copy)

    def finish(self):
        for copy in self.pending:
            copy.wait()


def staged_call(kernel, scalars, ins, outs, extra_outs, scratch, flops, copies, chunks=None, reverse=False):
    n_s, n_i, n_o, n_e = len(scalars), len(ins), len(outs), len(extra_outs)

    def body(*refs):
        cut = [0]
        for size in (n_s, n_i, n_o, n_e, n_i, n_o, len(scratch)):
            cut.append(cut[-1] + size)
        scalar, source, target, extra, buffer, result, own = [refs[a:b] for a, b in zip(cut, cut[1:])]
        stage = Staged(source, buffer, target, result, refs[-1], chunks or {})
        kernel(stage, scalar, buffer, result, extra, own)
        stage.finish()

    results = pl.pallas_call(
        body,
        in_specs=[SMEM] * n_s + [HBM] * n_i,
        out_specs=(HBM,) * (n_o + n_e),
        out_shape=shaped(*outs, *extra_outs),
        scratch_shapes=[pltpu.VMEM(a.shape, a.dtype) for a in ins]
        + [pltpu.VMEM(shape, kind) for shape, kind in outs]
        + [pltpu.VMEM(shape, kind) for shape, kind in scratch]
        + [pltpu.SemaphoreType.DMA((copies,))],
        compiler_params=pltpu.CompilerParams(vmem_limit_bytes=56 << 20),
        cost_estimate=pl.CostEstimate(flops=flops, bytes_accessed=8 << 20, transcendentals=0),
    )(*scalars, *ins)
    return results


def dot(left, right):
    return jnp.dot(left, right, preferred_element_type=F32)


def dot_lt(left, right):
    return lax.dot_general(left, right, (((0,), (0,)), ((), ())), preferred_element_type=F32)


def dot_rt(left, right):
    return lax.dot_general(left, right, (((1,), (1,)), ((), ())), preferred_element_type=F32)


def segment_order(tokens):
    steps = tokens // SUB
    to = lax.broadcasted_iota(jnp.int32, (tokens, tokens), 0)
    source = lax.broadcasted_iota(jnp.int32, (tokens, tokens), 1)
    return jnp.where(source == (to % SUB) * steps + to // SUB, 1.0, 0.0).astype(BF16)


def opened(first_len, seq_start, shape):
    sub = lax.broadcasted_iota(jnp.int32, shape, 0)
    rows = first_len.shape[0]
    result = jnp.ones(shape, F32)
    for r in range(rows):
        factor = jnp.where(first_len[r] == seq_start, 0.0, 1.0)
        result = jnp.where(sub == r * (SUB // rows), factor, result)
    return result


def at_row_start(shape, rows):
    return lax.broadcasted_iota(jnp.int32, shape, 0) % (SUB // rows) == 0


def at_row_end(shape, rows):
    parts = SUB // rows
    return lax.broadcasted_iota(jnp.int32, shape, 0) % parts == parts - 1


def rms(values):
    return lax.rsqrt(jnp.mean(values * values, axis=-1, keepdims=True) + EPS)


def fill_extended(ext, rim, first_len, seq_start, xhat_rim):
    lag, rows = rim.shape[1], rim.shape[0]
    width = ext.shape[-1]
    mask = opened(first_len, seq_start, (SUB, width))
    start = at_row_start((SUB, width), rows)
    total = ext.shape[0]
    for k in range(lag):
        near = pltpu.roll(ext[total - lag * SUB + k * SUB : total - lag * SUB + (k + 1) * SUB, :], 1, 0)
        ext[k * SUB : (k + 1) * SUB, :] = jnp.where(start, xhat_rim[k] * mask, near)


def rim_tiles(rim, spread):
    rows, lag, _ = rim.shape
    parts = SUB // rows
    spread[...] = jnp.zeros_like(spread)
    for k in range(lag):
        for r in range(rows):
            spread[k, r * parts : r * parts + 1, :] = rim[r, k : k + 1, :]
    return [spread[k] for k in range(lag)]


def gates_kernel(stage, scalars, ins, outs, extra, scratch):
    (first_len,) = scalars
    tokens, rim, gain_one, conv_weight, w_z, bias_z, w_h, cotangent = ins
    x_out, conv_out, keep_out, drive_out, cand_out, gate_out, pass_out, subk, subs, totals, up_out = outs
    ext, spread = scratch
    rows, group_len, width = tokens.shape
    count, lag = rows * group_len, rim.shape[1]
    hidden = w_z.shape[1]
    seq_start = lax.axis_index("seq") * group_len
    order = segment_order(count)
    stage.need(0)
    x = dot(order, tokens[...].reshape(count, width))
    x_out[...] = x.astype(BF16)
    stage.done(0)
    stage.need(1, 2, 3)
    normed = x * rms(x) * gain_one[...]
    ext[lag * SUB :, :] = normed
    rim_x = rim_tiles(rim, spread)
    fill_extended(ext, rim, first_len, seq_start, [v * rms(v) * gain_one[...] for v in rim_x])
    mixed = jnp.zeros((count, width), F32)
    for j in range(lag + 1):
        begin = (lag - j) * SUB
        mixed = mixed + conv_weight[j : j + 1, :] * ext[begin : begin + count, :]
    conv_out[...] = mixed.astype(BF16)
    stage.done(1)
    stage.need(4, 5, 6)
    mask = opened(first_len, seq_start, (SUB, hidden))
    block = 256
    for b in range(hidden // block):
        cols = slice(b * block, (b + 1) * block)
        g = dot(conv_out[...], w_z[:, cols]) + bias_z[:, cols]
        c = dot(conv_out[...], w_h[:, cols])
        small = jnp.exp(-jnp.abs(g))
        large = 1.0 / (1.0 + small)
        small = small * large
        zeta = jnp.where(g >= 0, large, small)
        sig = 1.0 / (1.0 + jnp.exp(-c))
        cand = jnp.where(c >= 0, c + 0.5, sig)
        keep_out[:, cols] = jnp.where(g >= 0, small, large)
        keep_out[0:SUB, cols] = keep_out[0:SUB, cols] * mask[:, cols]
        drive_out[:, cols] = zeta * cand
        cand_out[:, cols] = cand
        gate_out[:, cols] = (small * large).astype(BF16)
        pass_out[:, cols] = (zeta * jnp.where(c >= 0, 1.0, sig * (1.0 - sig))).astype(BF16)
        for i in (2, 3, 4, 5, 6):
            stage.send(outs[i].at[:, pl.ds(b * block, block)], stage.targets[i].at[:, pl.ds(b * block, block)])

    def step(i, carry):
        total, state = carry
        at = pl.ds(pl.multiple_of(i * SUB, SUB), SUB)
        keep = keep_out[at, :]
        return total * keep, keep * state + drive_out[at, :]

    total, state = lax.fori_loop(
        0, count // SUB, step, (jnp.ones((SUB, hidden), F32), jnp.zeros((SUB, hidden), F32)), unroll=8
    )
    subk[...] = total
    subs[...] = state
    parts = SUB // rows
    for r in range(rows):
        at = slice(r * parts, r * parts + 1)
        k, s = subk[at, :], subs[at, :]
        for h in range(1, parts):
            at = slice(r * parts + h, r * parts + h + 1)
            s = subs[at, :] + subk[at, :] * s
            k = k * subk[at, :]
        totals[0, r : r + 1, :] = k
        totals[1, r : r + 1, :] = s
    stage.done(7, 8, 9)
    stage.need(7)
    up_out[...] = dot(order, cotangent[...].reshape(count, width)).astype(BF16)
    stage.done(10)


def give_pair(stage, even, pairs):
    found = []
    for one, two, mine, other in pairs:
        found.append((stage.copy(one, mine), stage.copy(two, other), one, two, mine, other, stage.next))

    @pl.when(even)
    def _():
        for first, second, *_ in found:
            first.start()
            second.start()

    @pl.when(jnp.logical_not(even))
    def _():
        for _, _, one, two, mine, other, at in found:
            pltpu.make_async_copy(two, mine, stage.sems.at[at - 2]).start()
            pltpu.make_async_copy(one, other, stage.sems.at[at - 1]).start()

    for first, second, *_ in found:
        stage.pending += [first, second]


def mlp_kernel(stage, scalars, ins, outs, extra, scratch):
    (first_len,) = scalars
    carried, subk, subs, keep, drive, cand, gate, x, w_out, gain_two, w_up, w_down, up = ins
    blend, output, grad_middle_out, grad_gain_two, grad_state, subb, totals = outs
    mine_a, other_a, mine_b, other_b = extra
    before, low, second_low, tail, second_grad, middle_ref, for_even, for_odd, out_even, out_odd = scratch
    count, width = x.shape
    hidden, ff = keep.shape[1], w_up.shape[1]
    rows = carried.shape[0]
    group_len = count // rows
    parts = SUB // rows
    pairs = count // SUB // 2
    seq_start = lax.axis_index("seq") * group_len
    even = lax.axis_index("row") % 2 == 0
    stage.need(0, 1, 2)
    for r in range(rows):
        s = carried[r : r + 1, :]
        before[r * parts : r * parts + 1, :] = s
        for h in range(1, parts):
            at = slice(r * parts + h - 1, r * parts + h)
            s = subs[at, :] + subk[at, :] * s
            before[r * parts + h : r * parts + h + 1, :] = s

    def two(i, state):
        at = pl.ds(pl.multiple_of(i * 2 * SUB, 2 * SUB), 2 * SUB)
        k, d, c, g = keep[at, :], drive[at, :], cand[at, :], gate[at, :].astype(F32)
        first = k[:SUB] * state + d[:SUB]
        second = k[SUB:] * first + d[SUB:]
        low[at, :] = jnp.concatenate([first, second], axis=0).astype(BF16)
        earlier = jnp.concatenate([state, first], axis=0)
        blend[at, :] = ((c - earlier) * g).astype(BF16)
        return second

    state = before[...] * opened(first_len, seq_start, (SUB, hidden))
    for c in range(CHUNKS):
        stage.need_chunk(c, 3, 4, 5, 6)
        state = lax.fori_loop(c * pairs // CHUNKS, (c + 1) * pairs // CHUNKS, two, state, unroll=2)
    stage.done(0)
    stage.need(7, 8, 9)
    middle = x[...].astype(F32) + dot(low[...], w_out[...])
    middle_ref[...] = middle
    second_low[...] = (middle * rms(middle) * gain_two[...]).astype(BF16)
    tail[...] = jnp.zeros_like(tail)
    second_grad[...] = jnp.zeros_like(second_grad)
    stage.need(10, 11, 12)
    block = width
    half = ff // block // 2

    def part(b, carry):
        at = pl.ds(pl.multiple_of(b * block, block), block)
        pre = dot(second_low[...], w_up[:, at])
        back = dot_rt(up[...], w_down[at, :])
        scaled = pre * 0.7071067811865476
        phi = 0.5 + 0.5 * lax.erf(scaled)
        active = (pre * phi).astype(BF16)
        slope = phi + pre * (0.3989422804014327 * jnp.exp(-scaled * scaled))
        up_low = (slope * back).astype(BF16)
        for_even[at, :] = dot_lt(active, up[...])
        for_odd[at, :] = dot_lt(second_low[...], up_low)
        tail[...] += dot(active, w_down[at, :])
        second_grad[...] += dot_rt(up_low, w_up[:, at])
        return carry

    for k, (mine, other) in enumerate(((mine_a, other_a), (mine_b, other_b))):
        lax.fori_loop(k * half, (k + 1) * half, part, 0)
        at, to = pl.ds(k * half * block, half * block), pl.ds(0, half * block)
        give_pair(stage, even, [(for_even.at[at], for_odd.at[at], mine.at[to], other.at[to])])

    middle = middle_ref[...]
    scale = rms(middle)
    unit = middle * scale
    grad = second_grad[...]
    grad_gain_two[...] = jnp.sum(grad * unit, axis=0, keepdims=True)
    grad = grad * gain_two[...]
    grad_middle = up[...].astype(F32) + scale * (grad - unit * jnp.mean(grad * unit, axis=-1, keepdims=True))
    grad_middle_out[...] = grad_middle
    stage.done(2, 3)
    middle_low = grad_middle.astype(BF16)
    grad_state[...] = dot_rt(middle_low, w_out[...])
    stage.done(4)

    def back_step(i, passed):
        at = pl.ds(pl.multiple_of((2 * pairs - 1 - i) * SUB, SUB), SUB)
        return keep[at, :] * (grad_state[at, :] + passed)

    subb[...] = lax.fori_loop(0, 2 * pairs, back_step, jnp.zeros((SUB, hidden), F32), unroll=8)
    for r in range(rows):
        end = r * parts + parts - 1
        b = subb[end : end + 1, :]
        for h in range(parts - 2, -1, -1):
            at = slice(r * parts + h, r * parts + h + 1)
            b = subb[at, :] + subk[at, :] * b
        totals[r : r + 1, :] = b
    stage.done(5, 6)
    half_h = hidden // 2
    out_even[...] = dot_lt(low[:, :half_h], middle_low)
    out_odd[...] = dot_lt(low[:, half_h:], middle_low)
    to = pl.ds(half * block, half_h)
    give_pair(stage, even, [(out_even, out_odd, mine_b.at[to], other_b.at[to])])
    result = (middle_ref[...] + tail[...]).astype(BF16)
    output[...] = dot_lt(segment_order(count), result).astype(BF16).reshape(output.shape)
    stage.done(1)


def first_kernel(stage, scalars, ins, outs, extra, scratch):
    (first_len,) = scalars
    (returned, subk, subb, keep, grad_state, blend, passing, conv_low, w_z, w_h, x_ref, rim, gain_one, conv_weight,
     grad_middle, grad_gain_two) = ins
    grad_tokens, sent, tail_normed, tail_middle = outs
    mine_a, other_a, mine_b, other_b = extra
    incoming, gate_low, cand_low, ext, spread, grad_ext, bias_sum, small, for_even, for_odd, rest = scratch
    count, width = x_ref.shape
    hidden = keep.shape[1]
    rows, lag = rim.shape[0], rim.shape[1]
    parts = SUB // rows
    pairs = count // SUB // 2
    seq_start = lax.axis_index("seq") * (count // rows)
    even = lax.axis_index("row") % 2 == 0
    stage.need(0, 1, 2)
    for r in range(rows):
        b = returned[r : r + 1, :]
        incoming[r * parts + parts - 1 : (r + 1) * parts, :] = b
        for h in range(parts - 2, -1, -1):
            at = slice(r * parts + h + 1, r * parts + h + 2)
            b = subb[at, :] + subk[at, :] * b
            incoming[r * parts + h : r * parts + h + 1, :] = b

    def two(i, carry):
        passed, bias = carry
        at = pl.ds(pl.multiple_of((pairs - 1 - i) * 2 * SUB, 2 * SUB), 2 * SUB)
        k, g = keep[at, :], grad_state[at, :]
        late = g[SUB:] + passed
        early = g[:SUB] + k[SUB:] * late
        adjoint = jnp.concatenate([early, late], axis=0)
        grad_g = adjoint * blend[at, :].astype(F32)
        gate_low[at, :] = grad_g.astype(BF16)
        cand_low[at, :] = (adjoint * passing[at, :].astype(F32)).astype(BF16)
        return k[:SUB] * early, bias + grad_g[:SUB] + grad_g[SUB:]

    carry = (incoming[...], jnp.zeros((SUB, hidden), F32))
    for c in range(CHUNKS):
        stage.need_chunk(CHUNKS - 1 - c, 3, 4, 5, 6)
        carry = lax.fori_loop(c * pairs // CHUNKS, (c + 1) * pairs // CHUNKS, two, carry, unroll=2)
    bias = carry[1]
    bias_sum[...] = jnp.sum(bias, axis=0, keepdims=True)
    stage.need(7)
    half = width // 2
    for_even[...] = dot_lt(conv_low[...], gate_low[...])
    for_odd[...] = dot_lt(conv_low[...], cand_low[...])
    cols = pl.ds(0, hidden)
    low_rows, high_rows = pl.ds(0, half), pl.ds(half, half)
    give_pair(stage, even, [
        (for_even.at[low_rows], for_odd.at[low_rows], mine_a, other_a),
        (for_even.at[high_rows], for_odd.at[high_rows], mine_b.at[:, cols], other_b.at[:, cols]),
    ])
    stage.need(8, 9, 10, 11, 12, 13, 14, 15)
    grad_mixed = dot_rt(gate_low[...], w_z[...]) + dot_rt(cand_low[...], w_h[...])

    x = x_ref[...].astype(F32)
    scale = rms(x)
    unit = x * scale
    gain = gain_one[...]
    ext[lag * SUB :, :] = unit * gain
    rim_x = rim_tiles(rim, spread)
    rim_unit = [v * rms(v) for v in rim_x]
    fill_extended(ext, rim, first_len, seq_start, [v * gain for v in rim_unit])
    small[0:1, :] = jnp.zeros((1, width), F32)
    for j in range(lag + 1):
        begin = (lag - j) * SUB
        small[1 + j : 2 + j, :] = jnp.sum(grad_mixed * ext[begin : begin + count, :], axis=0, keepdims=True)
    for j in range(hidden // width):
        at = 2 + lag + j
        small[at : at + 1, :] = bias_sum[:, j * width : (j + 1) * width]
    last = 2 + lag + hidden // width
    small[last : last + 1, :] = grad_gain_two[...]
    grad_ext[...] = jnp.zeros_like(grad_ext)
    for j in range(lag + 1):
        begin = (lag - j) * SUB
        grad_ext[begin : begin + count, :] += conv_weight[j : j + 1, :] * grad_mixed
    mask = opened(first_len, seq_start, (SUB, width))
    start = at_row_start((SUB, width), rows)
    end = at_row_end((SUB, width), rows)
    grad_gain = jnp.zeros((SUB, width), F32)
    for k in range(lag):
        head = grad_ext[k * SUB : (k + 1) * SUB, :]
        tail_at = pl.ds(count + k * SUB, SUB)
        near = pltpu.roll(head, SUB - 1, 0)
        grad_ext[tail_at, :] = grad_ext[tail_at, :] + jnp.where(end, 0.0, near)
        to_rim = jnp.where(start, head * mask, 0.0)
        grad_gain = grad_gain + to_rim * rim_unit[k]
        spread[k] = to_rim
        for r in range(rows):
            sent[r, k : k + 1, :] = spread[k, r * parts : r * parts + 1, :]
    grad_normed = grad_ext[lag * SUB :, :]
    small[0:1, :] = jnp.sum(grad_normed * unit, axis=0, keepdims=True) + jnp.sum(
        grad_gain, axis=0, keepdims=True
    )
    rest[...] = jnp.zeros_like(rest)
    for j in range(width // 128):
        rest[j * SUB : (j + 1) * SUB, :] = small[:, j * 128 : (j + 1) * 128]
    past = pl.ds(hidden, 128)
    give_pair(stage, even, [(rest.at[low_rows], rest.at[high_rows], mine_b.at[:, past], other_b.at[:, past])])
    for k in range(lag):
        at = count - lag * SUB + k * SUB
        for r in range(rows):
            row = at + r * parts + parts - 1
            to = tail_normed.shape[1] - lag + k
            tail_normed[r, to : to + 1, :] = grad_ext[lag * SUB + row : lag * SUB + row + 1, :]
            tail_middle[r, to : to + 1, :] = grad_middle[row : row + 1, :]
    grad = grad_normed * gain
    grad_x = grad_middle[...] + scale * (grad - unit * jnp.mean(grad * unit, axis=-1, keepdims=True))
    stage.done(1, 2, 3)
    order = segment_order(count)
    grad_tokens[...] = dot_lt(order, grad_x.astype(BF16)).astype(BF16).reshape(grad_tokens.shape)
    stage.done(0)


def tail_kernel(tokens, tail_normed, tail_middle, received, gain_one, _, grad_tokens, spread):
    rows, tile, width = tokens.shape
    lag = received.shape[1]
    for r in range(rows):
        spread[tile - lag :, :] = tail_normed[r, tile - lag :, :] + received[r]
        x = tokens[r].astype(F32)
        scale = rms(x)
        unit = x * scale
        grad = spread[...] * gain_one[...]
        fixed = tail_middle[r] + scale * (grad - unit * jnp.mean(grad * unit, axis=-1, keepdims=True))
        changed = lax.broadcasted_iota(jnp.int32, (tile, width), 0) >= tile - lag
        grad_tokens[r] = jnp.where(changed, fixed, _[r].astype(F32)).astype(BF16)


def shaped(*shapes):
    return tuple(jax.ShapeDtypeStruct(shape, kind) for shape, kind in shapes)


def swapped(array, axis, bit):
    return lax.ppermute(array, axis, [(i, i ^ bit) for i in range(lax.axis_size(axis))])


def bits_of(axis):
    bit, result = 1, []
    while bit < lax.axis_size(axis):
        result.append(bit)
        bit *= 2
    return result


def upper(axis, bit):
    return (lax.axis_index(axis) // bit) % 2 == 1


def carry_forward(totals):
    keep, state = totals[0], totals[1]
    before_k, before_s = jnp.ones_like(keep), jnp.zeros_like(state)
    levels = []
    for bit in bits_of("seq"):
        other = swapped(jnp.stack([keep, state]), "seq", bit)
        other_k, other_s = other[0], other[1]
        late = upper("seq", bit)
        levels.append((keep, other_k))
        before_s = jnp.where(late, before_s + before_k * other_s, before_s)
        before_k = jnp.where(late, before_k * other_k, before_k)
        state = jnp.where(late, state + keep * other_s, other_s + other_k * state)
        keep = keep * other_k
    return before_s, levels


def carry_backward(passed, levels):
    after_b, after_k = jnp.zeros_like(passed), jnp.ones_like(passed)
    for bit, (keep, other_k) in zip(bits_of("seq"), levels):
        other_b = swapped(passed, "seq", bit)
        late = upper("seq", bit)
        after_b = jnp.where(late, after_b, after_b + after_k * other_b)
        after_k = jnp.where(late, after_k, after_k * other_k)
        passed = jnp.where(late, other_b + other_k * passed, passed + keep * other_b)
    return after_b


BOTH = ("row", "seq")


def axis_steps(kind):
    row = [("row", bit) for bit in bits_of("row")[1:]]
    seq = [("seq", bit) for bit in bits_of("seq")]
    near, far = seq[:1], seq[1:]
    even = {"P": near + row + far, "S": near + far + row, "T": far + near + row}[kind]
    return list(zip(even, row + near + far))


def exchanged(array, even, odd):
    rows, devices = lax.axis_size("row"), lax.axis_size("seq")
    pairs = []
    for r in range(rows):
        for s in range(devices):
            axis, bit = odd if r & 1 else even
            to = ((r ^ bit) * devices + s) if axis == "row" else (r * devices + (s ^ bit))
            pairs.append((r * devices + s, to))
    return lax.ppermute(array, BOTH, pairs)


def place_bit(even, odd):
    one, two = [lax.axis_index(axis) // bit % 2 for axis, bit in (even, odd)]
    return jnp.where(lax.axis_index("row") % 2 == 0, one, two).astype(jnp.int32).reshape(1)


def by_rows(total, body):
    chunk = next((c for c in (64, 32, 16, 8) if total % c == 0), total)
    if chunk == total:
        body(0, chunk)
        return

    def turn(i, carry):
        body(pl.multiple_of(i * chunk, chunk), chunk)
        return carry

    lax.fori_loop(0, total // chunk, turn, 0)


def aligned(at, half):
    return pl.multiple_of(at, SUB) if half % SUB == 0 else at


def split_kernel(_, bit, mine, received, send, keep):
    half = send.shape[0]
    if half % SUB:
        first = mine[:half, :] + received[:half, :]
        second = mine[half:, :] + received[half:, :]
        lower = jnp.broadcast_to(bit[0] == 0, first.shape)
        send[...] = jnp.where(lower, second, first)
        keep[...] = jnp.where(lower, first, second)
        return

    def body(i, chunk):
        to = pl.ds(i, chunk)
        for out, begin in ((send, (1 - bit[0]) * half), (keep, bit[0] * half)):
            at = pl.ds(pl.multiple_of(i + begin, SUB), chunk)
            out[to, :] = mine[at, :] + received[at, :]

    by_rows(half, body)


def add_kernel(_, mine, received, out):
    def body(i, chunk):
        at = pl.ds(i, chunk)
        out[at, :] = mine[at, :] + received[at, :]

    by_rows(mine.shape[0], body)


def join_kernel(_, bit, mine, received, out):
    half = mine.shape[0]
    if half % SUB:
        lower = jnp.broadcast_to(bit[0] == 0, mine.shape)
        out[:half, :] = jnp.where(lower, mine[...], received[...])
        out[half:, :] = jnp.where(lower, received[...], mine[...])
        return

    def body(i, chunk):
        at = pl.ds(i, chunk)
        for source, begin in ((mine, bit[0] * half), (received, (1 - bit[0]) * half)):
            out[pl.ds(pl.multiple_of(i + begin, SUB), chunk), :] = source[at, :]

    by_rows(half, body)


def piece_call(kernel, specs, outs, *operands):
    return pl.pallas_call(
        kernel,
        in_specs=[pl.BlockSpec(memory_space=pl.ANY)] + specs,
        out_specs=(VMEM,) * len(outs),
        out_shape=shaped(*[(shape, F32) for shape in outs]),
        compiler_params=pltpu.CompilerParams(vmem_limit_bytes=16 << 20),
        cost_estimate=pl.CostEstimate(flops=1, bytes_accessed=1, transcendentals=0),
    )(*operands)


class Summed:
    def __init__(self, mine, other, kind):
        self.steps = axis_steps(kind)
        self.core = (("row", 1),) * 2
        self.mine, self.other, self.at = mine, other, 0
        self.width = mine.shape[1]

    def advance(self, token):
        count, at = len(self.steps), self.at
        self.at += 1
        if at == 0:
            self.received = exchanged(self.other, *self.core)
            return token
        rows = self.mine.shape[0]
        if at <= count:
            step = self.steps[at - 1]
            half = (rows // 2, self.width)
            send, self.mine = piece_call(
                split_kernel, [SMEM, VMEM, VMEM], [half, half], token, place_bit(*step), self.mine, self.received
            )
            self.received = exchanged(send, *step)
            return self.mine
        if at == count + 1:
            (self.mine,) = piece_call(add_kernel, [VMEM] * 2, [self.mine.shape], token, self.mine, self.received)
        else:
            step = self.steps[2 * count + 1 - at]
            (self.mine,) = piece_call(
                join_kernel, [SMEM, VMEM, VMEM], [(2 * rows, self.width)], token, place_bit(*step), self.mine,
                self.received,
            )
        step = self.steps[2 * count - at] if at <= 2 * count else self.core
        self.received = exchanged(self.mine, *step)
        return self.mine

    def turns(self):
        return 2 * len(self.steps) + 2


def moved(stage_refs, routes, sems):
    into = []
    for i, (source, buffer, target) in enumerate(routes):
        copy = pltpu.make_async_copy(source, buffer, sems.at[i])
        copy.start()
        into.append(copy)
    out = []
    for i, (source, buffer, target) in enumerate(routes):
        into[i].wait()
        copy = pltpu.make_async_copy(buffer, target, sems.at[len(routes) + i])
        copy.start()
        out.append(copy)
    for copy in out:
        copy.wait()


def finish_mlp(_, mine_a, got_a, mine_b, got_b, grad_down, grad_up, grad_out, buffer_a, buffer_b, sems):
    rows, width = mine_a.shape
    half_h = grad_out.shape[0] // 2
    even = lax.axis_index("row") % 2 == 0

    def run(a, b):
        routes, room = [], {0: 0, 1: 0}
        for k, (pair, begin) in enumerate(((a, 0), (b, rows))):
            for j in range(rows // width):
                at, to = pl.ds(j * width, width), pl.ds(begin + j * width, width)
                buffers = buffer_a if k == 0 else buffer_b
                routes.append((pair[0].at[at], buffers.at[0].at[at], grad_down.at[to]))
                routes.append((pair[1].at[at], buffers.at[1].at[at], grad_up.at[:, to]))
        for k in range(2):
            at = pl.ds(rows, half_h)
            routes.append((b[k].at[at], buffer_b.at[k].at[at], grad_out.at[pl.ds(k * half_h, half_h)]))
        moved(None, routes, sems)

    @pl.when(even)
    def _():
        run((mine_a, got_a), (mine_b, got_b))

    @pl.when(jnp.logical_not(even))
    def _():
        run((got_a, mine_a), (got_b, mine_b))


def finish_gates(_, mine_c, got_c, mine_d, got_d, grad_z, grad_h, small, buffer_c, buffer_d, sems):
    half, hidden = grad_z.shape[0] // 2, grad_z.shape[1]
    even = lax.axis_index("row") % 2 == 0

    def run(c, d):
        cols, low, high = pl.ds(0, hidden), pl.ds(0, half), pl.ds(half, half)
        routes = []
        for k, target in enumerate((grad_z, grad_h)):
            routes.append((c[k], buffer_c.at[k], target.at[low]))
            routes.append((d[k].at[:, cols], buffer_d.at[k].at[:, cols], target.at[high]))
        few, past = pl.ds(0, small.shape[0]), pl.ds(hidden, 128)
        routes.append((d[0].at[few, past], buffer_d.at[0].at[few, past], small))
        moved(None, routes, sems)

    @pl.when(even)
    def _():
        run((mine_c, got_c), (mine_d, got_d))

    @pl.when(jnp.logical_not(even))
    def _():
        run((got_c, mine_c), (got_d, mine_d))


def finish_call(kernel, token, sums, outs, copies):
    arrays = [array for one in sums for array in (one.mine, one.received)]
    return pl.pallas_call(
        kernel,
        in_specs=[pl.BlockSpec(memory_space=pl.ANY)] + [HBM] * len(arrays),
        out_specs=(HBM,) * len(outs),
        out_shape=shaped(*outs),
        scratch_shapes=[pltpu.VMEM((2,) + one.mine.shape, F32) for one in sums]
        + [pltpu.SemaphoreType.DMA((2 * copies,))],
        compiler_params=pltpu.CompilerParams(vmem_limit_bytes=32 << 20),
        cost_estimate=pl.CostEstimate(flops=1, bytes_accessed=1, transcendentals=0),
    )(token, *arrays)


def per_device(
    tokens, first_len, gain_one, conv_weight, w_z, bias_z, w_h, w_out, gain_two, w_up, w_down, cotangent
):
    rows, group_len, width = tokens.shape
    hidden, ff = w_z.shape[1], w_up.shape[1]
    lag = conv_weight.shape[0] - 1
    count = rows * group_len
    devices = lax.axis_size("seq")
    gain_one, gain_two, bias_z = gain_one[None], gain_two[None], bias_z[None]
    rim = lax.ppermute(
        tokens[:, group_len - lag :].astype(F32), "seq", [(i, i + 1) for i in range(devices - 1)]
    )
    th, tw = (count, hidden), (count, width)
    chunks = {3: CHUNKS, 4: CHUNKS, 5: CHUNKS, 6: CHUNKS}
    x, conv_low, keep, drive, cand, gate, passing, subk, subs, totals, up = staged_call(
        gates_kernel,
        [first_len],
        [tokens, rim, gain_one, conv_weight, w_z, bias_z, w_h, cotangent],
        [(tw, BF16), (tw, BF16), (th, F32), (th, F32), (th, F32), (th, BF16), (th, BF16),
         ((SUB, hidden), F32), ((SUB, hidden), F32), ((2, rows, hidden), F32), (tw, BF16)],
        [],
        [((count + lag * SUB, width), F32), ((lag, SUB, width), F32)],
        4 * count * width * hidden,
        64,
    )
    carried, levels = carry_forward(totals)
    pairs_a = ((ff // 2, width), F32)
    pairs_b = ((ff // 2 + hidden // 2, width), F32)
    (blend, output, grad_middle, grad_gain_two, grad_state, subb, passed,
     mine_a, other_a, mine_b, other_b) = staged_call(
        mlp_kernel,
        [first_len],
        [carried, subk, subs, keep, drive, cand, gate, x, w_out, gain_two, w_up, w_down, up],
        [(th, BF16), (tokens.shape, BF16), (tw, F32), ((1, width), F32), (th, F32), ((SUB, hidden), F32),
         ((rows, hidden), F32)],
        [pairs_a, pairs_a, pairs_b, pairs_b],
        [((SUB, hidden), F32), (th, BF16), (tw, BF16), (tw, F32), (tw, F32), (tw, F32),
         ((ff, width), F32), ((ff, width), F32), ((hidden // 2, width), F32), ((hidden // 2, width), F32)],
        12 * count * width * ff,
        64,
        chunks,
    )
    returned = carry_backward(passed, levels)
    sums = [Summed(mine_a, other_a, KINDS[0]), Summed(mine_b, other_b, KINDS[1])]
    token = returned
    for turn in EARLY:
        token = sums[turn].advance(token)
    tile = 16
    pair = ((width // 2, hidden), F32)
    pair_small = ((width // 2, hidden + 128), F32)
    grad_tokens, sent, tail_normed, tail_middle, mine_c, other_c, mine_d, other_d = staged_call(
        first_kernel,
        [first_len],
        [returned, subk, subb, keep, grad_state, blend, passing, conv_low, w_z, w_h, x, rim, gain_one,
         conv_weight, grad_middle, grad_gain_two],
        [(tokens.shape, BF16), ((rows, lag, width), F32)] + [((rows, tile, width), F32)] * 2,
        [pair, pair, pair_small, pair_small],
        [((SUB, hidden), F32), (th, BF16), (th, BF16), ((count + lag * SUB, width), F32),
         ((lag, SUB, width), F32), ((count + lag * SUB, width), F32), ((1, hidden), F32), ((SUB, width), F32),
         ((width, hidden), F32), ((width, hidden), F32), ((width, 128), F32)],
        8 * count * width * hidden,
        64,
        chunks,
    )
    received = lax.ppermute(sent, "seq", [(i + 1, i) for i in range(devices - 1)])
    at_tail = pl.BlockSpec((rows, tile, width), lambda i: (0, group_len // tile - 1, 0))
    whole = lambda *shape: pl.BlockSpec(shape, lambda i: (0,) * len(shape))
    grad_tokens = pl.pallas_call(
        tail_kernel,
        grid=(1,),
        in_specs=[at_tail, whole(rows, tile, width), whole(rows, tile, width), whole(rows, lag, width),
                  whole(1, width), at_tail],
        out_specs=at_tail,
        out_shape=jax.ShapeDtypeStruct(tokens.shape, BF16),
        scratch_shapes=[pltpu.VMEM((tile, width), F32)],
        input_output_aliases={5: 0},
    )(tokens, tail_normed, tail_middle, received, gain_one, grad_tokens)
    sums += [Summed(mine_c, other_c, KINDS[2]), Summed(mine_d, other_d, KINDS[3])]
    token = tail_normed
    while any(one.at < one.turns() for one in sums):
        for one in sums:
            if one.at < one.turns():
                token = one.advance(token)
    grad_down, grad_up, grad_out = finish_call(
        finish_mlp, token, sums[:2], [((ff, width), F32), ((width, ff), F32), ((hidden, width), F32)],
        2 * (ff // width) + 2,
    )
    grad_z, grad_h, small = finish_call(
        finish_gates, token, sums[2:],
        [((width, hidden), F32), ((width, hidden), F32), ((SUB * width // 128, 128), F32)], 5,
    )
    small = small.reshape(width // 128, SUB, 128).swapaxes(0, 1).reshape(SUB, width)
    bias_at = 2 + lag
    gain_at = bias_at + hidden // width
    return (
        output,
        grad_tokens,
        small[0],
        small[1:bias_at],
        grad_z,
        small[bias_at:gain_at].reshape(hidden),
        grad_h,
        grad_out,
        small[gain_at],
        grad_up,
        grad_down,
    )


def solution(mesh):
    block, copied = P("row", "seq", None), P()
    return jax.shard_map(
        per_device,
        mesh=mesh,
        in_specs=(block, P("row")) + (copied,) * 9 + (block,),
        out_specs=(block, block) + (copied,) * 9,
        check_vma=False,
    )
```

```python
import functools

import jax
import jax.numpy as jnp
from jax import lax
from jax.experimental import pallas as pl
from jax.experimental.pallas import tpu as pltpu
from jax.sharding import PartitionSpec as P

F32, BF16 = jnp.float32, jnp.bfloat16
EPS = 1e-06
VMEM = pl.BlockSpec(memory_space=pltpu.VMEM)
SMEM = pl.BlockSpec(memory_space=pltpu.SMEM)
ORDERS = ("xyab", "abyx", "ayxb", "xbay")
CHUNKS = 4
HOLD = 3
SUB = 8


HBM = pl.BlockSpec(memory_space=pltpu.HBM)
ANY = pl.BlockSpec(memory_space=pl.ANY)


class Staged:
    def __init__(self, sources, buffers, targets, results, sems, chunks):
        self.ins, self.pending, self.sems, self.next = {}, [], sems, 0
        self.targets, self.results = targets, results
        order = []
        for i, (source, buffer) in enumerate(zip(sources, buffers)):
            parts = chunks.get(i, 1)
            rows = source.shape[0] // parts
            self.ins[i] = []
            for c in range(parts):
                at = pl.ds(c * rows, rows)
                pair = (source, buffer) if parts == 1 else (source.at[at], buffer.at[at])
                self.ins[i].append(self.copy(*pair))
                order.append((c, self.ins[i][-1]))
        for _, copy in sorted(order, key=lambda pair: pair[0]):
            copy.start()

    def copy(self, source, target):
        self.next += 1
        return pltpu.make_async_copy(source, target, self.sems.at[self.next - 1])

    def need(self, *indices):
        for i in indices:
            for copy in self.ins[i]:
                copy.wait()

    def need_chunk(self, c, *indices):
        for i in indices:
            self.ins[i][c].wait()

    def done(self, *indices):
        for i in indices:
            copy = self.copy(self.results[i], self.targets[i])
            copy.start()
            self.pending.append(copy)

    def send(self, source, target):
        copy = self.copy(source, target)
        copy.start()
        self.pending.append(copy)

    def finish(self):
        for copy in self.pending:
            copy.wait()


def staged_call(kernel, scalars, ins, outs, extra_outs, scratch, flops, copies, room, chunks=None):
    n_s, n_i, n_o, n_e = len(scalars), len(ins), len(outs), len(extra_outs)

    def body(*refs):
        cut = [0]
        for size in (n_s, n_i, n_o, n_e, n_i, n_o, len(scratch)):
            cut.append(cut[-1] + size)
        scalar, source, target, extra, buffer, result, own = [refs[a:b] for a, b in zip(cut, cut[1:])]
        stage = Staged(source, buffer, target, result, refs[-1], chunks or {})
        kernel(stage, scalar, buffer, result, extra, own)
        stage.finish()

    results = pl.pallas_call(
        body,
        in_specs=[SMEM] * n_s + [HBM] * n_i,
        out_specs=(HBM,) * (n_o + n_e),
        out_shape=shaped(*outs, *extra_outs),
        scratch_shapes=[pltpu.VMEM(a.shape, a.dtype) for a in ins]
        + [pltpu.VMEM(shape, kind) for shape, kind in outs]
        + [pltpu.VMEM(shape, kind) for shape, kind in scratch]
        + [pltpu.SemaphoreType.DMA((copies,))],
        compiler_params=pltpu.CompilerParams(vmem_limit_bytes=room << 20),
        cost_estimate=pl.CostEstimate(flops=flops, bytes_accessed=8 << 20, transcendentals=0),
    )(*scalars, *ins)
    return results


def dot(left, right):
    return jnp.dot(left, right, preferred_element_type=F32)


def dot_lt(left, right):
    return lax.dot_general(left, right, (((0,), (0,)), ((), ())), preferred_element_type=F32)


def dot_rt(left, right):
    return lax.dot_general(left, right, (((1,), (1,)), ((), ())), preferred_element_type=F32)


def segment_order(tokens):
    steps = tokens // SUB
    to = lax.broadcasted_iota(jnp.int32, (tokens, tokens), 0)
    source = lax.broadcasted_iota(jnp.int32, (tokens, tokens), 1)
    return jnp.where(source == (to % SUB) * steps + to // SUB, 1.0, 0.0).astype(BF16)


def opened(first_len, seq_start, shape):
    sub = lax.broadcasted_iota(jnp.int32, shape, 0)
    rows = first_len.shape[0]
    result = jnp.ones(shape, F32)
    for r in range(rows):
        factor = jnp.where(first_len[r] == seq_start, 0.0, 1.0)
        result = jnp.where(sub == r * (SUB // rows), factor, result)
    return result


def at_row_start(shape, rows):
    return lax.broadcasted_iota(jnp.int32, shape, 0) % (SUB // rows) == 0


def at_row_end(shape, rows):
    parts = SUB // rows
    return lax.broadcasted_iota(jnp.int32, shape, 0) % parts == parts - 1


def rms(values):
    return lax.rsqrt(jnp.mean(values * values, axis=-1, keepdims=True) + EPS)


def fill_extended(ext, rim, first_len, seq_start, xhat_rim):
    lag, rows = rim.shape[1], rim.shape[0]
    width = ext.shape[-1]
    mask = opened(first_len, seq_start, (SUB, width))
    start = at_row_start((SUB, width), rows)
    total = ext.shape[0]
    for k in range(lag):
        near = pltpu.roll(ext[total - lag * SUB + k * SUB : total - lag * SUB + (k + 1) * SUB, :], 1, 0)
        ext[k * SUB : (k + 1) * SUB, :] = jnp.where(start, xhat_rim[k] * mask, near)


def rim_tiles(rim, spread):
    rows, lag, _ = rim.shape
    parts = SUB // rows
    spread[...] = jnp.zeros_like(spread)
    for k in range(lag):
        for r in range(rows):
            spread[k, r * parts : r * parts + 1, :] = rim[r, k : k + 1, :]
    return [spread[k] for k in range(lag)]


def gates_kernel(stage, scalars, ins, outs, extra, scratch):
    (first_len,) = scalars
    tokens, rim, gain_one, conv_weight, w_z, bias_z, w_h, cotangent = ins
    x_out, conv_out, keep_out, drive_out, cand_out, gate_out, pass_out, subk, subs, totals, up_out = outs
    ext, spread = scratch
    rows, group_len, width = tokens.shape
    count, lag = rows * group_len, rim.shape[1]
    hidden = w_z.shape[1]
    seq_start = lax.axis_index("seq") * group_len
    order = segment_order(count)
    stage.need(0)
    x = dot(order, tokens[...].reshape(count, width))
    x_out[...] = x.astype(BF16)
    stage.done(0)
    stage.need(1, 2, 3)
    normed = x * rms(x) * gain_one[...]
    ext[lag * SUB :, :] = normed
    rim_x = rim_tiles(rim, spread)
    fill_extended(ext, rim, first_len, seq_start, [v * rms(v) * gain_one[...] for v in rim_x])
    mixed = jnp.zeros((count, width), F32)
    for j in range(lag + 1):
        begin = (lag - j) * SUB
        mixed = mixed + conv_weight[j : j + 1, :] * ext[begin : begin + count, :]
    conv_out[...] = mixed.astype(BF16)
    stage.done(1)
    stage.need(4, 5, 6)
    mask = opened(first_len, seq_start, (SUB, hidden))
    block = 256
    for b in range(hidden // block):
        cols = slice(b * block, (b + 1) * block)
        g = dot(conv_out[...], w_z[:, cols]) + bias_z[:, cols]
        c = dot(conv_out[...], w_h[:, cols])
        small = jnp.exp(-jnp.abs(g))
        large = 1.0 / (1.0 + small)
        small = small * large
        zeta = jnp.where(g >= 0, large, small)
        sig = 1.0 / (1.0 + jnp.exp(-c))
        cand = jnp.where(c >= 0, c + 0.5, sig)
        keep_out[:, cols] = jnp.where(g >= 0, small, large)
        keep_out[0:SUB, cols] = keep_out[0:SUB, cols] * mask[:, cols]
        drive_out[:, cols] = zeta * cand
        cand_out[:, cols] = cand
        gate_out[:, cols] = (small * large).astype(BF16)
        pass_out[:, cols] = (zeta * jnp.where(c >= 0, 1.0, sig * (1.0 - sig))).astype(BF16)
        for i in (2, 3, 4, 5, 6):
            stage.send(outs[i].at[:, pl.ds(b * block, block)], stage.targets[i].at[:, pl.ds(b * block, block)])

    def step(i, carry):
        total, state = carry
        at = pl.ds(pl.multiple_of(i * SUB, SUB), SUB)
        keep = keep_out[at, :]
        return total * keep, keep * state + drive_out[at, :]

    total, state = lax.fori_loop(
        0, count // SUB, step, (jnp.ones((SUB, hidden), F32), jnp.zeros((SUB, hidden), F32)), unroll=8
    )
    subk[...] = total
    subs[...] = state
    parts = SUB // rows
    for r in range(rows):
        at = slice(r * parts, r * parts + 1)
        k, s = subk[at, :], subs[at, :]
        for h in range(1, parts):
            at = slice(r * parts + h, r * parts + h + 1)
            s = subs[at, :] + subk[at, :] * s
            k = k * subk[at, :]
        totals[0, r : r + 1, :] = k
        totals[1, r : r + 1, :] = s
    stage.done(7, 8, 9)
    stage.need(7)
    up_out[...] = dot(order, cotangent[...].reshape(count, width)).astype(BF16)
    stage.done(10)


def give_pair(stage, even, pairs):
    found = []
    for one, two, mine, other in pairs:
        found.append((stage.copy(one, mine), stage.copy(two, other), one, two, mine, other, stage.next))

    @pl.when(even)
    def _():
        for first, second, *_ in found:
            first.start()
            second.start()

    @pl.when(jnp.logical_not(even))
    def _():
        for _, _, one, two, mine, other, at in found:
            pltpu.make_async_copy(two, mine, stage.sems.at[at - 2]).start()
            pltpu.make_async_copy(one, other, stage.sems.at[at - 1]).start()

    for first, second, *_ in found:
        stage.pending += [first, second]


def mlp_kernel(stage, scalars, ins, outs, extra, scratch):
    (first_len,) = scalars
    carried, subk, subs, keep, drive, cand, gate, x, w_out, gain_two, w_up, w_down, up = ins
    blend, output, grad_middle_out, grad_gain_two, grad_state, subb, totals = outs
    mine, other, mine_out, other_out = extra
    before, low, second_low, tail, second_grad, middle_ref, for_even, for_odd, out_even, out_odd = scratch
    count, width = x.shape
    hidden, ff = keep.shape[1], w_up.shape[1]
    rows = carried.shape[0]
    group_len = count // rows
    parts = SUB // rows
    pairs = count // SUB // 2
    seq_start = lax.axis_index("seq") * group_len
    even = lax.axis_index("row") % 2 == 0
    stage.need(0, 1, 2)
    for r in range(rows):
        s = carried[r : r + 1, :]
        before[r * parts : r * parts + 1, :] = s
        for h in range(1, parts):
            at = slice(r * parts + h - 1, r * parts + h)
            s = subs[at, :] + subk[at, :] * s
            before[r * parts + h : r * parts + h + 1, :] = s

    def two(i, state):
        at = pl.ds(pl.multiple_of(i * 2 * SUB, 2 * SUB), 2 * SUB)
        k, d, c, g = keep[at, :], drive[at, :], cand[at, :], gate[at, :].astype(F32)
        first = k[:SUB] * state + d[:SUB]
        second = k[SUB:] * first + d[SUB:]
        low[at, :] = jnp.concatenate([first, second], axis=0).astype(BF16)
        earlier = jnp.concatenate([state, first], axis=0)
        blend[at, :] = ((c - earlier) * g).astype(BF16)
        return second

    state = before[...] * opened(first_len, seq_start, (SUB, hidden))
    for c in range(CHUNKS):
        stage.need_chunk(c, 3, 4, 5, 6)
        state = lax.fori_loop(c * pairs // CHUNKS, (c + 1) * pairs // CHUNKS, two, state, unroll=2)
    stage.done(0)
    stage.need(7, 8, 9)
    middle = x[...].astype(F32) + dot(low[...], w_out[...])
    middle_ref[...] = middle
    second_low[...] = (middle * rms(middle) * gain_two[...]).astype(BF16)
    tail[...] = jnp.zeros_like(tail)
    second_grad[...] = jnp.zeros_like(second_grad)
    stage.need(10, 11, 12)
    block = width
    half = ff // block // 2

    def part(b, carry):
        at = pl.ds(pl.multiple_of(b * block, block), block)
        pre = dot(second_low[...], w_up[:, at])
        back = dot_rt(up[...], w_down[at, :])
        scaled = pre * 0.7071067811865476
        phi = 0.5 + 0.5 * lax.erf(scaled)
        active = (pre * phi).astype(BF16)
        slope = phi + pre * (0.3989422804014327 * jnp.exp(-scaled * scaled))
        up_low = (slope * back).astype(BF16)
        for_even[at, :] = dot_lt(active, up[...])
        for_odd[at, :] = dot_lt(second_low[...], up_low)
        tail[...] += dot(active, w_down[at, :])
        second_grad[...] += dot_rt(up_low, w_up[:, at])
        return carry

    for k in range(2):
        lax.fori_loop(k * half, (k + 1) * half, part, 0)
        at = pl.ds(k * half * block, half * block)
        give_pair(stage, even, [(for_even.at[at], for_odd.at[at], mine.at[at], other.at[at])])

    middle = middle_ref[...]
    scale = rms(middle)
    unit = middle * scale
    grad = second_grad[...]
    grad_gain_two[...] = jnp.sum(grad * unit, axis=0, keepdims=True)
    grad = grad * gain_two[...]
    grad_middle = up[...].astype(F32) + scale * (grad - unit * jnp.mean(grad * unit, axis=-1, keepdims=True))
    grad_middle_out[...] = grad_middle
    stage.done(2, 3)
    middle_low = grad_middle.astype(BF16)
    grad_state[...] = dot_rt(middle_low, w_out[...])
    stage.done(4)

    def back_step(i, passed):
        at = pl.ds(pl.multiple_of((2 * pairs - 1 - i) * SUB, SUB), SUB)
        return keep[at, :] * (grad_state[at, :] + passed)

    subb[...] = lax.fori_loop(0, 2 * pairs, back_step, jnp.zeros((SUB, hidden), F32), unroll=8)
    for r in range(rows):
        end = r * parts + parts - 1
        b = subb[end : end + 1, :]
        for h in range(parts - 2, -1, -1):
            at = slice(r * parts + h, r * parts + h + 1)
            b = subb[at, :] + subk[at, :] * b
        totals[r : r + 1, :] = b
    stage.done(5, 6)
    half_h = hidden // 2
    out_even[...] = dot_lt(low[:, :half_h], middle_low)
    out_odd[...] = dot_lt(low[:, half_h:], middle_low)
    give_pair(stage, even, [(out_even, out_odd, mine_out, other_out)])
    result = (middle_ref[...] + tail[...]).astype(BF16)
    output[...] = dot_lt(segment_order(count), result).astype(BF16).reshape(output.shape)
    stage.done(1)


def first_kernel(stage, scalars, ins, outs, extra, scratch):
    (first_len,) = scalars
    (returned, subk, subb, keep, grad_state, blend, passing, conv_low, w_z, w_h, x_ref, rim, gain_one, conv_weight,
     grad_middle, grad_gain_two) = ins
    grad_tokens, sent, tail_normed, tail_middle = outs
    mine_a, other_a, mine_b, other_b = extra
    incoming, gate_low, cand_low, ext, spread, grad_ext, bias_sum, small, for_even, for_odd, rest = scratch
    count, width = x_ref.shape
    hidden = keep.shape[1]
    rows, lag = rim.shape[0], rim.shape[1]
    parts = SUB // rows
    pairs = count // SUB // 2
    seq_start = lax.axis_index("seq") * (count // rows)
    even = lax.axis_index("row") % 2 == 0
    stage.need(0, 1, 2)
    for r in range(rows):
        b = returned[r : r + 1, :]
        incoming[r * parts + parts - 1 : (r + 1) * parts, :] = b
        for h in range(parts - 2, -1, -1):
            at = slice(r * parts + h + 1, r * parts + h + 2)
            b = subb[at, :] + subk[at, :] * b
            incoming[r * parts + h : r * parts + h + 1, :] = b

    def two(i, carry):
        passed, bias = carry
        at = pl.ds(pl.multiple_of((pairs - 1 - i) * 2 * SUB, 2 * SUB), 2 * SUB)
        k, g = keep[at, :], grad_state[at, :]
        late = g[SUB:] + passed
        early = g[:SUB] + k[SUB:] * late
        adjoint = jnp.concatenate([early, late], axis=0)
        grad_g = adjoint * blend[at, :].astype(F32)
        gate_low[at, :] = grad_g.astype(BF16)
        cand_low[at, :] = (adjoint * passing[at, :].astype(F32)).astype(BF16)
        return k[:SUB] * early, bias + grad_g[:SUB] + grad_g[SUB:]

    carry = (incoming[...], jnp.zeros((SUB, hidden), F32))
    for c in range(CHUNKS):
        stage.need_chunk(CHUNKS - 1 - c, 3, 4, 5, 6)
        carry = lax.fori_loop(c * pairs // CHUNKS, (c + 1) * pairs // CHUNKS, two, carry, unroll=2)
    bias = carry[1]
    bias_sum[...] = jnp.sum(bias, axis=0, keepdims=True)
    stage.need(7)
    half = width // 2
    for_even[...] = dot_lt(conv_low[...], gate_low[...])
    for_odd[...] = dot_lt(conv_low[...], cand_low[...])
    cols = pl.ds(0, hidden)
    low_rows, high_rows = pl.ds(0, half), pl.ds(half, half)
    give_pair(stage, even, [
        (for_even.at[low_rows], for_odd.at[low_rows], mine_a, other_a),
        (for_even.at[high_rows], for_odd.at[high_rows], mine_b.at[:, cols], other_b.at[:, cols]),
    ])
    stage.need(8, 9, 10, 11, 12, 13, 14, 15)
    grad_mixed = dot_rt(gate_low[...], w_z[...]) + dot_rt(cand_low[...], w_h[...])

    x = x_ref[...].astype(F32)
    scale = rms(x)
    unit = x * scale
    gain = gain_one[...]
    ext[lag * SUB :, :] = unit * gain
    rim_x = rim_tiles(rim, spread)
    rim_unit = [v * rms(v) for v in rim_x]
    fill_extended(ext, rim, first_len, seq_start, [v * gain for v in rim_unit])
    small[0:1, :] = jnp.zeros((1, width), F32)
    for j in range(lag + 1):
        begin = (lag - j) * SUB
        small[1 + j : 2 + j, :] = jnp.sum(grad_mixed * ext[begin : begin + count, :], axis=0, keepdims=True)
    for j in range(hidden // width):
        at = 2 + lag + j
        small[at : at + 1, :] = bias_sum[:, j * width : (j + 1) * width]
    last = 2 + lag + hidden // width
    small[last : last + 1, :] = grad_gain_two[...]
    grad_ext[...] = jnp.zeros_like(grad_ext)
    for j in range(lag + 1):
        begin = (lag - j) * SUB
        grad_ext[begin : begin + count, :] += conv_weight[j : j + 1, :] * grad_mixed
    mask = opened(first_len, seq_start, (SUB, width))
    start = at_row_start((SUB, width), rows)
    end = at_row_end((SUB, width), rows)
    grad_gain = jnp.zeros((SUB, width), F32)
    for k in range(lag):
        head = grad_ext[k * SUB : (k + 1) * SUB, :]
        tail_at = pl.ds(count + k * SUB, SUB)
        near = pltpu.roll(head, SUB - 1, 0)
        grad_ext[tail_at, :] = grad_ext[tail_at, :] + jnp.where(end, 0.0, near)
        to_rim = jnp.where(start, head * mask, 0.0)
        grad_gain = grad_gain + to_rim * rim_unit[k]
        spread[k] = to_rim
        for r in range(rows):
            sent[r, k : k + 1, :] = spread[k, r * parts : r * parts + 1, :]
    grad_normed = grad_ext[lag * SUB :, :]
    small[0:1, :] = jnp.sum(grad_normed * unit, axis=0, keepdims=True) + jnp.sum(
        grad_gain, axis=0, keepdims=True
    )
    rest[...] = jnp.zeros_like(rest)
    for j in range(width // 128):
        rest[j * SUB : (j + 1) * SUB, :] = small[:, j * 128 : (j + 1) * 128]
    past = pl.ds(hidden, 128)
    give_pair(stage, even, [(rest.at[low_rows], rest.at[high_rows], mine_b.at[:, past], other_b.at[:, past])])
    for k in range(lag):
        at = count - lag * SUB + k * SUB
        for r in range(rows):
            row = at + r * parts + parts - 1
            to = tail_normed.shape[1] - lag + k
            tail_normed[r, to : to + 1, :] = grad_ext[lag * SUB + row : lag * SUB + row + 1, :]
            tail_middle[r, to : to + 1, :] = grad_middle[row : row + 1, :]
    grad = grad_normed * gain
    grad_x = grad_middle[...] + scale * (grad - unit * jnp.mean(grad * unit, axis=-1, keepdims=True))
    stage.done(1, 2, 3)
    order = segment_order(count)
    grad_tokens[...] = dot_lt(order, grad_x.astype(BF16)).astype(BF16).reshape(grad_tokens.shape)
    stage.done(0)


def tail_kernel(tokens, tail_normed, tail_middle, received, gain_one, _, grad_tokens, spread):
    rows, tile, width = tokens.shape
    lag = received.shape[1]
    for r in range(rows):
        spread[tile - lag :, :] = tail_normed[r, tile - lag :, :] + received[r]
        x = tokens[r].astype(F32)
        scale = rms(x)
        unit = x * scale
        grad = spread[...] * gain_one[...]
        fixed = tail_middle[r] + scale * (grad - unit * jnp.mean(grad * unit, axis=-1, keepdims=True))
        changed = lax.broadcasted_iota(jnp.int32, (tile, width), 0) >= tile - lag
        grad_tokens[r] = jnp.where(changed, fixed, _[r].astype(F32)).astype(BF16)


def shaped(*shapes):
    return tuple(jax.ShapeDtypeStruct(shape, kind) for shape, kind in shapes)


def swapped(array, axis, bit):
    return lax.ppermute(array, axis, [(i, i ^ bit) for i in range(lax.axis_size(axis))])


def bits_of(axis):
    bit, result = 1, []
    while bit < lax.axis_size(axis):
        result.append(bit)
        bit *= 2
    return result


def upper(axis, bit):
    return (lax.axis_index(axis) // bit) % 2 == 1


def carry_forward(totals):
    keep, state = totals[0], totals[1]
    before_k, before_s = jnp.ones_like(keep), jnp.zeros_like(state)
    levels = []
    for bit in bits_of("seq"):
        other = swapped(jnp.stack([keep, state]), "seq", bit)
        other_k, other_s = other[0], other[1]
        late = upper("seq", bit)
        levels.append((keep, other_k))
        before_s = jnp.where(late, before_s + before_k * other_s, before_s)
        before_k = jnp.where(late, before_k * other_k, before_k)
        state = jnp.where(late, state + keep * other_s, other_s + other_k * state)
        keep = keep * other_k
    return before_s, levels


def carry_backward(passed, levels):
    after_b, after_k = jnp.zeros_like(passed), jnp.ones_like(passed)
    seen = []
    for bit, (keep, other_k) in zip(bits_of("seq"), levels):
        other_b = swapped(passed, "seq", bit)
        late = upper("seq", bit)
        after_b = jnp.where(late, after_b, after_b + after_k * other_b)
        after_k = jnp.where(late, after_k, after_k * other_k)
        passed = jnp.where(late, other_b + other_k * passed, passed + keep * other_b)
        seen.append(passed)
    return after_b, seen


BOTH = ("row", "seq")


def axis_steps(order):
    seq = [("seq", bit) for bit in bits_of("seq")]
    parts = {"x": seq[:1], "y": [("row", bit) for bit in bits_of("row")[1:]], "a": seq[1:2], "b": seq[2:]}
    swap = {"x": "y", "y": "x", "a": "a", "b": "b"}
    even = sum((parts[letter] for letter in order), [])
    odd = sum((parts[swap[letter]] for letter in order), [])
    return list(zip(even, odd))


def exchanged(array, even, odd):
    rows, devices = lax.axis_size("row"), lax.axis_size("seq")
    pairs = []
    for r in range(rows):
        for s in range(devices):
            axis, bit = odd if r & 1 else even
            to = ((r ^ bit) * devices + s) if axis == "row" else (r * devices + (s ^ bit))
            pairs.append((r * devices + s, to))
    return lax.ppermute(array, BOTH, pairs)


def place_bit(step):
    even, odd = [lax.axis_index(axis) // bit % 2 for axis, bit in step]
    return jnp.where(lax.axis_index("row") % 2 == 0, even, odd)


def by_rows(total, body):
    chunk = next((c for c in (64, 32, 16, 8) if total % c == 0), total)
    if chunk == total:
        body(0, chunk)
        return

    def turn(i, carry):
        body(pl.multiple_of(i * chunk, chunk), chunk)
        return carry

    lax.fori_loop(0, total // chunk, turn, 0)


def tiled(first, rows):
    return pl.multiple_of(first, SUB) if rows % SUB == 0 else first


def split_rows(step, mine, received, send, keep):
    half, bit = send.shape[0], place_bit(step)
    if half % SUB:
        first = mine[:half, :] + received[:half, :]
        second = mine[half:, :] + received[half:, :]
        lower = jnp.broadcast_to(bit == 0, first.shape)
        send[...] = jnp.where(lower, second, first)
        keep[...] = jnp.where(lower, first, second)
        return

    def body(i, chunk):
        to = pl.ds(i, chunk)
        for out, begin in ((send, (1 - bit) * half), (keep, bit * half)):
            at = pl.ds(pl.multiple_of(i + begin, SUB), chunk)
            out[to, :] = mine[at, :] + received[at, :]

    by_rows(half, body)


def add_rows(_, mine, received, out):
    def body(i, chunk):
        at = pl.ds(i, chunk)
        out[at, :] = mine[at, :] + received[at, :]

    by_rows(mine.shape[0], body)


def join_rows(step, mine, received, out):
    half, bit = mine.shape[0], place_bit(step)
    if half % SUB:
        lower = jnp.broadcast_to(bit == 0, mine.shape)
        out[:half, :] = jnp.where(lower, mine[...], received[...])
        out[half:, :] = jnp.where(lower, received[...], mine[...])
        return

    def body(i, chunk):
        at = pl.ds(i, chunk)
        for source, begin in ((mine, bit * half), (received, (1 - bit) * half)):
            out[pl.ds(pl.multiple_of(i + begin, SUB), chunk), :] = source[at, :]

    by_rows(half, body)


CORE = (("row", 1),) * 2


class Summed:
    def __init__(self, mine, other, order):
        self.steps = axis_steps(order)
        self.mine, self.stage = mine, 1
        self.received = exchanged(other, *CORE)

    def work(self):
        count = len(self.steps)
        rows, width = self.mine.shape
        if self.stage <= count:
            return split_rows, self.steps[self.stage - 1], [(rows // 2, width)] * 2
        if self.stage == count + 1:
            return add_rows, None, [(rows, width)]
        return join_rows, self.steps[2 * count + 1 - self.stage], [(2 * rows, width)]

    def give(self, outs):
        count = len(self.steps)
        self.mine = outs[-1]
        step = self.steps[self.stage - 1 if self.stage <= count else 2 * count - self.stage]
        self.received = exchanged(outs[0], *step)
        self.stage += 1

    def busy(self):
        return self.stage <= 2 * len(self.steps)

    def across(self):
        self.others = exchanged(self.mine, *CORE), exchanged(self.received, *CORE)


def wave(tokens, sums, through=()):
    works = [one.work() for one in sums]

    def kernel(*refs):
        refs = refs[len(tokens) + len(through) :]
        ins, outs = refs[: 2 * len(sums)], list(refs[2 * len(sums) + len(through) :])
        for i, (rows, step, shapes) in enumerate(works):
            mine_outs = [outs.pop(0) for _ in shapes]
            rows(step, ins[2 * i], ins[2 * i + 1], *mine_outs)

    shapes = [shape for _, _, shapes in works for shape in shapes]
    outs = list(pl.pallas_call(
        kernel,
        in_specs=[ANY] * (len(tokens) + len(through)) + [VMEM] * (2 * len(sums)),
        out_specs=(ANY,) * len(through) + (VMEM,) * len(shapes),
        out_shape=shaped(*[(array.shape, F32) for array in through], *[(shape, F32) for shape in shapes]),
        input_output_aliases={len(tokens) + i: i for i in range(len(through))},
        compiler_params=pltpu.CompilerParams(vmem_limit_bytes=24 << 20),
        cost_estimate=pl.CostEstimate(flops=1, bytes_accessed=1, transcendentals=0),
    )(*tokens, *through, *[array for one in sums for array in (one.mine, one.received)]))
    passed = [outs.pop(0) for _ in through]
    first = outs[0]
    for one, (_, _, shapes) in zip(sums, works):
        one.give([outs.pop(0) for _ in shapes])
    return first, passed


def finish_kernel(steps, routes, total, _, *refs):
    count = len(steps)
    arrays, outs = refs[: 4 * count], refs[4 * count : 4 * count + total]
    buffers, sems = refs[4 * count + total : -1], refs[-1]
    even = lax.axis_index("row") % 2 == 0
    base, plans = 0, []
    for k, step in enumerate(steps):
        own = arrays[4 * k : 4 * k + 4]
        rows = own[0].shape[0]
        for parity in range(2):
            axis, bit = step[parity]
            place = lax.axis_index(axis) // bit % 2
            longest = 0
            for is_own in (True, False):
                for upper_half in range(2):
                    pair = own[:2] if is_own else own[2:]
                    plan = []
                    for half in range(2):
                        source = pair[half ^ upper_half]
                        buffer = buffers[k].at[parity, half]
                        for at, columns, output, to in routes(k, parity, half * rows, rows):
                            plan.append((source.at[at, columns], buffer.at[at, columns], outs[output].at[to]))
                    mine = even if is_own == (parity == 0) else jnp.logical_not(even)
                    plans.append((jnp.logical_and(mine, place == upper_half), plan, base))
                    longest = max(longest, len(plan))
            base += longest
    for condition, plan, first in plans:

        @pl.when(condition)
        def _():
            for i, (source, buffer, _) in enumerate(plan):
                pltpu.make_async_copy(source, buffer, sems.at[0, first + i]).start()

    for condition, plan, first in plans:

        @pl.when(condition)
        def _():
            for i, (source, buffer, target) in enumerate(plan):
                pltpu.make_async_copy(source, buffer, sems.at[0, first + i]).wait()
                pltpu.make_async_copy(buffer, target, sems.at[1, first + i]).start()

    for condition, plan, first in plans:

        @pl.when(condition)
        def _():
            for i, (source, buffer, target) in enumerate(plan):
                pltpu.make_async_copy(buffer, target, sems.at[1, first + i]).wait()


def finish_call(routes, token, sums, outs):
    arrays = [array for one in sums for array in (one.mine, one.received, *one.others)]
    return pl.pallas_call(
        functools.partial(finish_kernel, [one.steps[0] for one in sums], routes, len(outs)),
        in_specs=[pl.BlockSpec(memory_space=pl.ANY)] * (1 + len(arrays)),
        out_specs=(HBM,) * len(outs),
        out_shape=shaped(*outs),
        scratch_shapes=[pltpu.VMEM((2, 2) + one.mine.shape, F32) for one in sums]
        + [pltpu.SemaphoreType.DMA((2, 48))],
        compiler_params=pltpu.CompilerParams(vmem_limit_bytes=32 << 20),
        cost_estimate=pl.CostEstimate(flops=1, bytes_accessed=1, transcendentals=0),
    )(token, *arrays)


def cut(first, rows, marks):
    inside = [first] + [m for m in marks if first < m < first + rows] + [first + rows]
    return [(a - first, a, b - a) for a, b in zip(inside, inside[1:])]


def per_device(
    tokens, first_len, gain_one, conv_weight, w_z, bias_z, w_h, w_out, gain_two, w_up, w_down, cotangent
):
    rows, group_len, width = tokens.shape
    hidden, ff = w_z.shape[1], w_up.shape[1]
    lag = conv_weight.shape[0] - 1
    count = rows * group_len
    devices = lax.axis_size("seq")
    gain_one, gain_two, bias_z = gain_one[None], gain_two[None], bias_z[None]
    rim = lax.ppermute(
        tokens[:, group_len - lag :].astype(F32), "seq", [(i, i + 1) for i in range(devices - 1)]
    )
    th, tw = (count, hidden), (count, width)
    chunks = {3: CHUNKS, 4: CHUNKS, 5: CHUNKS, 6: CHUNKS}
    x, conv_low, keep, drive, cand, gate, passing, subk, subs, totals, up = staged_call(
        gates_kernel,
        [first_len],
        [tokens, rim, gain_one, conv_weight, w_z, bias_z, w_h, cotangent],
        [(tw, BF16), (tw, BF16), (th, F32), (th, F32), (th, F32), (th, BF16), (th, BF16),
         ((SUB, hidden), F32), ((SUB, hidden), F32), ((2, rows, hidden), F32), (tw, BF16)],
        [],
        [((count + lag * SUB, width), F32), ((lag, SUB, width), F32)],
        4 * count * width * hidden,
        64,
        56,
    )
    carried, levels = carry_forward(totals)
    mlp_pair, out_pair = ((ff, width), F32), ((hidden // 2, width), F32)
    blend, output, grad_middle, grad_gain_two, grad_state, subb, passed, mine_a, other_a, mine_b, other_b = staged_call(
        mlp_kernel,
        [first_len],
        [carried, subk, subs, keep, drive, cand, gate, x, w_out, gain_two, w_up, w_down, up],
        [(th, BF16), (tokens.shape, BF16), (tw, F32), ((1, width), F32), (th, F32), ((SUB, hidden), F32),
         ((rows, hidden), F32)],
        [mlp_pair, mlp_pair, out_pair, out_pair],
        [((SUB, hidden), F32), (th, BF16), (tw, BF16), (tw, F32), (tw, F32), (tw, F32),
         ((ff, width), F32), ((ff, width), F32), ((hidden // 2, width), F32), ((hidden // 2, width), F32)],
        12 * count * width * ff,
        64,
        56,
        chunks,
    )
    returned, seen = carry_backward(passed, levels)
    early = [Summed(mine_a, other_a, ORDERS[0]), Summed(mine_b, other_b, ORDERS[1])]
    token, _ = wave([(passed, *seen)[HOLD]], early)
    tile = 16
    pair = ((width // 2, hidden), F32)
    pair_small = ((width // 2, hidden + 128), F32)
    grad_tokens, sent, tail_normed, tail_middle, mine_c, other_c, mine_d, other_d = staged_call(
        first_kernel,
        [first_len],
        [returned, subk, subb, keep, grad_state, blend, passing, conv_low, w_z, w_h, x, rim, gain_one,
         conv_weight, grad_middle, grad_gain_two],
        [(tokens.shape, BF16), ((rows, lag, width), F32)] + [((rows, tile, width), F32)] * 2,
        [pair, pair, pair_small, pair_small],
        [((SUB, hidden), F32), (th, BF16), (th, BF16), ((count + lag * SUB, width), F32),
         ((lag, SUB, width), F32), ((count + lag * SUB, width), F32), ((1, hidden), F32), ((SUB, width), F32),
         ((width, hidden), F32), ((width, hidden), F32), ((width, 128), F32)],
        8 * count * width * hidden,
        64,
        30,
        chunks,
    )
    received = lax.ppermute(sent, "seq", [(i + 1, i) for i in range(devices - 1)])
    at_tail = pl.BlockSpec((rows, tile, width), lambda i: (0, group_len // tile - 1, 0))
    whole = lambda *shape: pl.BlockSpec(shape, lambda i: (0,) * len(shape))
    grad_tokens = pl.pallas_call(
        tail_kernel,
        grid=(1,),
        in_specs=[at_tail, whole(rows, tile, width), whole(rows, tile, width), whole(rows, lag, width),
                  whole(1, width), at_tail],
        out_specs=at_tail,
        out_shape=jax.ShapeDtypeStruct(tokens.shape, BF16),
        scratch_shapes=[pltpu.VMEM((tile, width), F32)],
        input_output_aliases={5: 0},
    )(tokens, tail_normed, tail_middle, received, gain_one, grad_tokens)
    late = [Summed(mine_c, other_c, ORDERS[2]), Summed(mine_d, other_d, ORDERS[3])]
    tokens = [[tail_normed], [grad_tokens]]
    while late[0].busy():
        more = tokens.pop(0) if tokens else []
        if early[0].busy():
            token, _ = wave([token, *more], early + late)
        else:
            token, ready = wave([token, *more], late, [one.received for one in early])
            for one, received in zip(early, ready):
                one.received = received
    for one in early:
        one.across()
    for one in late:
        one.across()

    def mlp_routes(k, parity, first, rows):
        everything, plan = pl.ds(0, width), []
        if k == 1:
            return [(pl.ds(0, rows), everything, 2, (pl.ds(first + parity * hidden // 2, rows), everything))]
        for offset, at, size in cut(first, rows, range(0, ff, width)):
            inner = pl.ds(offset, size)
            if parity == 0:
                plan.append((inner, everything, 0, (pl.ds(at, size), everything)))
            else:
                block = at // width * width
                plan.append((inner, everything, 1, (pl.ds(at - block, size), pl.ds(block, width))))
        return plan

    def gate_routes(k, parity, first, rows):
        inner, cols = pl.ds(0, rows), pl.ds(0, hidden)
        plan = [(inner, cols, parity, (pl.ds(first + k * width // 2, rows), cols))]
        few = SUB * width // 128
        if k == 1 and parity == 0 and first < few:
            least = min(rows, few - first)
            at, all_cols = pl.ds(0, least), pl.ds(0, 128)
            plan.append((at, pl.ds(hidden, 128), 2, (pl.ds(first, least), all_cols)))
        return plan

    grad_down, grad_up, grad_out = finish_call(
        mlp_routes, token, early, [((ff, width), F32), ((width, ff), F32), ((hidden, width), F32)]
    )
    grad_z, grad_h, small = finish_call(
        gate_routes, grad_out, late,
        [((width, hidden), F32), ((width, hidden), F32), ((SUB * width // 128, 128), F32)],
    )
    small = small.reshape(width // 128, SUB, 128).swapaxes(0, 1).reshape(SUB, width)
    bias_at = 2 + lag
    gain_at = bias_at + hidden // width
    return (
        output,
        grad_tokens,
        small[0],
        small[1:bias_at],
        grad_z,
        small[bias_at:gain_at].reshape(hidden),
        grad_h,
        grad_out,
        small[gain_at],
        grad_up,
        grad_down,
    )


def solution(mesh):
    block, copied = P("row", "seq", None), P()
    return jax.shard_map(
        per_device,
        mesh=mesh,
        in_specs=(block, P("row")) + (copied,) * 9 + (block,),
        out_specs=(block, block) + (copied,) * 9,
        check_vma=False,
    )
```

```python
import functools

import jax
import jax.numpy as jnp
from jax import lax
from jax.experimental import pallas as pl
from jax.experimental.pallas import tpu as pltpu
from jax.sharding import PartitionSpec as P

F32, BF16 = jnp.float32, jnp.bfloat16
EPS = 1e-06
VMEM = pl.BlockSpec(memory_space=pltpu.VMEM)
SMEM = pl.BlockSpec(memory_space=pltpu.SMEM)
ORDERS = ("xyab", "xyab", "abxy", "xyab")
TAIL = 5
CHUNKS = 4
FINISH = 56
WAVE = 24
LAST = 30
UNROLL = 2
HOLD = 1
SUB = 8


HBM = pl.BlockSpec(memory_space=pltpu.HBM)
ANY = pl.BlockSpec(memory_space=pl.ANY)


class Staged:
    def __init__(self, sources, buffers, targets, results, sems, chunks):
        self.ins, self.pending, self.sems, self.next = {}, [], sems, 0
        self.targets, self.results = targets, results
        order = []
        for i, (source, buffer) in enumerate(zip(sources, buffers)):
            parts = chunks.get(i, 1)
            rows = source.shape[0] // parts
            self.ins[i] = []
            for c in range(parts):
                at = pl.ds(c * rows, rows)
                pair = (source, buffer) if parts == 1 else (source.at[at], buffer.at[at])
                self.ins[i].append(self.copy(*pair))
                order.append((c, self.ins[i][-1]))
        for _, copy in sorted(order, key=lambda pair: pair[0]):
            copy.start()

    def copy(self, source, target):
        self.next += 1
        return pltpu.make_async_copy(source, target, self.sems.at[self.next - 1])

    def need(self, *indices):
        for i in indices:
            for copy in self.ins[i]:
                copy.wait()

    def need_chunk(self, c, *indices):
        for i in indices:
            self.ins[i][c].wait()

    def done(self, *indices):
        for i in indices:
            copy = self.copy(self.results[i], self.targets[i])
            copy.start()
            self.pending.append(copy)

    def send(self, source, target):
        copy = self.copy(source, target)
        copy.start()
        self.pending.append(copy)

    def finish(self):
        for copy in self.pending:
            copy.wait()


def staged_call(kernel, scalars, ins, outs, extra_outs, scratch, flops, copies, room, chunks=None):
    views = [one[1] if isinstance(one, tuple) else None for one in ins]
    ins = [one[0] if isinstance(one, tuple) else one for one in ins]
    inside = [one.shape if view is None else tuple(at.size for at in view) for one, view in zip(ins, views)]
    n_s, n_i, n_o, n_e = len(scalars), len(ins), len(outs), len(extra_outs)

    def body(*refs):
        cut = [0]
        for size in (n_s, n_i, n_o, n_e, n_i, n_o, len(scratch)):
            cut.append(cut[-1] + size)
        scalar, source, target, extra, buffer, result, own = [refs[a:b] for a, b in zip(cut, cut[1:])]
        source = [ref if view is None else ref.at[view] for ref, view in zip(source, views)]
        stage = Staged(source, buffer, target, result, refs[-1], chunks or {})
        kernel(stage, scalar, buffer, result, extra, own)
        stage.finish()

    results = pl.pallas_call(
        body,
        in_specs=[SMEM] * n_s + [HBM] * n_i,
        out_specs=(HBM,) * (n_o + n_e),
        out_shape=shaped(*outs, *extra_outs),
        scratch_shapes=[pltpu.VMEM(shape, a.dtype) for shape, a in zip(inside, ins)]
        + [pltpu.VMEM(shape, kind) for shape, kind in outs]
        + [pltpu.VMEM(shape, kind) for shape, kind in scratch]
        + [pltpu.SemaphoreType.DMA((copies,))],
        compiler_params=pltpu.CompilerParams(vmem_limit_bytes=room << 20),
        cost_estimate=pl.CostEstimate(flops=flops, bytes_accessed=8 << 20, transcendentals=0),
    )(*scalars, *ins)
    return results


def dot(left, right):
    return jnp.dot(left, right, preferred_element_type=F32)


def dot_lt(left, right):
    return lax.dot_general(left, right, (((0,), (0,)), ((), ())), preferred_element_type=F32)


def dot_rt(left, right):
    return lax.dot_general(left, right, (((1,), (1,)), ((), ())), preferred_element_type=F32)


def segment_order(tokens):
    steps = tokens // SUB
    to = lax.broadcasted_iota(jnp.int32, (tokens, tokens), 0)
    source = lax.broadcasted_iota(jnp.int32, (tokens, tokens), 1)
    return jnp.where(source == (to % SUB) * steps + to // SUB, 1.0, 0.0).astype(BF16)


def opened(first_len, seq_start, shape):
    sub = lax.broadcasted_iota(jnp.int32, shape, 0)
    rows = first_len.shape[0]
    result = jnp.ones(shape, F32)
    for r in range(rows):
        factor = jnp.where(first_len[r] == seq_start, 0.0, 1.0)
        result = jnp.where(sub == r * (SUB // rows), factor, result)
    return result


def at_row_start(shape, rows):
    return lax.broadcasted_iota(jnp.int32, shape, 0) % (SUB // rows) == 0


def at_row_end(shape, rows):
    parts = SUB // rows
    return lax.broadcasted_iota(jnp.int32, shape, 0) % parts == parts - 1


def rms(values):
    return lax.rsqrt(jnp.mean(values * values, axis=-1, keepdims=True) + EPS)


def fill_extended(ext, rim, first_len, seq_start, xhat_rim):
    lag, rows = rim.shape[1], rim.shape[0]
    width = ext.shape[-1]
    mask = opened(first_len, seq_start, (SUB, width))
    start = at_row_start((SUB, width), rows)
    total = ext.shape[0]
    for k in range(lag):
        near = pltpu.roll(ext[total - lag * SUB + k * SUB : total - lag * SUB + (k + 1) * SUB, :], 1, 0)
        ext[k * SUB : (k + 1) * SUB, :] = jnp.where(start, xhat_rim[k] * mask, near)


def rim_tiles(rim, spread):
    rows, lag, _ = rim.shape
    parts = SUB // rows
    spread[...] = jnp.zeros_like(spread)
    for k in range(lag):
        for r in range(rows):
            spread[k, r * parts : r * parts + 1, :] = rim[r, k : k + 1, :]
    return [spread[k] for k in range(lag)]


def gates_kernel(stage, scalars, ins, outs, extra, scratch):
    (first_len,) = scalars
    tokens, rim, gain_one, conv_weight, w_z, bias_z, w_h, cotangent = ins
    x_out, conv_out, keep_out, drive_out, cand_out, gate_out, pass_out, subk, subs, totals, up_out = outs
    ext, spread = scratch
    rows, group_len, width = tokens.shape
    count, lag = rows * group_len, rim.shape[1]
    hidden = w_z.shape[1]
    seq_start = lax.axis_index("seq") * group_len
    order = segment_order(count)
    stage.need(0)
    x = dot(order, tokens[...].reshape(count, width))
    x_out[...] = x.astype(BF16)
    stage.done(0)
    stage.need(1, 2, 3)
    normed = x * rms(x) * gain_one[...]
    ext[lag * SUB :, :] = normed
    rim_x = rim_tiles(rim, spread)
    fill_extended(ext, rim, first_len, seq_start, [v * rms(v) * gain_one[...] for v in rim_x])
    mixed = jnp.zeros((count, width), F32)
    for j in range(lag + 1):
        begin = (lag - j) * SUB
        mixed = mixed + conv_weight[j : j + 1, :] * ext[begin : begin + count, :]
    conv_out[...] = mixed.astype(BF16)
    stage.done(1)
    stage.need(4, 5, 6)
    mask = opened(first_len, seq_start, (SUB, hidden))
    block = 256
    for b in range(hidden // block):
        cols = slice(b * block, (b + 1) * block)
        g = dot(conv_out[...], w_z[:, cols]) + bias_z[:, cols]
        c = dot(conv_out[...], w_h[:, cols])
        small = jnp.exp(-jnp.abs(g))
        large = 1.0 / (1.0 + small)
        small = small * large
        zeta = jnp.where(g >= 0, large, small)
        sig = 1.0 / (1.0 + jnp.exp(-c))
        cand = jnp.where(c >= 0, c + 0.5, sig)
        keep_out[:, cols] = jnp.where(g >= 0, small, large)
        keep_out[0:SUB, cols] = keep_out[0:SUB, cols] * mask[:, cols]
        drive_out[:, cols] = zeta * cand
        cand_out[:, cols] = cand
        gate_out[:, cols] = (small * large).astype(BF16)
        pass_out[:, cols] = (zeta * jnp.where(c >= 0, 1.0, sig * (1.0 - sig))).astype(BF16)
        for i in (2, 3, 4, 5, 6):
            stage.send(outs[i].at[:, pl.ds(b * block, block)], stage.targets[i].at[:, pl.ds(b * block, block)])

    def step(i, carry):
        total, state = carry
        at = pl.ds(pl.multiple_of(i * SUB, SUB), SUB)
        keep = keep_out[at, :]
        return total * keep, keep * state + drive_out[at, :]

    total, state = lax.fori_loop(
        0, count // SUB, step, (jnp.ones((SUB, hidden), F32), jnp.zeros((SUB, hidden), F32)), unroll=8
    )
    subk[...] = total
    subs[...] = state
    parts = SUB // rows
    for r in range(rows):
        at = slice(r * parts, r * parts + 1)
        k, s = subk[at, :], subs[at, :]
        for h in range(1, parts):
            at = slice(r * parts + h, r * parts + h + 1)
            s = subs[at, :] + subk[at, :] * s
            k = k * subk[at, :]
        totals[0, r : r + 1, :] = k
        totals[1, r : r + 1, :] = s
    stage.done(7, 8, 9)
    stage.need(7)
    up_out[...] = dot(order, cotangent[...].reshape(count, width)).astype(BF16)
    stage.done(10)


def give_pair(stage, even, pairs):
    found = []
    for one, two, mine, other in pairs:
        found.append((stage.copy(one, mine), stage.copy(two, other), one, two, mine, other, stage.next))

    @pl.when(even)
    def _():
        for first, second, *_ in found:
            first.start()
            second.start()

    @pl.when(jnp.logical_not(even))
    def _():
        for _, _, one, two, mine, other, at in found:
            pltpu.make_async_copy(two, mine, stage.sems.at[at - 2]).start()
            pltpu.make_async_copy(one, other, stage.sems.at[at - 1]).start()

    for first, second, *_ in found:
        stage.pending += [first, second]


def mlp_blocks(pre_in, up, w_up, w_down, tail, second_grad, for_even, for_odd):
    block = pre_in.shape[1]

    def part(b, carry):
        at = pl.ds(pl.multiple_of(b * block, block), block)
        pre = dot(pre_in[...], w_up[:, at])
        back = dot_rt(up[...], w_down[at, :])
        scaled = pre * 0.7071067811865476
        phi = 0.5 + 0.5 * lax.erf(scaled)
        active = (pre * phi).astype(BF16)
        slope = phi + pre * (0.3989422804014327 * jnp.exp(-scaled * scaled))
        up_low = (slope * back).astype(BF16)
        for_even[at, :] = dot_lt(active, up[...])
        for_odd[at, :] = dot_lt(pre_in[...], up_low)
        tail[...] += dot(active, w_down[at, :])
        second_grad[...] += dot_rt(up_low, w_up[:, at])
        return carry

    lax.fori_loop(0, w_down.shape[0] // block, part, 0, unroll=UNROLL)


def state_kernel(stage, scalars, ins, outs, extra, scratch):
    (first_len,) = scalars
    carried, subk, subs, keep, drive, cand, gate, x, w_out, gain_two, w_up, w_down, up = ins
    blend, low, middle_ref, second_low, tail, second_grad = outs
    mine, other = extra
    before, for_even, for_odd = scratch
    count, width = x.shape
    hidden = keep.shape[1]
    rows = carried.shape[0]
    parts = SUB // rows
    pairs = count // SUB // 2
    seq_start = lax.axis_index("seq") * (count // rows)
    even = lax.axis_index("row") % 2 == 0
    stage.need(0, 1, 2)
    for r in range(rows):
        s = carried[r : r + 1, :]
        before[r * parts : r * parts + 1, :] = s
        for h in range(1, parts):
            at = slice(r * parts + h - 1, r * parts + h)
            s = subs[at, :] + subk[at, :] * s
            before[r * parts + h : r * parts + h + 1, :] = s

    def two(i, state):
        at = pl.ds(pl.multiple_of(i * 2 * SUB, 2 * SUB), 2 * SUB)
        k, d, c, g = keep[at, :], drive[at, :], cand[at, :], gate[at, :].astype(F32)
        first = k[:SUB] * state + d[:SUB]
        second = k[SUB:] * first + d[SUB:]
        low[at, :] = jnp.concatenate([first, second], axis=0).astype(BF16)
        earlier = jnp.concatenate([state, first], axis=0)
        blend[at, :] = ((c - earlier) * g).astype(BF16)
        return second

    state = before[...] * opened(first_len, seq_start, (SUB, hidden))
    for c in range(CHUNKS):
        stage.need_chunk(c, 3, 4, 5, 6)
        state = lax.fori_loop(c * pairs // CHUNKS, (c + 1) * pairs // CHUNKS, two, state, unroll=2)
    stage.done(0, 1)
    stage.need(7, 8, 9)
    middle = x[...].astype(F32) + dot(low[...], w_out[...])
    middle_ref[...] = middle
    second_low[...] = (middle * rms(middle) * gain_two[...]).astype(BF16)
    stage.done(2, 3)
    tail[...] = jnp.zeros_like(tail)
    second_grad[...] = jnp.zeros_like(second_grad)
    stage.need(10, 11, 12)
    mlp_blocks(second_low, up, w_up, w_down, tail, second_grad, for_even, for_odd)
    stage.done(4, 5)
    give_pair(stage, even, [(for_even, for_odd, mine, other)])


def mlp_kernel(stage, scalars, ins, outs, extra, scratch):
    second_low, up, w_up, w_down, tail, second_grad, middle_ref, gain_two, w_out, low, keep, subk = ins
    output, grad_middle_out, grad_gain_two, grad_state, subb, totals = outs
    mine, other, mine_out, other_out = extra
    for_even, for_odd, out_even, out_odd = scratch
    count, width = middle_ref.shape
    hidden = keep.shape[1]
    rows = totals.shape[0]
    parts = SUB // rows
    pairs = count // SUB // 2
    even = lax.axis_index("row") % 2 == 0
    stage.need(0, 1, 2, 3, 4, 5)
    mlp_blocks(second_low, up, w_up, w_down, tail, second_grad, for_even, for_odd)
    give_pair(stage, even, [(for_even, for_odd, mine, other)])
    stage.need(6, 7, 8)
    middle = middle_ref[...]
    scale = rms(middle)
    unit = middle * scale
    grad = second_grad[...]
    grad_gain_two[...] = jnp.sum(grad * unit, axis=0, keepdims=True)
    grad = grad * gain_two[...]
    grad_middle = up[...].astype(F32) + scale * (grad - unit * jnp.mean(grad * unit, axis=-1, keepdims=True))
    grad_middle_out[...] = grad_middle
    stage.done(1, 2)
    middle_low = grad_middle.astype(BF16)
    grad_state[...] = dot_rt(middle_low, w_out[...])
    stage.done(3)
    stage.need(9, 10, 11)

    def back_step(i, passed):
        at = pl.ds(pl.multiple_of((2 * pairs - 1 - i) * SUB, SUB), SUB)
        return keep[at, :] * (grad_state[at, :] + passed)

    subb[...] = lax.fori_loop(0, 2 * pairs, back_step, jnp.zeros((SUB, hidden), F32), unroll=8)
    for r in range(rows):
        end = r * parts + parts - 1
        b = subb[end : end + 1, :]
        for h in range(parts - 2, -1, -1):
            at = slice(r * parts + h, r * parts + h + 1)
            b = subb[at, :] + subk[at, :] * b
        totals[r : r + 1, :] = b
    stage.done(4, 5)
    half_h = hidden // 2
    out_even[...] = dot_lt(low[:, :half_h], middle_low)
    out_odd[...] = dot_lt(low[:, half_h:], middle_low)
    give_pair(stage, even, [(out_even, out_odd, mine_out, other_out)])
    result = (middle_ref[...] + tail[...]).astype(BF16)
    output[...] = dot_lt(segment_order(count), result).astype(BF16).reshape(output.shape)
    stage.done(0)


def first_kernel(stage, scalars, ins, outs, extra, scratch):
    (first_len,) = scalars
    (returned, subk, subb, keep, grad_state, blend, passing, conv_low, w_z, w_h, x_ref, rim, gain_one, conv_weight,
     grad_middle, grad_gain_two) = ins
    grad_tokens, sent, tail_normed, tail_middle = outs
    mine, other = extra
    incoming, gate_low, cand_low, ext, spread, grad_ext, bias_sum, small, for_even, for_odd, rest = scratch
    count, width = x_ref.shape
    hidden = keep.shape[1]
    rows, lag = rim.shape[0], rim.shape[1]
    parts = SUB // rows
    pairs = count // SUB // 2
    seq_start = lax.axis_index("seq") * (count // rows)
    even = lax.axis_index("row") % 2 == 0
    stage.need(0, 1, 2)
    for r in range(rows):
        b = returned[r : r + 1, :]
        incoming[r * parts + parts - 1 : (r + 1) * parts, :] = b
        for h in range(parts - 2, -1, -1):
            at = slice(r * parts + h + 1, r * parts + h + 2)
            b = subb[at, :] + subk[at, :] * b
            incoming[r * parts + h : r * parts + h + 1, :] = b

    def two(i, carry):
        passed, bias = carry
        at = pl.ds(pl.multiple_of((pairs - 1 - i) * 2 * SUB, 2 * SUB), 2 * SUB)
        k, g = keep[at, :], grad_state[at, :]
        late = g[SUB:] + passed
        early = g[:SUB] + k[SUB:] * late
        adjoint = jnp.concatenate([early, late], axis=0)
        grad_g = adjoint * blend[at, :].astype(F32)
        gate_low[at, :] = grad_g.astype(BF16)
        cand_low[at, :] = (adjoint * passing[at, :].astype(F32)).astype(BF16)
        return k[:SUB] * early, bias + grad_g[:SUB] + grad_g[SUB:]

    carry = (incoming[...], jnp.zeros((SUB, hidden), F32))
    for c in range(CHUNKS):
        stage.need_chunk(CHUNKS - 1 - c, 3, 4, 5, 6)
        carry = lax.fori_loop(c * pairs // CHUNKS, (c + 1) * pairs // CHUNKS, two, carry, unroll=2)
    bias = carry[1]
    bias_sum[...] = jnp.sum(bias, axis=0, keepdims=True)
    stage.need(7)
    for_even[...] = dot_lt(conv_low[...], gate_low[...])
    for_odd[...] = dot_lt(conv_low[...], cand_low[...])
    cols = pl.ds(0, hidden)
    give_pair(stage, even, [(for_even, for_odd, mine.at[:, cols], other.at[:, cols])])
    stage.need(8, 9, 10, 11, 12, 13, 14, 15)
    grad_mixed = dot_rt(gate_low[...], w_z[...]) + dot_rt(cand_low[...], w_h[...])

    x = x_ref[...].astype(F32)
    scale = rms(x)
    unit = x * scale
    gain = gain_one[...]
    ext[lag * SUB :, :] = unit * gain
    rim_x = rim_tiles(rim, spread)
    rim_unit = [v * rms(v) for v in rim_x]
    fill_extended(ext, rim, first_len, seq_start, [v * gain for v in rim_unit])
    small[0:1, :] = jnp.zeros((1, width), F32)
    for j in range(lag + 1):
        begin = (lag - j) * SUB
        small[1 + j : 2 + j, :] = jnp.sum(grad_mixed * ext[begin : begin + count, :], axis=0, keepdims=True)
    for j in range(hidden // width):
        at = 2 + lag + j
        small[at : at + 1, :] = bias_sum[:, j * width : (j + 1) * width]
    last = 2 + lag + hidden // width
    small[last : last + 1, :] = grad_gain_two[...]
    grad_ext[...] = jnp.zeros_like(grad_ext)
    for j in range(lag + 1):
        begin = (lag - j) * SUB
        grad_ext[begin : begin + count, :] += conv_weight[j : j + 1, :] * grad_mixed
    mask = opened(first_len, seq_start, (SUB, width))
    start = at_row_start((SUB, width), rows)
    end = at_row_end((SUB, width), rows)
    grad_gain = jnp.zeros((SUB, width), F32)
    for k in range(lag):
        head = grad_ext[k * SUB : (k + 1) * SUB, :]
        tail_at = pl.ds(count + k * SUB, SUB)
        near = pltpu.roll(head, SUB - 1, 0)
        grad_ext[tail_at, :] = grad_ext[tail_at, :] + jnp.where(end, 0.0, near)
        to_rim = jnp.where(start, head * mask, 0.0)
        grad_gain = grad_gain + to_rim * rim_unit[k]
        spread[k] = to_rim
        for r in range(rows):
            sent[r, k : k + 1, :] = spread[k, r * parts : r * parts + 1, :]
    grad_normed = grad_ext[lag * SUB :, :]
    small[0:1, :] = jnp.sum(grad_normed * unit, axis=0, keepdims=True) + jnp.sum(
        grad_gain, axis=0, keepdims=True
    )
    rest[...] = jnp.zeros_like(rest)
    for j in range(width // 128):
        rest[j * SUB : (j + 1) * SUB, :] = small[:, j * 128 : (j + 1) * 128]
    past = pl.ds(hidden, 128)
    give_pair(stage, even, [(rest, rest, mine.at[:, past], other.at[:, past])])
    for k in range(lag):
        at = count - lag * SUB + k * SUB
        for r in range(rows):
            row = at + r * parts + parts - 1
            to = tail_normed.shape[1] - lag + k
            tail_normed[r, to : to + 1, :] = grad_ext[lag * SUB + row : lag * SUB + row + 1, :]
            tail_middle[r, to : to + 1, :] = grad_middle[row : row + 1, :]
    grad = grad_normed * gain
    grad_x = grad_middle[...] + scale * (grad - unit * jnp.mean(grad * unit, axis=-1, keepdims=True))
    stage.done(1, 2, 3)
    order = segment_order(count)
    grad_tokens[...] = dot_lt(order, grad_x.astype(BF16)).astype(BF16).reshape(grad_tokens.shape)
    stage.done(0)


def tail_kernel(tokens, tail_normed, tail_middle, received, gain_one, _, grad_tokens, spread):
    rows, tile, width = tokens.shape
    lag = received.shape[1]
    for r in range(rows):
        spread[tile - lag :, :] = tail_normed[r, tile - lag :, :] + received[r]
        x = tokens[r].astype(F32)
        scale = rms(x)
        unit = x * scale
        grad = spread[...] * gain_one[...]
        fixed = tail_middle[r] + scale * (grad - unit * jnp.mean(grad * unit, axis=-1, keepdims=True))
        changed = lax.broadcasted_iota(jnp.int32, (tile, width), 0) >= tile - lag
        grad_tokens[r] = jnp.where(changed, fixed, _[r].astype(F32)).astype(BF16)


def shaped(*shapes):
    return tuple(jax.ShapeDtypeStruct(shape, kind) for shape, kind in shapes)


def swapped(array, axis, bit):
    return lax.ppermute(array, axis, [(i, i ^ bit) for i in range(lax.axis_size(axis))])


def bits_of(axis):
    bit, result = 1, []
    while bit < lax.axis_size(axis):
        result.append(bit)
        bit *= 2
    return result


def upper(axis, bit):
    return (lax.axis_index(axis) // bit) % 2 == 1


def carry_forward(totals):
    keep, state = totals[0], totals[1]
    before_k, before_s = jnp.ones_like(keep), jnp.zeros_like(state)
    levels = []
    for bit in bits_of("seq"):
        other = swapped(jnp.stack([keep, state]), "seq", bit)
        other_k, other_s = other[0], other[1]
        late = upper("seq", bit)
        levels.append((keep, other_k))
        before_s = jnp.where(late, before_s + before_k * other_s, before_s)
        before_k = jnp.where(late, before_k * other_k, before_k)
        state = jnp.where(late, state + keep * other_s, other_s + other_k * state)
        keep = keep * other_k
    return before_s, levels


def carry_backward(passed, levels, between):
    after_b, after_k = jnp.zeros_like(passed), jnp.ones_like(passed)
    for i, (bit, (keep, other_k)) in enumerate(zip(bits_of("seq"), levels)):
        if i == HOLD:
            passed = between(passed)
        other_b = swapped(passed, "seq", bit)
        late = upper("seq", bit)
        after_b = jnp.where(late, after_b, after_b + after_k * other_b)
        after_k = jnp.where(late, after_k, after_k * other_k)
        passed = jnp.where(late, other_b + other_k * passed, passed + keep * other_b)
    return after_b


BOTH = ("row", "seq")


def axis_steps(order):
    seq = [("seq", bit) for bit in bits_of("seq")]
    parts = {"x": seq[:1], "y": [("row", bit) for bit in bits_of("row")[1:]], "a": seq[1:2], "b": seq[2:]}
    swap = {"x": "y", "y": "x", "a": "a", "b": "b"}
    even = sum((parts[letter] for letter in order), [])
    odd = sum((parts[swap[letter]] for letter in order), [])
    return list(zip(even, odd))


def exchanged(array, even, odd):
    rows, devices = lax.axis_size("row"), lax.axis_size("seq")
    pairs = []
    for r in range(rows):
        for s in range(devices):
            axis, bit = odd if r & 1 else even
            to = ((r ^ bit) * devices + s) if axis == "row" else (r * devices + (s ^ bit))
            pairs.append((r * devices + s, to))
    return lax.ppermute(array, BOTH, pairs)


def place_bit(step):
    even, odd = [lax.axis_index(axis) // bit % 2 for axis, bit in step]
    return jnp.where(lax.axis_index("row") % 2 == 0, even, odd)


def by_rows(total, body):
    chunk = next((c for c in (64, 32, 16, 8) if total % c == 0), total)
    if chunk == total:
        body(0, chunk)
        return

    def turn(i, carry):
        body(pl.multiple_of(i * chunk, chunk), chunk)
        return carry

    lax.fori_loop(0, total // chunk, turn, 0)


def tiled(first, rows):
    return pl.multiple_of(first, SUB) if rows % SUB == 0 else first


def split_rows(step, mine, received, send, keep):
    half, bit = send.shape[0], place_bit(step)
    if half % SUB:
        first = mine[:half, :] + received[:half, :]
        second = mine[half:, :] + received[half:, :]
        lower = jnp.broadcast_to(bit == 0, first.shape)
        send[...] = jnp.where(lower, second, first)
        keep[...] = jnp.where(lower, first, second)
        return

    def body(i, chunk):
        to = pl.ds(i, chunk)
        for out, begin in ((send, (1 - bit) * half), (keep, bit * half)):
            at = pl.ds(pl.multiple_of(i + begin, SUB), chunk)
            out[to, :] = mine[at, :] + received[at, :]

    by_rows(half, body)


def add_rows(_, mine, received, out):
    def body(i, chunk):
        at = pl.ds(i, chunk)
        out[at, :] = mine[at, :] + received[at, :]

    by_rows(mine.shape[0], body)


def join_rows(step, mine, received, out):
    half, bit = mine.shape[0], place_bit(step)
    if half % SUB:
        lower = jnp.broadcast_to(bit == 0, mine.shape)
        out[:half, :] = jnp.where(lower, mine[...], received[...])
        out[half:, :] = jnp.where(lower, received[...], mine[...])
        return

    def body(i, chunk):
        at = pl.ds(i, chunk)
        for source, begin in ((mine, bit * half), (received, (1 - bit) * half)):
            out[pl.ds(pl.multiple_of(i + begin, SUB), chunk), :] = source[at, :]

    by_rows(half, body)


CORE = (("row", 1),) * 2


class Summed:
    def __init__(self, mine, other, order):
        self.steps = axis_steps(order)
        self.mine, self.stage = mine, 1
        self.received = exchanged(other, *CORE)

    def work(self):
        count = len(self.steps)
        rows, width = self.mine.shape
        if self.stage <= count:
            return split_rows, self.steps[self.stage - 1], [(rows // 2, width)] * 2
        if self.stage == count + 1:
            return add_rows, None, [(rows, width)]
        return join_rows, self.steps[2 * count + 1 - self.stage], [(2 * rows, width)]

    def give(self, outs):
        count = len(self.steps)
        self.mine = outs[-1]
        step = self.steps[self.stage - 1 if self.stage <= count else 2 * count - self.stage]
        self.received = exchanged(outs[0], *step)
        self.stage += 1

    def busy(self):
        return self.stage <= 2 * len(self.steps)

    def across(self):
        self.others = exchanged(self.mine, *CORE), exchanged(self.received, *CORE)


def wave(tokens, sums, through=()):
    works = [one.work() for one in sums]

    def kernel(*refs):
        refs = refs[len(tokens) + len(through) :]
        ins, outs = refs[: 2 * len(sums)], list(refs[2 * len(sums) + len(through) :])
        for i, (rows, step, shapes) in enumerate(works):
            mine_outs = [outs.pop(0) for _ in shapes]
            rows(step, ins[2 * i], ins[2 * i + 1], *mine_outs)

    shapes = [shape for _, _, shapes in works for shape in shapes]
    outs = list(pl.pallas_call(
        kernel,
        in_specs=[ANY] * (len(tokens) + len(through)) + [VMEM] * (2 * len(sums)),
        out_specs=(ANY,) * len(through) + (VMEM,) * len(shapes),
        out_shape=shaped(*[(array.shape, F32) for array in through], *[(shape, F32) for shape in shapes]),
        input_output_aliases={len(tokens) + i: i for i in range(len(through))},
        compiler_params=pltpu.CompilerParams(vmem_limit_bytes=WAVE << 20),
        cost_estimate=pl.CostEstimate(flops=1, bytes_accessed=1, transcendentals=0),
    )(*tokens, *through, *[array for one in sums for array in (one.mine, one.received)]))
    passed = [outs.pop(0) for _ in through]
    first = outs[0]
    for one, (_, _, shapes) in zip(sums, works):
        one.give([outs.pop(0) for _ in shapes])
    return first, passed


def finish_kernel(steps, routes, total, few, _, *refs):
    count = len(steps)
    arrays, outs = refs[: 4 * count], refs[4 * count : 4 * count + total]
    buffers, sems = refs[4 * count + total : 5 * count + total], refs[-1]
    even = lax.axis_index("row") % 2 == 0
    base, plans = 0, []
    for k, step in enumerate(steps):
        own = arrays[4 * k : 4 * k + 4]
        rows = own[0].shape[0]
        for parity in range(2):
            axis, bit = step[parity]
            place = lax.axis_index(axis) // bit % 2
            longest = 0
            for is_own in (True, False):
                for upper_half in range(2):
                    pair = own[:2] if is_own else own[2:]
                    plan = []
                    for half in range(2):
                        source = pair[half ^ upper_half]
                        buffer = buffers[k].at[parity, half]
                        for at, columns, output, to in routes(k, parity, half * rows, rows):
                            plan.append((source.at[at, columns], buffer.at[at, columns], outs[output].at[to]))
                    mine = even if is_own == (parity == 0) else jnp.logical_not(even)
                    plans.append((jnp.logical_and(mine, place == upper_half), plan, base))
                    longest = max(longest, len(plan))
            base += longest
    for condition, plan, first in plans:

        @pl.when(condition)
        def _():
            for i, (source, buffer, _) in enumerate(plan):
                pltpu.make_async_copy(source, buffer, sems.at[0, first + i]).start()

    for condition, plan, first in plans:

        @pl.when(condition)
        def _():
            for i, (source, buffer, target) in enumerate(plan):
                pltpu.make_async_copy(source, buffer, sems.at[0, first + i]).wait()
                pltpu.make_async_copy(buffer, target, sems.at[1, first + i]).start()

    for condition, plan, first in plans:

        @pl.when(condition)
        def _():
            for i, (source, buffer, target) in enumerate(plan):
                pltpu.make_async_copy(buffer, target, sems.at[1, first + i]).wait()

    if few:
        spread_small(outs[2:], refs[5 * count + total :])


def spread_small(outs, scratch):
    packed, *targets = outs
    tiles, *rows, sems = scratch
    copy = pltpu.make_async_copy(packed, tiles, sems.at[0, 0])
    copy.start()
    copy.wait()
    width = targets[0].shape[1]
    line = 0
    for row in rows:
        for r in range(row.shape[0]):
            for j in range(row.shape[1] // 128):
                at = (line + j * 128 // width, j * 128 % width // 128)
                source = at[1] * SUB + at[0]
                row[r : r + 1, j * 128 : (j + 1) * 128] = tiles[source : source + 1, :]
            line += row.shape[1] // width
    copies = [pltpu.make_async_copy(row, out, sems.at[1, i]) for i, (row, out) in enumerate(zip(rows, targets))]
    for copy in copies:
        copy.start()
    for copy in copies:
        copy.wait()


def finish_call(routes, token, sums, outs, few=0):
    arrays = [array for one in sums for array in (one.mine, one.received, *one.others)]
    return pl.pallas_call(
        functools.partial(finish_kernel, [one.steps[0] for one in sums], routes, len(outs), few),
        in_specs=[pl.BlockSpec(memory_space=pl.ANY)] * (1 + len(arrays)),
        out_specs=(HBM,) * len(outs),
        out_shape=shaped(*outs),
        scratch_shapes=[pltpu.VMEM((2, 2) + one.mine.shape, F32) for one in sums]
        + ([pltpu.VMEM(*out) for out in outs[2:]] if few else [])
        + [pltpu.SemaphoreType.DMA((2, 48))],
        compiler_params=pltpu.CompilerParams(vmem_limit_bytes=FINISH << 20),
        cost_estimate=pl.CostEstimate(flops=1, bytes_accessed=1, transcendentals=0),
    )(token, *arrays)


def cut(first, rows, marks):
    inside = [first] + [m for m in marks if first < m < first + rows] + [first + rows]
    return [(a - first, a, b - a) for a, b in zip(inside, inside[1:])]


def per_device(
    tokens, first_len, gain_one, conv_weight, w_z, bias_z, w_h, w_out, gain_two, w_up, w_down, cotangent
):
    rows, group_len, width = tokens.shape
    hidden, ff = w_z.shape[1], w_up.shape[1]
    lag = conv_weight.shape[0] - 1
    count = rows * group_len
    devices = lax.axis_size("seq")
    gain_one, gain_two, bias_z = gain_one[None], gain_two[None], bias_z[None]
    rim = lax.ppermute(
        tokens[:, group_len - lag :].astype(F32), "seq", [(i, i + 1) for i in range(devices - 1)]
    )
    th, tw = (count, hidden), (count, width)
    chunks = {3: CHUNKS, 4: CHUNKS, 5: CHUNKS, 6: CHUNKS}
    x, conv_low, keep, drive, cand, gate, passing, subk, subs, totals, up = staged_call(
        gates_kernel,
        [first_len],
        [tokens, rim, gain_one, conv_weight, w_z, bias_z, w_h, cotangent],
        [(tw, BF16), (tw, BF16), (th, F32), (th, F32), (th, F32), (th, BF16), (th, BF16),
         ((SUB, hidden), F32), ((SUB, hidden), F32), ((2, rows, hidden), F32), (tw, BF16)],
        [],
        [((count + lag * SUB, width), F32), ((lag, SUB, width), F32)],
        4 * count * width * hidden,
        64,
        56,
    )
    carried, levels = carry_forward(totals)
    half_ff = ff // 2
    mlp_pair, out_pair = ((half_ff, width), F32), ((hidden // 2, width), F32)
    low_half, high_half, every = pl.ds(0, half_ff), pl.ds(half_ff, half_ff), pl.ds(0, width)
    blend, low, middle, second_low, tail, second_grad, mine_a, other_a = staged_call(
        state_kernel,
        [first_len],
        [carried, subk, subs, keep, drive, cand, gate, x, w_out, gain_two, (w_up, (every, low_half)),
         (w_down, (low_half, every)), up],
        [(th, BF16), (th, BF16), (tw, F32), (tw, BF16), (tw, F32), (tw, F32)],
        [mlp_pair, mlp_pair],
        [((SUB, hidden), F32), ((half_ff, width), F32), ((half_ff, width), F32)],
        6 * count * width * ff,
        64,
        56,
        chunks,
    )
    output, grad_middle, grad_gain_two, grad_state, subb, passed, mine_b, other_b, mine_c, other_c = staged_call(
        mlp_kernel,
        [],
        [second_low, up, (w_up, (every, high_half)), (w_down, (high_half, every)), tail, second_grad, middle, gain_two,
         w_out, low, keep, subk],
        [(tokens.shape, BF16), (tw, F32), ((1, width), F32), (th, F32), ((SUB, hidden), F32), ((rows, hidden), F32)],
        [mlp_pair, mlp_pair, out_pair, out_pair],
        [((half_ff, width), F32)] * 2 + [((hidden // 2, width), F32)] * 2,
        8 * count * width * ff,
        64,
        56,
    )
    first = Summed(mine_a, other_a, ORDERS[0])
    early = [Summed(mine_b, other_b, ORDERS[1]), Summed(mine_c, other_c, ORDERS[2])]

    def between(passed):
        return wave([], [first], [passed])[1][0]

    returned = carry_backward(passed, levels, between)
    token, (returned,) = wave([], [first] + early, [returned])
    tile = 16
    pair = ((width, hidden + 128), F32)
    grad_tokens, sent, tail_normed, tail_middle, mine_d, other_d = staged_call(
        first_kernel,
        [first_len],
        [returned, subk, subb, keep, grad_state, blend, passing, conv_low, w_z, w_h, x, rim, gain_one,
         conv_weight, grad_middle, grad_gain_two],
        [(tokens.shape, BF16), ((rows, lag, width), F32)] + [((rows, tile, width), F32)] * 2,
        [pair, pair],
        [((SUB, hidden), F32), (th, BF16), (th, BF16), ((count + lag * SUB, width), F32),
         ((lag, SUB, width), F32), ((count + lag * SUB, width), F32), ((1, hidden), F32), ((SUB, width), F32),
         ((width, hidden), F32), ((width, hidden), F32), ((width, 128), F32)],
        8 * count * width * hidden,
        64,
        LAST,
        chunks,
    )
    received = lax.ppermute(sent, "seq", [(i + 1, i) for i in range(devices - 1)])
    at_tail = pl.BlockSpec((rows, tile, width), lambda i: (0, group_len // tile - 1, 0))
    whole = lambda *shape: pl.BlockSpec(shape, lambda i: (0,) * len(shape))
    grad_tokens = pl.pallas_call(
        tail_kernel,
        grid=(1,),
        in_specs=[at_tail, whole(rows, tile, width), whole(rows, tile, width), whole(rows, lag, width),
                  whole(1, width), at_tail],
        out_specs=at_tail,
        out_shape=jax.ShapeDtypeStruct(tokens.shape, BF16),
        scratch_shapes=[pltpu.VMEM((tile, width), F32)],
        input_output_aliases={5: 0},
    )(tokens, tail_normed, tail_middle, received, gain_one, grad_tokens)
    late = Summed(mine_d, other_d, ORDERS[3])
    tokens = [[tail_normed]] + [[]] * (TAIL - 3) + [[grad_tokens]]
    left = [[first], early]
    while late.busy():
        more = tokens.pop(0) if tokens else []
        ended = [] if not left or left[0][0].busy() else left.pop(0)
        running = sum(left, []) + [late]
        token, ready = wave([token, *more], running, [one.received for one in ended])
        for one, received in zip(ended, ready):
            one.received = received
            one.across()
    def mlp_routes(k, parity, first, rows):
        everything, plan = pl.ds(0, width), []
        first = first + k * half_ff
        if k == 2:
            first = first - ff
            return [(pl.ds(0, rows), everything, 2, (pl.ds(first + parity * hidden // 2, rows), everything))]
        for offset, at, size in cut(first, rows, range(0, ff, width)):
            inner = pl.ds(offset, size)
            if parity == 0:
                plan.append((inner, everything, 0, (pl.ds(at, size), everything)))
            else:
                block = at // width * width
                plan.append((inner, everything, 1, (pl.ds(at - block, size), pl.ds(block, width))))
        return plan

    few = SUB * width // 128

    def gate_routes(k, parity, first, rows):
        inner, cols = pl.ds(0, rows), pl.ds(0, hidden)
        plan = [(inner, cols, parity, (pl.ds(first, rows), cols))]
        if parity == 0 and first < few:
            least = min(rows, few - first)
            at, all_cols = pl.ds(0, least), pl.ds(0, 128)
            plan.append((at, pl.ds(hidden, 128), 2, (pl.ds(first, least), all_cols)))
        return plan

    grad_down, grad_up, grad_out = finish_call(
        mlp_routes, token, [first, *early], [((ff, width), F32), ((width, ff), F32), ((hidden, width), F32)]
    )
    (late.received,) = held([grad_out], [late.received])
    late.across()
    grad_z, grad_h, small, grad_gain_one, grad_conv, grad_bias, grad_gain = finish_call(
        gate_routes, grad_out, [late],
        [((width, hidden), F32), ((width, hidden), F32), ((SUB * width // 128, 128), F32), ((1, width), F32),
         ((lag + 1, width), F32), ((1, hidden), F32), ((1, width), F32)],
        few,
    )
    return (
        output,
        grad_tokens,
        grad_gain_one.reshape(width),
        grad_conv,
        grad_z,
        grad_bias.reshape(hidden),
        grad_h,
        grad_out,
        grad_gain.reshape(width),
        grad_up,
        grad_down,
    )


def held(tokens, arrays):
    return pl.pallas_call(
        lambda *_: None,
        in_specs=[ANY] * (len(tokens) + len(arrays)),
        out_specs=(ANY,) * len(arrays),
        out_shape=shaped(*[(array.shape, F32) for array in arrays]),
        input_output_aliases={len(tokens) + i: i for i in range(len(arrays))},
    )(*tokens, *arrays)


def solution(mesh):
    block, copied = P("row", "seq", None), P()
    return jax.shard_map(
        per_device,
        mesh=mesh,
        in_specs=(block, P("row")) + (copied,) * 9 + (block,),
        out_specs=(block, block) + (copied,) * 9,
        check_vma=False,
    )
```

```python
import functools

import jax
import jax.numpy as jnp
from jax import lax
from jax.experimental import pallas as pl
from jax.experimental.pallas import tpu as pltpu
from jax.sharding import PartitionSpec as P

F32, BF16 = jnp.float32, jnp.bfloat16
EPS = 1e-06
VMEM = pl.BlockSpec(memory_space=pltpu.VMEM)
SMEM = pl.BlockSpec(memory_space=pltpu.SMEM)
ORDERS = ("xyab", "xyab", "abxy", "xyab")
FIRST = 3
TAIL = 5
CHUNKS = 4
FINISH = 36
HELD = 30
WAVE = 24
LAST = 30
UNROLL = 2
HOLD = 1
SUB = 8


HBM = pl.BlockSpec(memory_space=pltpu.HBM)
ANY = pl.BlockSpec(memory_space=pl.ANY)


class Staged:
    def __init__(self, sources, buffers, targets, results, sems, chunks):
        self.ins, self.pending, self.sems, self.next = {}, [], sems, 0
        self.targets, self.results = targets, results
        order = []
        for i, (source, buffer) in enumerate(zip(sources, buffers)):
            parts = chunks.get(i, 1)
            rows = source.shape[0] // parts
            self.ins[i] = []
            for c in range(parts):
                at = pl.ds(c * rows, rows)
                pair = (source, buffer) if parts == 1 else (source.at[at], buffer.at[at])
                self.ins[i].append(self.copy(*pair))
                order.append((c, self.ins[i][-1]))
        for _, copy in sorted(order, key=lambda pair: pair[0]):
            copy.start()

    def copy(self, source, target):
        self.next += 1
        return pltpu.make_async_copy(source, target, self.sems.at[self.next - 1])

    def need(self, *indices):
        for i in indices:
            for copy in self.ins[i]:
                copy.wait()

    def need_chunk(self, c, *indices):
        for i in indices:
            self.ins[i][c].wait()

    def done(self, *indices):
        for i in indices:
            copy = self.copy(self.results[i], self.targets[i])
            copy.start()
            self.pending.append(copy)

    def send(self, source, target):
        copy = self.copy(source, target)
        copy.start()
        self.pending.append(copy)

    def finish(self):
        for copy in self.pending:
            copy.wait()


def staged_call(kernel, scalars, ins, outs, extra_outs, scratch, flops, copies, room, chunks=None):
    views = [one[1] if isinstance(one, tuple) else None for one in ins]
    ins = [one[0] if isinstance(one, tuple) else one for one in ins]
    inside = [one.shape if view is None else tuple(at.size for at in view) for one, view in zip(ins, views)]
    n_s, n_i, n_o, n_e = len(scalars), len(ins), len(outs), len(extra_outs)

    def body(*refs):
        cut = [0]
        for size in (n_s, n_i, n_o, n_e, n_i, n_o, len(scratch)):
            cut.append(cut[-1] + size)
        scalar, source, target, extra, buffer, result, own = [refs[a:b] for a, b in zip(cut, cut[1:])]
        source = [ref if view is None else ref.at[view] for ref, view in zip(source, views)]
        stage = Staged(source, buffer, target, result, refs[-1], chunks or {})
        kernel(stage, scalar, buffer, result, extra, own)
        stage.finish()

    results = pl.pallas_call(
        body,
        in_specs=[SMEM] * n_s + [HBM] * n_i,
        out_specs=(HBM,) * (n_o + n_e),
        out_shape=shaped(*outs, *extra_outs),
        scratch_shapes=[pltpu.VMEM(shape, a.dtype) for shape, a in zip(inside, ins)]
        + [pltpu.VMEM(shape, kind) for shape, kind in outs]
        + [pltpu.VMEM(shape, kind) for shape, kind in scratch]
        + [pltpu.SemaphoreType.DMA((copies,))],
        compiler_params=pltpu.CompilerParams(vmem_limit_bytes=room << 20),
        cost_estimate=pl.CostEstimate(flops=flops, bytes_accessed=8 << 20, transcendentals=0),
    )(*scalars, *ins)
    return results


def dot(left, right):
    return jnp.dot(left, right, preferred_element_type=F32)


def dot_lt(left, right):
    return lax.dot_general(left, right, (((0,), (0,)), ((), ())), preferred_element_type=F32)


def dot_rt(left, right):
    return lax.dot_general(left, right, (((1,), (1,)), ((), ())), preferred_element_type=F32)


def segment_order(tokens):
    steps = tokens // SUB
    to = lax.broadcasted_iota(jnp.int32, (tokens, tokens), 0)
    source = lax.broadcasted_iota(jnp.int32, (tokens, tokens), 1)
    return jnp.where(source == (to % SUB) * steps + to // SUB, 1.0, 0.0).astype(BF16)


def opened(first_len, seq_start, shape):
    sub = lax.broadcasted_iota(jnp.int32, shape, 0)
    rows = first_len.shape[0]
    result = jnp.ones(shape, F32)
    for r in range(rows):
        factor = jnp.where(first_len[r] == seq_start, 0.0, 1.0)
        result = jnp.where(sub == r * (SUB // rows), factor, result)
    return result


def at_row_start(shape, rows):
    return lax.broadcasted_iota(jnp.int32, shape, 0) % (SUB // rows) == 0


def at_row_end(shape, rows):
    parts = SUB // rows
    return lax.broadcasted_iota(jnp.int32, shape, 0) % parts == parts - 1


def rms(values):
    return lax.rsqrt(jnp.mean(values * values, axis=-1, keepdims=True) + EPS)


def fill_extended(ext, rim, first_len, seq_start, xhat_rim):
    lag, rows = rim.shape[1], rim.shape[0]
    width = ext.shape[-1]
    mask = opened(first_len, seq_start, (SUB, width))
    start = at_row_start((SUB, width), rows)
    total = ext.shape[0]
    for k in range(lag):
        near = pltpu.roll(ext[total - lag * SUB + k * SUB : total - lag * SUB + (k + 1) * SUB, :], 1, 0)
        ext[k * SUB : (k + 1) * SUB, :] = jnp.where(start, xhat_rim[k] * mask, near)


def rim_tiles(rim, spread):
    rows, lag, _ = rim.shape
    parts = SUB // rows
    spread[...] = jnp.zeros_like(spread)
    for k in range(lag):
        for r in range(rows):
            spread[k, r * parts : r * parts + 1, :] = rim[r, k : k + 1, :]
    return [spread[k] for k in range(lag)]


def gates_kernel(stage, scalars, ins, outs, extra, scratch):
    (first_len,) = scalars
    tokens, rim, gain_one, conv_weight, w_z, bias_z, w_h, cotangent = ins
    x_out, conv_out, keep_out, drive_out, cand_out, gate_out, pass_out, subk, subs, totals, up_out = outs
    ext, spread = scratch
    rows, group_len, width = tokens.shape
    count, lag = rows * group_len, rim.shape[1]
    hidden = w_z.shape[1]
    seq_start = lax.axis_index("seq") * group_len
    order = segment_order(count)
    stage.need(0)
    x = dot(order, tokens[...].reshape(count, width))
    x_out[...] = x.astype(BF16)
    stage.done(0)
    stage.need(1, 2, 3)
    normed = x * rms(x) * gain_one[...]
    ext[lag * SUB :, :] = normed
    rim_x = rim_tiles(rim, spread)
    fill_extended(ext, rim, first_len, seq_start, [v * rms(v) * gain_one[...] for v in rim_x])
    mixed = jnp.zeros((count, width), F32)
    for j in range(lag + 1):
        begin = (lag - j) * SUB
        mixed = mixed + conv_weight[j : j + 1, :] * ext[begin : begin + count, :]
    conv_out[...] = mixed.astype(BF16)
    stage.done(1)
    stage.need(4, 5, 6)
    mask = opened(first_len, seq_start, (SUB, hidden))
    block = 256
    for b in range(hidden // block):
        cols = slice(b * block, (b + 1) * block)
        g = dot(conv_out[...], w_z[:, cols]) + bias_z[:, cols]
        c = dot(conv_out[...], w_h[:, cols])
        small = jnp.exp(-jnp.abs(g))
        large = 1.0 / (1.0 + small)
        small = small * large
        zeta = jnp.where(g >= 0, large, small)
        sig = 1.0 / (1.0 + jnp.exp(-c))
        cand = jnp.where(c >= 0, c + 0.5, sig)
        keep_out[:, cols] = jnp.where(g >= 0, small, large)
        keep_out[0:SUB, cols] = keep_out[0:SUB, cols] * mask[:, cols]
        drive_out[:, cols] = zeta * cand
        cand_out[:, cols] = cand
        gate_out[:, cols] = (small * large).astype(BF16)
        pass_out[:, cols] = (zeta * jnp.where(c >= 0, 1.0, sig * (1.0 - sig))).astype(BF16)
        for i in (2, 3, 4, 5, 6):
            stage.send(outs[i].at[:, pl.ds(b * block, block)], stage.targets[i].at[:, pl.ds(b * block, block)])

    def step(i, carry):
        total, state = carry
        at = pl.ds(pl.multiple_of(i * SUB, SUB), SUB)
        keep = keep_out[at, :]
        return total * keep, keep * state + drive_out[at, :]

    total, state = lax.fori_loop(
        0, count // SUB, step, (jnp.ones((SUB, hidden), F32), jnp.zeros((SUB, hidden), F32)), unroll=8
    )
    subk[...] = total
    subs[...] = state
    parts = SUB // rows
    for r in range(rows):
        at = slice(r * parts, r * parts + 1)
        k, s = subk[at, :], subs[at, :]
        for h in range(1, parts):
            at = slice(r * parts + h, r * parts + h + 1)
            s = subs[at, :] + subk[at, :] * s
            k = k * subk[at, :]
        totals[0, r : r + 1, :] = k
        totals[1, r : r + 1, :] = s
    stage.done(7, 8, 9)
    stage.need(7)
    up_out[...] = dot(order, cotangent[...].reshape(count, width)).astype(BF16)
    stage.done(10)


def give_pair(stage, even, pairs):
    found = []
    for one, two, mine, other in pairs:
        found.append((stage.copy(one, mine), stage.copy(two, other), one, two, mine, other, stage.next))

    @pl.when(even)
    def _():
        for first, second, *_ in found:
            first.start()
            second.start()

    @pl.when(jnp.logical_not(even))
    def _():
        for _, _, one, two, mine, other, at in found:
            pltpu.make_async_copy(two, mine, stage.sems.at[at - 2]).start()
            pltpu.make_async_copy(one, other, stage.sems.at[at - 1]).start()

    for first, second, *_ in found:
        stage.pending += [first, second]


def mlp_blocks(pre_in, up, w_up, w_down, tail, second_grad, for_even, for_odd):
    block = pre_in.shape[1]

    def part(b, carry):
        at = pl.ds(pl.multiple_of(b * block, block), block)
        pre = dot(pre_in[...], w_up[:, at])
        back = dot_rt(up[...], w_down[at, :])
        scaled = pre * 0.7071067811865476
        phi = 0.5 + 0.5 * lax.erf(scaled)
        active = (pre * phi).astype(BF16)
        slope = phi + pre * (0.3989422804014327 * jnp.exp(-scaled * scaled))
        up_low = (slope * back).astype(BF16)
        for_even[at, :] = dot_lt(active, up[...])
        for_odd[at, :] = dot_lt(pre_in[...], up_low)
        tail[...] += dot(active, w_down[at, :])
        second_grad[...] += dot_rt(up_low, w_up[:, at])
        return carry

    lax.fori_loop(0, w_down.shape[0] // block, part, 0, unroll=min(UNROLL, w_down.shape[0] // block))


def state_kernel(stage, scalars, ins, outs, extra, scratch):
    (first_len,) = scalars
    carried, subk, subs, keep, drive, cand, gate, x, w_out, gain_two, w_up, w_down, up = ins
    blend, low, middle_ref, second_low, tail, second_grad = outs
    mine, other = extra
    before, for_even, for_odd = scratch
    count, width = x.shape
    hidden = keep.shape[1]
    rows = carried.shape[0]
    parts = SUB // rows
    pairs = count // SUB // 2
    seq_start = lax.axis_index("seq") * (count // rows)
    even = lax.axis_index("row") % 2 == 0
    stage.need(0, 1, 2)
    for r in range(rows):
        s = carried[r : r + 1, :]
        before[r * parts : r * parts + 1, :] = s
        for h in range(1, parts):
            at = slice(r * parts + h - 1, r * parts + h)
            s = subs[at, :] + subk[at, :] * s
            before[r * parts + h : r * parts + h + 1, :] = s

    def two(i, state):
        at = pl.ds(pl.multiple_of(i * 2 * SUB, 2 * SUB), 2 * SUB)
        k, d, c, g = keep[at, :], drive[at, :], cand[at, :], gate[at, :].astype(F32)
        first = k[:SUB] * state + d[:SUB]
        second = k[SUB:] * first + d[SUB:]
        low[at, :] = jnp.concatenate([first, second], axis=0).astype(BF16)
        earlier = jnp.concatenate([state, first], axis=0)
        blend[at, :] = ((c - earlier) * g).astype(BF16)
        return second

    state = before[...] * opened(first_len, seq_start, (SUB, hidden))
    for c in range(CHUNKS):
        stage.need_chunk(c, 3, 4, 5, 6)
        state = lax.fori_loop(c * pairs // CHUNKS, (c + 1) * pairs // CHUNKS, two, state, unroll=2)
    stage.done(0, 1)
    stage.need(7, 8, 9)
    middle = x[...].astype(F32) + dot(low[...], w_out[...])
    middle_ref[...] = middle
    second_low[...] = (middle * rms(middle) * gain_two[...]).astype(BF16)
    stage.done(2, 3)
    tail[...] = jnp.zeros_like(tail)
    second_grad[...] = jnp.zeros_like(second_grad)
    stage.need(10, 11, 12)
    mlp_blocks(second_low, up, w_up, w_down, tail, second_grad, for_even, for_odd)
    stage.done(4, 5)
    give_pair(stage, even, [(for_even, for_odd, mine, other)])


def mlp_kernel(stage, scalars, ins, outs, extra, scratch):
    second_low, up, w_up, w_down, tail, second_grad, middle_ref, gain_two, w_out, low, keep, subk = ins
    output, grad_middle_out, grad_gain_two, grad_state, subb, totals = outs
    mine, other, mine_out, other_out = extra
    for_even, for_odd, out_even, out_odd = scratch
    count, width = middle_ref.shape
    hidden = keep.shape[1]
    rows = totals.shape[0]
    parts = SUB // rows
    pairs = count // SUB // 2
    even = lax.axis_index("row") % 2 == 0
    stage.need(0, 1, 2, 3, 4, 5)
    mlp_blocks(second_low, up, w_up, w_down, tail, second_grad, for_even, for_odd)
    give_pair(stage, even, [(for_even, for_odd, mine, other)])
    stage.need(6, 7, 8)
    middle = middle_ref[...]
    scale = rms(middle)
    unit = middle * scale
    grad = second_grad[...]
    grad_gain_two[...] = jnp.sum(grad * unit, axis=0, keepdims=True)
    grad = grad * gain_two[...]
    grad_middle = up[...].astype(F32) + scale * (grad - unit * jnp.mean(grad * unit, axis=-1, keepdims=True))
    grad_middle_out[...] = grad_middle
    stage.done(1, 2)
    middle_low = grad_middle.astype(BF16)
    grad_state[...] = dot_rt(middle_low, w_out[...])
    stage.done(3)
    stage.need(9, 10, 11)

    def back_step(i, passed):
        at = pl.ds(pl.multiple_of((2 * pairs - 1 - i) * SUB, SUB), SUB)
        return keep[at, :] * (grad_state[at, :] + passed)

    subb[...] = lax.fori_loop(0, 2 * pairs, back_step, jnp.zeros((SUB, hidden), F32), unroll=8)
    for r in range(rows):
        end = r * parts + parts - 1
        b = subb[end : end + 1, :]
        for h in range(parts - 2, -1, -1):
            at = slice(r * parts + h, r * parts + h + 1)
            b = subb[at, :] + subk[at, :] * b
        totals[r : r + 1, :] = b
    stage.done(4, 5)
    half_h = hidden // 2
    out_even[...] = dot_lt(low[:, :half_h], middle_low)
    out_odd[...] = dot_lt(low[:, half_h:], middle_low)
    give_pair(stage, even, [(out_even, out_odd, mine_out, other_out)])
    result = (middle_ref[...] + tail[...]).astype(BF16)
    output[...] = dot_lt(segment_order(count), result).astype(BF16).reshape(output.shape)
    stage.done(0)


def first_kernel(stage, scalars, ins, outs, extra, scratch):
    (first_len,) = scalars
    (returned, subk, subb, keep, grad_state, blend, passing, conv_low, w_z, w_h, x_ref, rim, gain_one, conv_weight,
     grad_middle, grad_gain_two) = ins
    grad_tokens, sent, tail_normed, tail_middle = outs
    mine, other = extra
    incoming, gate_low, cand_low, ext, spread, grad_ext, bias_sum, small, for_even, for_odd, rest = scratch
    count, width = x_ref.shape
    hidden = keep.shape[1]
    rows, lag = rim.shape[0], rim.shape[1]
    parts = SUB // rows
    pairs = count // SUB // 2
    seq_start = lax.axis_index("seq") * (count // rows)
    even = lax.axis_index("row") % 2 == 0
    stage.need(0, 1, 2)
    for r in range(rows):
        b = returned[r : r + 1, :]
        incoming[r * parts + parts - 1 : (r + 1) * parts, :] = b
        for h in range(parts - 2, -1, -1):
            at = slice(r * parts + h + 1, r * parts + h + 2)
            b = subb[at, :] + subk[at, :] * b
            incoming[r * parts + h : r * parts + h + 1, :] = b

    def two(i, carry):
        passed, bias = carry
        at = pl.ds(pl.multiple_of((pairs - 1 - i) * 2 * SUB, 2 * SUB), 2 * SUB)
        k, g = keep[at, :], grad_state[at, :]
        late = g[SUB:] + passed
        early = g[:SUB] + k[SUB:] * late
        adjoint = jnp.concatenate([early, late], axis=0)
        grad_g = adjoint * blend[at, :].astype(F32)
        gate_low[at, :] = grad_g.astype(BF16)
        cand_low[at, :] = (adjoint * passing[at, :].astype(F32)).astype(BF16)
        return k[:SUB] * early, bias + grad_g[:SUB] + grad_g[SUB:]

    carry = (incoming[...], jnp.zeros((SUB, hidden), F32))
    for c in range(CHUNKS):
        stage.need_chunk(CHUNKS - 1 - c, 3, 4, 5, 6)
        carry = lax.fori_loop(c * pairs // CHUNKS, (c + 1) * pairs // CHUNKS, two, carry, unroll=2)
    bias = carry[1]
    bias_sum[...] = jnp.sum(bias, axis=0, keepdims=True)
    stage.need(7)
    for_even[...] = dot_lt(conv_low[...], gate_low[...])
    for_odd[...] = dot_lt(conv_low[...], cand_low[...])
    cols = pl.ds(0, hidden)
    give_pair(stage, even, [(for_even, for_odd, mine.at[:, cols], other.at[:, cols])])
    stage.need(8, 9, 10, 11, 12, 13, 14, 15)
    grad_mixed = dot_rt(gate_low[...], w_z[...]) + dot_rt(cand_low[...], w_h[...])

    x = x_ref[...].astype(F32)
    scale = rms(x)
    unit = x * scale
    gain = gain_one[...]
    ext[lag * SUB :, :] = unit * gain
    rim_x = rim_tiles(rim, spread)
    rim_unit = [v * rms(v) for v in rim_x]
    fill_extended(ext, rim, first_len, seq_start, [v * gain for v in rim_unit])
    small[0:1, :] = jnp.zeros((1, width), F32)
    for j in range(lag + 1):
        begin = (lag - j) * SUB
        small[1 + j : 2 + j, :] = jnp.sum(grad_mixed * ext[begin : begin + count, :], axis=0, keepdims=True)
    for j in range(hidden // width):
        at = 2 + lag + j
        small[at : at + 1, :] = bias_sum[:, j * width : (j + 1) * width]
    last = 2 + lag + hidden // width
    small[last : last + 1, :] = grad_gain_two[...]
    grad_ext[...] = jnp.zeros_like(grad_ext)
    for j in range(lag + 1):
        begin = (lag - j) * SUB
        grad_ext[begin : begin + count, :] += conv_weight[j : j + 1, :] * grad_mixed
    mask = opened(first_len, seq_start, (SUB, width))
    start = at_row_start((SUB, width), rows)
    end = at_row_end((SUB, width), rows)
    grad_gain = jnp.zeros((SUB, width), F32)
    for k in range(lag):
        head = grad_ext[k * SUB : (k + 1) * SUB, :]
        tail_at = pl.ds(count + k * SUB, SUB)
        near = pltpu.roll(head, SUB - 1, 0)
        grad_ext[tail_at, :] = grad_ext[tail_at, :] + jnp.where(end, 0.0, near)
        to_rim = jnp.where(start, head * mask, 0.0)
        grad_gain = grad_gain + to_rim * rim_unit[k]
        spread[k] = to_rim
        for r in range(rows):
            sent[r, k : k + 1, :] = spread[k, r * parts : r * parts + 1, :]
    grad_normed = grad_ext[lag * SUB :, :]
    small[0:1, :] = jnp.sum(grad_normed * unit, axis=0, keepdims=True) + jnp.sum(
        grad_gain, axis=0, keepdims=True
    )
    rest[...] = jnp.zeros_like(rest)
    for j in range(width // 128):
        rest[j * SUB : (j + 1) * SUB, :] = small[:, j * 128 : (j + 1) * 128]
    past = pl.ds(hidden, 128)
    give_pair(stage, even, [(rest, rest, mine.at[:, past], other.at[:, past])])
    for k in range(lag):
        at = count - lag * SUB + k * SUB
        for r in range(rows):
            row = at + r * parts + parts - 1
            to = tail_normed.shape[1] - lag + k
            tail_normed[r, to : to + 1, :] = grad_ext[lag * SUB + row : lag * SUB + row + 1, :]
            tail_middle[r, to : to + 1, :] = grad_middle[row : row + 1, :]
    grad = grad_normed * gain
    grad_x = grad_middle[...] + scale * (grad - unit * jnp.mean(grad * unit, axis=-1, keepdims=True))
    stage.done(1, 2, 3)
    order = segment_order(count)
    grad_tokens[...] = dot_lt(order, grad_x.astype(BF16)).astype(BF16).reshape(grad_tokens.shape)
    stage.done(0)


def tail_kernel(tokens, tail_normed, tail_middle, received, gain_one, _, grad_tokens, spread):
    rows, tile, width = tokens.shape
    lag = received.shape[1]
    for r in range(rows):
        spread[tile - lag :, :] = tail_normed[r, tile - lag :, :] + received[r]
        x = tokens[r].astype(F32)
        scale = rms(x)
        unit = x * scale
        grad = spread[...] * gain_one[...]
        fixed = tail_middle[r] + scale * (grad - unit * jnp.mean(grad * unit, axis=-1, keepdims=True))
        changed = lax.broadcasted_iota(jnp.int32, (tile, width), 0) >= tile - lag
        grad_tokens[r] = jnp.where(changed, fixed, _[r].astype(F32)).astype(BF16)


def shaped(*shapes):
    return tuple(jax.ShapeDtypeStruct(shape, kind) for shape, kind in shapes)


def swapped(array, axis, bit):
    return lax.ppermute(array, axis, [(i, i ^ bit) for i in range(lax.axis_size(axis))])


def bits_of(axis):
    bit, result = 1, []
    while bit < lax.axis_size(axis):
        result.append(bit)
        bit *= 2
    return result


def upper(axis, bit):
    return (lax.axis_index(axis) // bit) % 2 == 1


def carry_forward(totals):
    keep, state = totals[0], totals[1]
    before_k, before_s = jnp.ones_like(keep), jnp.zeros_like(state)
    levels = []
    for bit in bits_of("seq"):
        other = swapped(jnp.stack([keep, state]), "seq", bit)
        other_k, other_s = other[0], other[1]
        late = upper("seq", bit)
        levels.append((keep, other_k))
        before_s = jnp.where(late, before_s + before_k * other_s, before_s)
        before_k = jnp.where(late, before_k * other_k, before_k)
        state = jnp.where(late, state + keep * other_s, other_s + other_k * state)
        keep = keep * other_k
    return before_s, levels


def carry_backward(passed, levels, between):
    after_b, after_k = jnp.zeros_like(passed), jnp.ones_like(passed)
    for i, (bit, (keep, other_k)) in enumerate(zip(bits_of("seq"), levels)):
        if i == HOLD:
            passed = between(passed)
        other_b = swapped(passed, "seq", bit)
        late = upper("seq", bit)
        after_b = jnp.where(late, after_b, after_b + after_k * other_b)
        after_k = jnp.where(late, after_k, after_k * other_k)
        passed = jnp.where(late, other_b + other_k * passed, passed + keep * other_b)
    return after_b


BOTH = ("row", "seq")


def axis_steps(order):
    seq = [("seq", bit) for bit in bits_of("seq")]
    parts = {"x": seq[:1], "y": [("row", bit) for bit in bits_of("row")[1:]], "a": seq[1:2], "b": seq[2:]}
    swap = {"x": "y", "y": "x", "a": "a", "b": "b"}
    even = sum((parts[letter] for letter in order), [])
    odd = sum((parts[swap[letter]] for letter in order), [])
    return list(zip(even, odd))


def exchanged(array, even, odd):
    rows, devices = lax.axis_size("row"), lax.axis_size("seq")
    pairs = []
    for r in range(rows):
        for s in range(devices):
            axis, bit = odd if r & 1 else even
            to = ((r ^ bit) * devices + s) if axis == "row" else (r * devices + (s ^ bit))
            pairs.append((r * devices + s, to))
    return lax.ppermute(array, BOTH, pairs)


def place_bit(step):
    even, odd = [lax.axis_index(axis) // bit % 2 for axis, bit in step]
    return jnp.where(lax.axis_index("row") % 2 == 0, even, odd)


def by_rows(total, body):
    chunk = next((c for c in (64, 32, 16, 8) if total % c == 0), total)
    if chunk == total:
        body(0, chunk)
        return

    def turn(i, carry):
        body(pl.multiple_of(i * chunk, chunk), chunk)
        return carry

    lax.fori_loop(0, total // chunk, turn, 0)


def tiled(first, rows):
    return pl.multiple_of(first, SUB) if rows % SUB == 0 else first


def split_rows(step, mine, received, send, keep):
    half, bit = send.shape[0], place_bit(step)
    if half % SUB:
        first = mine[:half, :] + received[:half, :]
        second = mine[half:, :] + received[half:, :]
        lower = jnp.broadcast_to(bit == 0, first.shape)
        send[...] = jnp.where(lower, second, first)
        keep[...] = jnp.where(lower, first, second)
        return

    def body(i, chunk):
        to = pl.ds(i, chunk)
        for out, begin in ((send, (1 - bit) * half), (keep, bit * half)):
            at = pl.ds(pl.multiple_of(i + begin, SUB), chunk)
            out[to, :] = mine[at, :] + received[at, :]

    by_rows(half, body)


def add_rows(_, mine, received, out):
    def body(i, chunk):
        at = pl.ds(i, chunk)
        out[at, :] = mine[at, :] + received[at, :]

    by_rows(mine.shape[0], body)


def join_rows(step, mine, received, out):
    half, bit = mine.shape[0], place_bit(step)
    if half % SUB:
        lower = jnp.broadcast_to(bit == 0, mine.shape)
        out[:half, :] = jnp.where(lower, mine[...], received[...])
        out[half:, :] = jnp.where(lower, received[...], mine[...])
        return

    def body(i, chunk):
        at = pl.ds(i, chunk)
        for source, begin in ((mine, bit * half), (received, (1 - bit) * half)):
            out[pl.ds(pl.multiple_of(i + begin, SUB), chunk), :] = source[at, :]

    by_rows(half, body)


CORE = (("row", 1),) * 2


class Summed:
    def __init__(self, mine, other, order):
        self.steps = axis_steps(order)
        self.mine, self.stage = mine, 1
        self.received = exchanged(other, *CORE)

    def work(self):
        count = len(self.steps)
        rows, width = self.mine.shape
        if self.stage <= count:
            return split_rows, self.steps[self.stage - 1], [(rows // 2, width)] * 2
        if self.stage == count + 1:
            return add_rows, None, [(rows, width)]
        return join_rows, self.steps[2 * count + 1 - self.stage], [(2 * rows, width)]

    def give(self, outs):
        count = len(self.steps)
        self.mine = outs[-1]
        step = self.steps[self.stage - 1 if self.stage <= count else 2 * count - self.stage]
        self.received = exchanged(outs[0], *step)
        self.stage += 1

    def busy(self):
        return self.stage <= 2 * len(self.steps)

    def across(self):
        self.others = exchanged(self.mine, *CORE), exchanged(self.received, *CORE)


def wave(tokens, sums, through=()):
    works = [one.work() for one in sums]

    def kernel(*refs):
        refs = refs[len(tokens) + len(through) :]
        ins, outs = refs[: 2 * len(sums)], list(refs[2 * len(sums) + len(through) :])
        for i, (rows, step, shapes) in enumerate(works):
            mine_outs = [outs.pop(0) for _ in shapes]
            rows(step, ins[2 * i], ins[2 * i + 1], *mine_outs)

    shapes = [shape for _, _, shapes in works for shape in shapes]
    outs = list(pl.pallas_call(
        kernel,
        in_specs=[ANY] * (len(tokens) + len(through)) + [VMEM] * (2 * len(sums)),
        out_specs=(ANY,) * len(through) + (VMEM,) * len(shapes),
        out_shape=shaped(*[(array.shape, F32) for array in through], *[(shape, F32) for shape in shapes]),
        input_output_aliases={len(tokens) + i: i for i in range(len(through))},
        compiler_params=pltpu.CompilerParams(vmem_limit_bytes=WAVE << 20),
        cost_estimate=pl.CostEstimate(flops=1, bytes_accessed=1, transcendentals=0),
    )(*tokens, *through, *[array for one in sums for array in (one.mine, one.received)]))
    passed = [outs.pop(0) for _ in through]
    first = outs[0]
    for one, (_, _, shapes) in zip(sums, works):
        one.give([outs.pop(0) for _ in shapes])
    return first, passed


def finish_kernel(steps, routes, total, few, skip, *refs):
    count = len(steps)
    before, into = skip
    arrays = refs[before : before + 4 * count]
    refs = arrays + refs[before + 4 * count + into :]
    outs = refs[4 * count : 4 * count + total]
    buffers, sems = refs[4 * count + total : 5 * count + total], refs[-1]
    even = lax.axis_index("row") % 2 == 0
    base, plans = 0, []
    for k, step in enumerate(steps):
        own = arrays[4 * k : 4 * k + 4]
        rows = own[0].shape[0]
        for parity in range(2):
            axis, bit = step[parity]
            place = lax.axis_index(axis) // bit % 2
            longest = 0
            for is_own in (True, False):
                for upper_half in range(2):
                    pair = own[:2] if is_own else own[2:]
                    plan = []
                    for half in range(2):
                        source = pair[half ^ upper_half]
                        buffer = buffers[k].at[parity, half]
                        for at, columns, output, to in routes(k, parity, half * rows, rows):
                            target = None if output is None else outs[output].at[to]
                            plan.append((source.at[at, columns], buffer.at[at, columns], target))
                    mine = even if is_own == (parity == 0) else jnp.logical_not(even)
                    plans.append((jnp.logical_and(mine, place == upper_half), plan, base))
                    longest = max(longest, len(plan))
            base += longest
    for condition, plan, first in plans:

        @pl.when(condition)
        def _():
            for i, (source, buffer, _) in enumerate(plan):
                pltpu.make_async_copy(source, buffer, sems.at[0, first + i]).start()

    for condition, plan, first in plans:

        @pl.when(condition)
        def _():
            for i, (source, buffer, target) in enumerate(plan):
                pltpu.make_async_copy(source, buffer, sems.at[0, first + i]).wait()
                if target is not None:
                    pltpu.make_async_copy(buffer, target, sems.at[1, first + i]).start()

    small = []
    if few:
        packed = buffers[0].at[0, 0, pl.ds(0, few), pl.ds(outs[0].shape[1], 128)]
        small = spread_small(packed, outs[2:], refs[5 * count + total : -1], sems)

    for condition, plan, first in plans:

        @pl.when(condition)
        def _():
            for i, (source, buffer, target) in enumerate(plan):
                if target is not None:
                    pltpu.make_async_copy(buffer, target, sems.at[1, first + i]).wait()

    for copy in small:
        copy.wait()


def spread_small(tiles, targets, rows, sems):
    width = targets[0].shape[1]
    line = 0
    for row in rows:
        for r in range(row.shape[0]):
            for j in range(row.shape[1] // 128):
                source = j * 128 % width // 128 * SUB + line + j * 128 // width
                row[r : r + 1, j * 128 : (j + 1) * 128] = tiles[source : source + 1, :]
            line += row.shape[1] // width
    last = sems.shape[1] - len(rows)
    copies = [pltpu.make_async_copy(row, out, sems.at[1, last + i]) for i, (row, out) in enumerate(zip(rows, targets))]
    for copy in copies:
        copy.start()
    return copies


def finish_call(routes, tokens, sums, outs, few=0, into=()):
    arrays = [array for one in sums for array in (one.mine, one.received, *one.others)]
    before = len(tokens) + len(arrays)
    return pl.pallas_call(
        functools.partial(
            finish_kernel, [one.steps[0] for one in sums], routes, len(outs), few, (len(tokens), len(into))
        ),
        in_specs=[ANY] * (before + len(into)),
        out_specs=(HBM,) * len(outs),
        out_shape=shaped(*outs),
        input_output_aliases={before + i: i for i in range(len(into))},
        scratch_shapes=[pltpu.VMEM((2, 2) + one.mine.shape, F32) for one in sums]
        + ([pltpu.VMEM(*out) for out in outs[2:]] if few else [])
        + [pltpu.SemaphoreType.DMA((2, 48))],
        compiler_params=pltpu.CompilerParams(vmem_limit_bytes=FINISH << 20),
        cost_estimate=pl.CostEstimate(flops=1, bytes_accessed=1, transcendentals=0),
    )(*tokens, *arrays, *into)


def cut(first, rows, marks):
    inside = [first] + [m for m in marks if first < m < first + rows] + [first + rows]
    return [(a - first, a, b - a) for a, b in zip(inside, inside[1:])]


def per_device(
    tokens, first_len, gain_one, conv_weight, w_z, bias_z, w_h, w_out, gain_two, w_up, w_down, cotangent
):
    rows, group_len, width = tokens.shape
    hidden, ff = w_z.shape[1], w_up.shape[1]
    lag = conv_weight.shape[0] - 1
    count = rows * group_len
    devices = lax.axis_size("seq")
    gain_one, gain_two, bias_z = gain_one[None], gain_two[None], bias_z[None]
    rim = lax.ppermute(
        tokens[:, group_len - lag :].astype(F32), "seq", [(i, i + 1) for i in range(devices - 1)]
    )
    th, tw = (count, hidden), (count, width)
    chunks = {3: CHUNKS, 4: CHUNKS, 5: CHUNKS, 6: CHUNKS}
    x, conv_low, keep, drive, cand, gate, passing, subk, subs, totals, up = staged_call(
        gates_kernel,
        [first_len],
        [tokens, rim, gain_one, conv_weight, w_z, bias_z, w_h, cotangent],
        [(tw, BF16), (tw, BF16), (th, F32), (th, F32), (th, F32), (th, BF16), (th, BF16),
         ((SUB, hidden), F32), ((SUB, hidden), F32), ((2, rows, hidden), F32), (tw, BF16)],
        [],
        [((count + lag * SUB, width), F32), ((lag, SUB, width), F32)],
        4 * count * width * hidden,
        64,
        56,
    )
    carried, levels = carry_forward(totals)
    early_ff = ff * FIRST // 4
    pair_a, pair_b, out_pair = [((size, width), F32) for size in (early_ff, ff - early_ff, hidden // 2)]
    low_half, high_half, every = pl.ds(0, early_ff), pl.ds(early_ff, ff - early_ff), pl.ds(0, width)
    blend, low, middle, second_low, tail, second_grad, mine_a, other_a = staged_call(
        state_kernel,
        [first_len],
        [carried, subk, subs, keep, drive, cand, gate, x, w_out, gain_two, (w_up, (every, low_half)),
         (w_down, (low_half, every)), up],
        [(th, BF16), (th, BF16), (tw, F32), (tw, BF16), (tw, F32), (tw, F32)],
        [pair_a, pair_a],
        [((SUB, hidden), F32), pair_a, pair_a],
        6 * count * width * ff,
        64,
        56,
        chunks,
    )
    output, grad_middle, grad_gain_two, grad_state, subb, passed, mine_b, other_b, mine_c, other_c = staged_call(
        mlp_kernel,
        [],
        [second_low, up, (w_up, (every, high_half)), (w_down, (high_half, every)), tail, second_grad, middle, gain_two,
         w_out, low, keep, subk],
        [(tokens.shape, BF16), (tw, F32), ((1, width), F32), (th, F32), ((SUB, hidden), F32), ((rows, hidden), F32)],
        [pair_b, pair_b, out_pair, out_pair],
        [pair_b, pair_b, out_pair, out_pair],
        8 * count * width * ff,
        64,
        56,
    )
    first = Summed(mine_a, other_a, ORDERS[0])
    early = [Summed(mine_b, other_b, ORDERS[1]), Summed(mine_c, other_c, ORDERS[2])]

    def between(passed):
        return wave([], [first], [passed])[1][0]

    returned = carry_backward(passed, levels, between)
    (returned,) = held([one.received for one in early], [returned])
    tile = 16
    pair = ((width, hidden + 128), F32)
    grad_tokens, sent, tail_normed, tail_middle, mine_d, other_d = staged_call(
        first_kernel,
        [first_len],
        [returned, subk, subb, keep, grad_state, blend, passing, conv_low, w_z, w_h, x, rim, gain_one,
         conv_weight, grad_middle, grad_gain_two],
        [(tokens.shape, BF16), ((rows, lag, width), F32)] + [((rows, tile, width), F32)] * 2,
        [pair, pair],
        [((SUB, hidden), F32), (th, BF16), (th, BF16), ((count + lag * SUB, width), F32),
         ((lag, SUB, width), F32), ((count + lag * SUB, width), F32), ((1, hidden), F32), ((SUB, width), F32),
         ((width, hidden), F32), ((width, hidden), F32), ((width, 128), F32)],
        8 * count * width * hidden,
        64,
        LAST,
        chunks,
    )
    received = lax.ppermute(sent, "seq", [(i + 1, i) for i in range(devices - 1)])
    at_tail = pl.BlockSpec((rows, tile, width), lambda i: (0, group_len // tile - 1, 0))
    whole = lambda *shape: pl.BlockSpec(shape, lambda i: (0,) * len(shape))
    grad_tokens = pl.pallas_call(
        tail_kernel,
        grid=(1,),
        in_specs=[at_tail, whole(rows, tile, width), whole(rows, tile, width), whole(rows, lag, width),
                  whole(1, width), at_tail],
        out_specs=at_tail,
        out_shape=jax.ShapeDtypeStruct(tokens.shape, BF16),
        scratch_shapes=[pltpu.VMEM((tile, width), F32)],
        input_output_aliases={5: 0},
    )(tokens, tail_normed, tail_middle, received, gain_one, grad_tokens)
    late = Summed(mine_d, other_d, ORDERS[3])
    tokens = [[]] * (TAIL - 2) + [[grad_tokens]]
    left = [[first], early]
    token, _ = wave([tail_normed], [first] + early)
    def mlp_routes(past, k, parity, first, rows):
        everything, plan, k = pl.ds(0, width), [], k + past
        first = first + (0, early_ff, ff)[k]
        if k == 2:
            first = first - ff
            return [(pl.ds(0, rows), everything, 2, (pl.ds(first + parity * hidden // 2, rows), everything))]
        for offset, at, size in cut(first, rows, range(0, ff, width)):
            inner = pl.ds(offset, size)
            if parity == 0:
                plan.append((inner, everything, 0, (pl.ds(at, size), everything)))
            else:
                block = at // width * width
                plan.append((inner, everything, 1, (pl.ds(at - block, size), pl.ds(block, width))))
        return plan

    grad_down = grad_up = None
    while late.busy():
        more = tokens.pop(0) if tokens else []
        ended = left.pop(0) if left and not left[0][0].busy() else []
        token, ready = wave([token, *more], sum(left, []) + [late], [one.received for one in ended])
        for one, received in zip(ended, ready):
            one.received = received
            one.across()
        if ended == [first]:
            grad_down, grad_up = finish_call(
                functools.partial(mlp_routes, 0), [token], ended, [((ff, width), F32), ((width, ff), F32)]
            )
            tokens.insert(0, [grad_down])
    for one in sum(left, []):
        one.across()

    few = SUB * width // 128

    def gate_routes(k, parity, first, rows):
        inner, cols = pl.ds(0, rows), pl.ds(0, hidden)
        plan = [(inner, cols, parity, (pl.ds(first, rows), cols))]
        if parity == 0 and first < few:
            plan.append((pl.ds(0, few), pl.ds(hidden, 128), None, None))
        return plan

    grad_down, grad_up, grad_out = finish_call(
        functools.partial(mlp_routes, 1), [token], early,
        [((ff, width), F32), ((width, ff), F32), ((hidden, width), F32)], 0, [grad_down, grad_up],
    )
    (late.received,) = held([grad_out], [late.received])
    late.across()
    grad_z, grad_h, grad_gain_one, grad_conv, grad_bias, grad_gain = finish_call(
        gate_routes, [grad_out], [late],
        [((width, hidden), F32), ((width, hidden), F32), ((1, width), F32), ((lag + 1, width), F32),
         ((1, hidden), F32), ((1, width), F32)],
        few,
    )
    return (
        output,
        grad_tokens,
        grad_gain_one.reshape(width),
        grad_conv,
        grad_z,
        grad_bias.reshape(hidden),
        grad_h,
        grad_out,
        grad_gain.reshape(width),
        grad_up,
        grad_down,
    )


def held(tokens, arrays):
    return pl.pallas_call(
        lambda *_: None,
        in_specs=[ANY] * (len(tokens) + len(arrays)),
        out_specs=(ANY,) * len(arrays),
        out_shape=shaped(*[(array.shape, F32) for array in arrays]),
        input_output_aliases={len(tokens) + i: i for i in range(len(arrays))},
        compiler_params=pltpu.CompilerParams(vmem_limit_bytes=HELD << 20),
    )(*tokens, *arrays)


def solution(mesh):
    block, copied = P("row", "seq", None), P()
    return jax.shard_map(
        per_device,
        mesh=mesh,
        in_specs=(block, P("row")) + (copied,) * 9 + (block,),
        out_specs=(block, block) + (copied,) * 9,
        check_vma=False,
    )
```
